32 devices in a mesh: sec: 4 (over y, core), gx: 4 (over z), gy: 2 (over x).
Axes of the slice: x: 2, y: 2, z: 4, core: 2. Of those that a mesh axis runs over, the one named last changes fastest.
Arguments:
- composition_matrix: float32 [22, 32, 32, 512], P(None, 'gx', 'gy', 'sec'), may hold values from 0 to 1
- local_mixing_coefficient: float32 [32, 32, 512], P('gx', 'gy', 'sec'), may hold values from 0.3 to 3
- thermal_field: float32 [32, 32, 512], P('gx', 'gy', 'sec'), may hold values from 0.5 to 2
- component_mixing_weight: float32 [22], replicated, may hold values from 0.05 to 1
- kinetics_jacobian: float32 [22, 22], replicated, may hold values from -1.25 to 1.25
- mixture_classes: int32 [32, 32, 512], P('gx', 'gy', 'sec'), may hold values from 0 to 63, as said below
- streamwise_positions: int32 [32], replicated, may hold values from 0 to 15, as said below
Outputs:
- advanced_composition: float32 [22, 32, 32, 512], P(None, 'gx', 'gy', 'sec')
- cond_means: float32 [22, 16, 64], P(None, 'gx')
The draws below stay inside these ranges and needn't reach their ends.
Inputs may be any that keep to these rules, and one draw needn't show every extreme that they name: `mixture_classes`: bins of each plane cluster around a plane-dependent range. `streamwise_positions`: plane p has station ((p + h) // 2) mod 16 for one odd h between 1 and 7, so each station holds two axial planes.
All inputs are finite; a program needn't handle non-finite values.
Results may differ from the reference program's by a relative error of at most 0.0003.
Values sent between devices are 32-bit elements; how exact they have to be, the bound alone decides.
No kernel may reach another device: no remote copies, remote signals or barrier semaphores. Data moves between devices by JAX's collectives and lax.ppermute only.
A program may use at most 64 MiB of HBM per device.

```python
import math
import jax
import jax.numpy as jnp
from jax import lax

S = 22
NB = 64
CX = 8
STREAMWISE_SLABS = 32
LATERAL_VOXELS = 32
SPANWISE_VOXELS = 512
NST = 16


def draw_mixture_classes(key, part):
    key_low = jax.random.fold_in(key, 11)
    key_noise = jax.random.fold_in(key, 12)
    plane = jnp.arange(STREAMWISE_SLABS, dtype=jnp.int32)
    lowest = jax.random.randint(key_low, (STREAMWISE_SLABS,), 0, 33, dtype=jnp.int32)
    lowest = jnp.where(plane == 0, 0, jnp.where(plane == STREAMWISE_SLABS - 1, 32, lowest))
    across = jnp.arange(LATERAL_VOXELS, dtype=jnp.int32) * 32 // LATERAL_VOXELS
    noise = jax.random.randint(key_noise, (STREAMWISE_SLABS, LATERAL_VOXELS, SPANWISE_VOXELS), -4, 5, dtype=jnp.int32)
    result = lowest[:, None, None] + across[None, :, None] + noise
    return jnp.clip(result, 0, NB - 1).astype(jnp.int32)


def draw_streamwise_positions(key, part):
    key_shift = jax.random.fold_in(key, 21)
    shift = 2 * jax.random.randint(key_shift, (), 0, CX // 2, dtype=jnp.int32) + 1
    plane = jnp.arange(STREAMWISE_SLABS, dtype=jnp.int32)
    return ((plane + shift) // 2 % NST).astype(jnp.int32)


def steps_of(key, extent, split, least, largest):
    loudness, own = 1.0, jax.random.fold_in(key, 6)
    for dim, shards_of in split:
        heights = jnp.exp(jax.random.uniform(jax.random.fold_in(own, dim), (shards_of,), jnp.float32, least / len(split), largest / len(split)))
        loudness = loudness * jnp.repeat(heights, extent[dim] // shards_of).reshape([-1 if axis == dim else 1 for axis in range(len(extent))])
    return loudness


def gaussian(own_key, extent, spread, reach, kind=jnp.bfloat16):
    values = spread * jax.random.normal(own_key, extent, jnp.float32)
    return jnp.clip(values, min=-reach, max=reach).astype(kind)


def setup_inputs(seed: int = 0) -> dict:
    seeds = jax.random.split(jax.random.key(seed), 8)
    return {
        "composition_matrix": jnp.clip(1.0 * jax.random.uniform(seeds[0], (S, STREAMWISE_SLABS, LATERAL_VOXELS, SPANWISE_VOXELS), jnp.float32) ** steps_of(seeds[0], (S, STREAMWISE_SLABS, LATERAL_VOXELS, SPANWISE_VOXELS), ((1, 4), (2, 2), (3, 4)), -0.2, 0.2), 0.0, 1.0),
        "local_mixing_coefficient": jnp.clip(jnp.exp(math.log(3.0) - 2.3025851 * jax.random.uniform(seeds[1], (STREAMWISE_SLABS, LATERAL_VOXELS, SPANWISE_VOXELS), jnp.float32) ** steps_of(seeds[1], (STREAMWISE_SLABS, LATERAL_VOXELS, SPANWISE_VOXELS), ((0, 4), (1, 2), (2, 4)), -0.2, 0.2)), 0.3, 3.0),
        "thermal_field": jnp.clip(0.5 + 1.5 * jax.random.uniform(seeds[2], (STREAMWISE_SLABS, LATERAL_VOXELS, SPANWISE_VOXELS), jnp.float32) ** steps_of(seeds[2], (STREAMWISE_SLABS, LATERAL_VOXELS, SPANWISE_VOXELS), ((0, 4), (1, 2), (2, 4)), -0.2, 0.2), 0.5, 2.0),
        "component_mixing_weight": jnp.clip(jnp.exp(jax.random.uniform(seeds[3], (S,), jnp.float32, math.log(0.05), math.log(1.0))), 0.05, 1.0),
        "kinetics_jacobian": gaussian(seeds[4], (S, S), S ** -0.5, 1.25, jnp.float32),
        "mixture_classes": draw_mixture_classes(jax.random.fold_in(seeds[7], 71), 0),
        "streamwise_positions": draw_streamwise_positions(jax.random.fold_in(seeds[7], 71), 0),
    }


def neighbour(padded_composition, axis, start):
    index = [slice(None), slice(1, -1), slice(1, -1), slice(1, -1)]
    index[axis] = slice(start, start + padded_composition.shape[axis] - 2)
    return padded_composition[tuple(index)]


def advance_explicit_step(padded_composition, interior_block, thermal_field, component_mixing_weight, kinetics_jacobian):
    central_voxels = interior_block[:-1]
    diff_core = interior_block[-1]
    total = jnp.zeros_like(central_voxels)
    for axis in (1, 2, 3):
        for start in (0, 2):
            other = neighbour(padded_composition, axis, start)
            total = total + 0.5 * (diff_core + other[-1]) * (other[:-1] - central_voxels)
    averaged_composition = jnp.einsum("kj,jxyz->kxyz", kinetics_jacobian, central_voxels, precision=lax.Precision.HIGHEST)
    reactive_yield_term = 4.0 * jnp.exp(-2.0 / thermal_field) * averaged_composition
    return central_voxels + 0.05 * (component_mixing_weight[:, None, None, None] * total + reactive_yield_term)


def reference(composition_matrix, local_mixing_coefficient, thermal_field, component_mixing_weight, kinetics_jacobian, mixture_classes, streamwise_positions):
    collected_slabs = jnp.concatenate([composition_matrix, local_mixing_coefficient[None]], axis=0)
    padded_composition = jnp.pad(collected_slabs, ((0, 0), (1, 1), (1, 1), (1, 1)))
    advanced_composition = advance_explicit_step(padded_composition, collected_slabs, thermal_field, component_mixing_weight, kinetics_jacobian)
    values = jnp.concatenate([advanced_composition, jnp.ones_like(advanced_composition[:1])], axis=0)
    levels = jnp.arange(NB, dtype=jnp.int32)

    def plane_sums(item):
        plane, plane_bins = item
        onehot = (plane_bins[None] == levels[:, None, None]).astype(jnp.float32)
        return jnp.einsum("kyz,byz->kb", plane, onehot, precision=lax.Precision.HIGHEST)

    partial_sums = lax.map(plane_sums, (jnp.moveaxis(values, 1, 0), mixture_classes))
    owner = (streamwise_positions[:, None] == jnp.arange(NST, dtype=jnp.int32)[None]).astype(jnp.float32)
    totals = jnp.einsum("xkb,xs->ksb", partial_sums, owner, precision=lax.Precision.HIGHEST)
    cond_means = totals[:-1] / jnp.maximum(totals[-1], 1.0)[None]
    return advanced_composition, cond_means
```

```python
import functools

import jax
import jax.numpy as jnp
from jax import lax
from jax.experimental import pallas as pl
from jax.experimental.pallas import tpu as pltpu
from jax.sharding import PartitionSpec as P

NB = 64
SUBLANES = 8
LANES = 128
F32 = jnp.float32
BF16 = jnp.bfloat16
VMEM = pl.BlockSpec(memory_space=pltpu.VMEM)
ANY = pl.BlockSpec(memory_space=pl.ANY)
DT = 0.05


def padded_rows(species):
    return -(-(species + 2) // SUBLANES) * SUBLANES


def lanes_of(shape):
    return lax.broadcasted_iota(jnp.int32, shape, len(shape) - 1)


def rows_of(shape):
    return lax.broadcasted_iota(jnp.int32, shape, len(shape) - 2)


def halves(block):
    high = block.astype(BF16).astype(F32)
    return jnp.concatenate([high, block - high], axis=0).astype(BF16)


def weight_column(weights_ref, rows):
    species = weights_ref.shape[1]
    shape = (rows, species)
    spread = jnp.where(rows_of(shape) == lanes_of(shape), weights_ref[...], 0.0)
    return DT * jnp.sum(spread, axis=1, keepdims=True)


def binned(values, classes):
    shape = (NB, values.shape[1])
    hits = (classes == rows_of(shape).astype(F32)).astype(F32).astype(BF16)
    return lax.dot_general(
        values, hits, (((1,), (1,)), ((), ())), preferred_element_type=F32
    )


def folded(product):
    rows = product.shape[0] // 2
    return product[:rows] + product[rows:]


def pack_kernel(planes, has_b, cells, mixing, classes, *refs):
    outs, sem = refs[:-1], refs[-1]
    rows_out, own_z = outs[0], outs[1]
    faces = list(outs[2:])
    species, row_count, depth = cells.shape
    width = row_count // planes
    for plane in range(planes):
        span = pl.ds(plane * width, width)
        for k in range(species):
            pltpu.make_async_copy(
                cells.at[k, span], rows_out.at[span, k, :], sem.at[plane]
            ).start()
    for r in range(0, row_count, SUBLANES):
        span = pl.ds(r, SUBLANES)
        rows_out[span, species, :] = mixing[span, :]
        rows_out[span, species + 1, :] = classes[span, :].astype(F32)
    shape = rows_out.shape[1:]
    lane = lanes_of(shape)
    low = jnp.zeros(shape, F32)
    high = jnp.zeros(shape, F32)
    for plane in range(planes):
        span = pl.ds(plane * width, width)
        pltpu.make_async_copy(
            cells.at[:, span], rows_out.at[pl.ds(0, species), pl.ds(0, width), :], sem.at[plane]
        ).wait()
        for r in range(plane * width, (plane + 1) * width):
            turned = pltpu.roll(rows_out[r], r, axis=1) if r else rows_out[r]
            low = jnp.where(lane == r, turned, low)
            high = jnp.where(lane == (r - 1) % depth, turned, high)
    high = pltpu.roll(high, 1, axis=1)
    own_z[0] = low
    own_z[1] = high
    for axis, both in zip(("gx", "gy", "sec"), has_b):
        even = lax.axis_index(axis) % 2 == 0
        for side in range(1 + both):
            out = faces.pop(0)
            upper = even if side == 0 else jnp.logical_not(even)
            if axis == "gx":
                first = jnp.where(upper, row_count - width, 0)
                for y in range(width):
                    out[y] = rows_out[first + y]
            elif axis == "gy":
                first = jnp.where(upper, width - 1, 0)
                for x in range(planes):
                    out[x] = rows_out[first + x * width]
            else:
                out[...] = own_z[jnp.where(upper, 1, 0)]


def inner_kernel(
    planes, cells, mixing, thermal, weights, jacobian, advanced, station_sums, coefs, square
):
    row_count, rows, depth = cells.shape
    species = jacobian.shape[0]
    width = row_count // planes
    shape = (row_count, depth)
    lane, row = lanes_of(shape), rows_of(shape)
    mix = mixing[...]
    up = 0.5 * (mix + pltpu.roll(mix, depth - 1, axis=1))
    up = jnp.where(lane == depth - 1, 0.0, up)
    coefs[0] = up
    down = pltpu.roll(up, 1, axis=1)
    coefs[1] = down
    total = up + down
    up = 0.5 * (mix + pltpu.roll(mix, row_count - 1, axis=0))
    up = jnp.where(row % width == width - 1, 0.0, up)
    coefs[2] = up
    down = pltpu.roll(up, 1, axis=0)
    coefs[3] = down
    total = total + (up + down)
    edge = jnp.zeros((width, depth), F32)
    up = jnp.concatenate([0.5 * (mix[: row_count - width] + mix[width:]), edge], axis=0)
    coefs[4] = up
    down = jnp.concatenate([edge, up[: row_count - width]], axis=0)
    coefs[5] = down
    coefs[6] = total + (up + down)
    coefs[7] = (4.0 * DT) * jnp.exp(-2.0 / thermal[...])

    square[...] = jnp.zeros_like(square)
    matrix = jacobian[...]
    matrix_high = matrix.astype(BF16).astype(F32)
    square[:species, :species] = matrix_high
    square[:species, rows : rows + species] = matrix_high
    square[rows : rows + species, :species] = matrix - matrix_high
    left = square[...].astype(BF16)

    weight = jnp.broadcast_to(weight_column(weights, rows), (rows, depth))
    ones = rows_of((rows, depth)) >= species
    station_sums[...] = jnp.zeros_like(station_sums)

    @pl.loop(0, planes)
    def _(x):
        base = x * width
        below = jnp.maximum(x - 1, 0) * width
        above = jnp.minimum(x + 1, planes - 1) * width
        made = jnp.zeros((2 * rows, NB), F32)
        for first in range(0, width, 2):
            pair = (first, first + 1)
            here = [cells[base + y] for y in pair]
            mixed = folded(
                jnp.dot(
                    left,
                    jnp.concatenate([halves(c) for c in here], axis=1),
                    preferred_element_type=F32,
                )
            )
            values, classes = [], []
            for i, y in enumerate(pair):
                r = base + y
                c = here[i]
                at = lambda n: coefs[n, pl.ds(r, 1), :]
                flux = at(0) * pltpu.roll(c, depth - 1, axis=1)
                flux += at(1) * pltpu.roll(c, 1, axis=1)
                if y < width - 1:
                    flux += at(2) * cells[r + 1]
                if y > 0:
                    flux += at(3) * cells[r - 1]
                flux += at(4) * cells[above + y]
                flux += at(5) * cells[below + y]
                flux -= at(6) * c
                new = c + weight * flux + at(7) * mixed[:, i * depth : (i + 1) * depth]
                new = jnp.where(ones, 1.0, new)
                advanced[r] = new
                values.append(halves(new))
                classes.append(cells[r, species + 1 : species + 2, :])
            made += binned(jnp.concatenate(values, axis=1), jnp.concatenate(classes, axis=1))
        station_sums[(x + 1) // 2] += folded(made)


def edge_kernel(planes, has_b, cells, own_z, sums, weights, positions, *refs):
    halos = list(refs[: 3 + sum(has_b)])
    own, carry, dx, dy, dz, station_sums = refs[3 + sum(has_b) :]
    row_count, rows, depth = cells.shape
    species = weights.shape[1]
    width = row_count // planes
    weight = jnp.broadcast_to(weight_column(weights, rows), (rows, depth))
    received = {}
    for axis, both in zip(("gx", "gy", "sec"), has_b):
        received[axis] = [halos.pop(0), halos.pop(0) if both else None]
    evens = {axis: lax.axis_index(axis) % 2 == 0 for axis in received}

    def added(c, halo):
        if halo is None:
            return weight * (0.5 * c[species : species + 1]) * (0.0 - c)
        d = 0.5 * (c[species : species + 1] + halo[species : species + 1])
        return weight * d * (halo - c)

    station_sums[...] = sums[...]
    for side in range(2):
        upper = evens["gx"] if side == 0 else jnp.logical_not(evens["gx"])
        plane = jnp.where(upper, planes - 1, 0)
        halo = received["gx"][side]
        made = jnp.zeros((2 * rows, NB), F32)
        for first in range(0, width, 2):
            values, classes = [], []
            for y in (first, first + 1):
                r = plane * width + y
                delta = added(cells[r], None if halo is None else halo[y])
                dx[side, y] = delta
                values.append(halves(delta))
                classes.append(cells[r, species + 1 : species + 2, :])
            made += binned(jnp.concatenate(values, axis=1), jnp.concatenate(classes, axis=1))
        station_sums[(plane + 1) // 2] += folded(made)
    for side in range(2):
        upper = evens["gy"] if side == 0 else jnp.logical_not(evens["gy"])
        place = jnp.where(upper, width - 1, 0)
        halo = received["gy"][side]
        for x in range(planes):
            r = place + x * width
            delta = added(cells[r], None if halo is None else halo[x])
            dy[side, x] = delta
            station_sums[(x + 1) // 2] += folded(
                binned(halves(delta), cells[r, species + 1 : species + 2, :])
            )
    stations = planes // 2 + 1
    lane = lanes_of((1, row_count))
    station = ((lane // width + 1) // 2).astype(F32)
    for side in range(2):
        upper = evens["sec"] if side == 0 else jnp.logical_not(evens["sec"])
        c = own_z[jnp.where(upper, 1, 0)]
        halo = received["sec"][side]
        delta = added(c, None if halo is None else halo[...])
        dz[side] = delta
        value = halves(delta)
        classes = c[species + 1 : species + 2]
        for j in range(stations):
            station_sums[j] += folded(binned(value, jnp.where(station == j, classes, -1.0)))
    shift = jnp.broadcast_to(positions[0:1, 0:1], (rows, NB))
    per_device = planes // 2
    for half, out in enumerate((own, carry)):
        for s in range(0, per_device, 2):
            parts = []
            for slot in (half * per_device + s, half * per_device + s + 1):
                part = jnp.zeros((rows, NB), F32)
                for j in range(stations):
                    if 0 <= slot - j < per_device:
                        part += jnp.where(shift == slot - j, station_sums[j], 0.0)
                parts.append(part)
            out[s // 2] = jnp.concatenate(parts, axis=1)


def finish_kernel(planes, advanced, dx, dy, dz, out, total, sem):
    row_count, rows, depth = advanced.shape
    species = out.shape[0]
    width = row_count // planes
    total[...] = advanced[...]
    evens = {axis: lax.axis_index(axis) % 2 == 0 for axis in ("gx", "gy", "sec")}
    for side in range(2):
        upper = evens["gx"] if side == 0 else jnp.logical_not(evens["gx"])
        first = jnp.where(upper, row_count - width, 0)
        for y in range(width):
            total[first + y] += dx[side, y]
    for side in range(2):
        upper = evens["gy"] if side == 0 else jnp.logical_not(evens["gy"])
        place = jnp.where(upper, width - 1, 0)
        for x in range(planes):
            total[place + x * width] += dy[side, x]
    shape = (rows, depth)
    lane = lanes_of(shape)
    even = jnp.broadcast_to(evens["sec"], shape)
    high = jnp.where(even, dz[0], dz[1])
    low = jnp.where(even, dz[1], dz[0])
    high = pltpu.roll(high, depth - 1, axis=1)
    for plane in range(planes):
        for r in range(plane * width, (plane + 1) * width):
            turned = depth - r if r else 0
            a = pltpu.roll(low, turned, axis=1) if r else low
            b = pltpu.roll(high, turned, axis=1) if r else high
            total[r] += jnp.where(lane == 0, a, jnp.where(lane == depth - 1, b, 0.0))
        span = pl.ds(plane * width, width)
        for k in range(species):
            pltpu.make_async_copy(
                total.at[span, k, :], out.at[k, span], sem.at[plane]
            ).start()
    for plane in range(planes):
        span = pl.ds(plane * width, width)
        pltpu.make_async_copy(
            total.at[pl.ds(0, species), pl.ds(0, width), :], out.at[:, span], sem.at[plane]
        ).wait()


def means_kernel(first, second, out):
    species, per_device, bins = out.shape
    for s in range(0, per_device, 2):
        block = first[s // 2] + second[s // 2]
        means = block / jnp.maximum(block[species + 1 : species + 2], 1.0)
        out[:, s, :] = means[:species, :bins]
        out[:, s + 1, :] = means[:species, bins:]


def struct(*shape):
    return jax.ShapeDtypeStruct(shape, F32)


def call(kernel, name, out_shape, n_in, out_specs, in_specs=None, scratch=(), flops=0, moved=0):
    return pl.pallas_call(
        kernel,
        out_shape=out_shape,
        in_specs=in_specs or [VMEM] * n_in,
        out_specs=out_specs,
        scratch_shapes=list(scratch),
        name=name,
        compiler_params=pltpu.CompilerParams(vmem_limit_bytes=32 * 1024 * 1024),
        cost_estimate=pl.CostEstimate(flops=flops, bytes_accessed=moved, transcendentals=0),
    )


def swapped(block, axis, side):
    count = lax.axis_size(axis)
    pairs = []
    for i in range(side, count - 1, 2):
        pairs += [(i, i + 1), (i + 1, i)]
    return lax.ppermute(block, axis, pairs)


def summed(block, axis):
    count = lax.axis_size(axis)
    if count & (count - 1):
        return lax.psum(block, axis)
    step = 1
    while step < count:
        block = block + lax.ppermute(block, axis, [(i, i ^ step) for i in range(count)])
        step *= 2
    return block


def on_device(
    composition_matrix,
    local_mixing_coefficient,
    thermal_field,
    component_mixing_weight,
    kinetics_jacobian,
    mixture_classes,
    streamwise_positions,
):
    species, planes, width, depth = composition_matrix.shape
    row_count = planes * width
    rows = padded_rows(species)
    cells = composition_matrix.reshape(species, row_count, depth)
    mixing = local_mixing_coefficient.reshape(row_count, depth)
    thermal = thermal_field.reshape(row_count, depth)
    classes = mixture_classes.reshape(row_count, depth)
    weights = component_mixing_weight.reshape(1, species)
    positions = streamwise_positions.reshape(1, -1)
    per_device = planes // 2
    has_b = tuple(lax.axis_size(axis) > 2 for axis in ("gx", "gy", "sec"))
    shapes = {"gx": (width, rows, depth), "gy": (planes, rows, depth), "sec": (rows, row_count)}
    sides = [
        (axis, side)
        for axis, both in zip(("gx", "gy", "sec"), has_b)
        for side in range(1 + both)
    ]
    face_shapes = [struct(*shapes[axis]) for axis, _ in sides]

    cells = pltpu.with_memory_space_constraint(cells, pltpu.HBM)
    packed = call(
        functools.partial(pack_kernel, planes, has_b),
        "faces",
        [struct(row_count, rows, depth), struct(2, rows, row_count), *face_shapes],
        3,
        [VMEM] * (2 + len(sides)),
        in_specs=[ANY, VMEM, VMEM],
        scratch=[pltpu.SemaphoreType.DMA((planes,))],
    )(cells, mixing, classes)
    rows_in, own_z, faces = packed[0], packed[1], packed[2:]
    halos = [swapped(face, axis, side) for face, (axis, side) in zip(faces, sides)]

    inner, sums = call(
        functools.partial(inner_kernel, planes),
        "inside",
        [struct(row_count, rows, depth), struct(per_device + 1, rows, NB)],
        5,
        [VMEM] * 2,
        scratch=[
            pltpu.VMEM((8, row_count, depth), F32),
            pltpu.VMEM((2 * rows, 2 * rows), F32),
        ],
        flops=10_000_000,
        moved=4_000_000,
    )(rows_in, mixing, thermal, weights, kinetics_jacobian)

    own, carry, dx, dy, dz = call(
        functools.partial(edge_kernel, planes, has_b),
        "edges",
        [
            struct(per_device // 2, rows, 2 * NB),
            struct(per_device // 2, rows, 2 * NB),
            struct(2, width, rows, depth),
            struct(2, planes, rows, depth),
            struct(2, rows, row_count),
        ],
        5 + len(halos),
        [VMEM] * 5,
        scratch=[pltpu.VMEM((per_device + 1, rows, NB), F32)],
    )(rows_in, own_z, sums, weights, positions, *halos)

    gx = lax.axis_size("gx")
    passed = lax.ppermute(carry, "gx", [(i, (i + 1) % gx) for i in range(gx)])
    window = own + passed
    window = summed(window, "sec")
    gy = lax.axis_size("gy")
    if gy == 2:
        other = lax.ppermute(window, "gy", [(0, 1), (1, 0)])
    else:
        window = summed(window, "gy")
        other = jnp.zeros_like(window)

    advanced = call(
        functools.partial(finish_kernel, planes),
        "advance",
        struct(species, row_count, depth),
        4,
        ANY,
        scratch=[
            pltpu.VMEM((row_count, rows, depth), F32),
            pltpu.SemaphoreType.DMA((planes,)),
        ],
        flops=1_000_000,
        moved=3_000_000,
    )(inner, dx, dy, dz)
    cond_means = call(means_kernel, "means", struct(species, per_device, NB), 2, VMEM)(
        window, other
    )
    return advanced.reshape(composition_matrix.shape), cond_means


def solution(mesh):
    in_specs = (
        P(None, "gx", "gy", "sec"),
        P("gx", "gy", "sec"),
        P("gx", "gy", "sec"),
        P(),
        P(),
        P("gx", "gy", "sec"),
        P(),
    )
    out_specs = (P(None, "gx", "gy", "sec"), P(None, "gx", None))
    return jax.shard_map(
        on_device, mesh=mesh, in_specs=in_specs, out_specs=out_specs, check_vma=False
    )
```

```python
import functools

import jax
import jax.numpy as jnp
from jax import lax
from jax.experimental import pallas as pl
from jax.experimental.pallas import tpu as pltpu
from jax.sharding import PartitionSpec as P

NB = 64
SUBLANES = 8
LANES = 128
F32 = jnp.float32
BF16 = jnp.bfloat16
VMEM = pl.BlockSpec(memory_space=pltpu.VMEM)
ANY = pl.BlockSpec(memory_space=pl.ANY)
DT = 0.05


def padded_rows(species):
    return -(-(species + 2) // SUBLANES) * SUBLANES


def lanes_of(shape):
    return lax.broadcasted_iota(jnp.int32, shape, len(shape) - 1)


def rows_of(shape):
    return lax.broadcasted_iota(jnp.int32, shape, len(shape) - 2)


def halves(block):
    high = block.astype(BF16).astype(F32)
    return jnp.concatenate([high, block - high], axis=0).astype(BF16)


def weight_column(weights_ref, rows):
    species = weights_ref.shape[1]
    shape = (rows, species)
    spread = jnp.where(rows_of(shape) == lanes_of(shape), weights_ref[...], 0.0)
    return DT * jnp.sum(spread, axis=1, keepdims=True)


def binned(values, classes):
    shape = (NB, values.shape[1])
    hits = (classes == rows_of(shape).astype(F32)).astype(F32).astype(BF16)
    return lax.dot_general(
        values, hits, (((1,), (1,)), ((), ())), preferred_element_type=F32
    )


def folded(product):
    rows = product.shape[0] // 2
    return product[:rows] + product[rows:]


def pack_kernel(planes, has_b, cells, mixing, classes, *refs):
    outs, (bins, sem, field_sem) = refs[:-3], refs[-3:]
    rows_out, own_z = outs[0], outs[1]
    faces = list(outs[2:])
    species, row_count, depth = cells.shape
    width = row_count // planes
    for plane in range(planes):
        span = pl.ds(plane * width, width)
        for k in range(species):
            pltpu.make_async_copy(
                cells.at[k, span], rows_out.at[span, k, :], sem.at[plane]
            ).start()
    field_copies = [
        pltpu.make_async_copy(mixing, rows_out.at[:, species, :], field_sem.at[0]),
        pltpu.make_async_copy(classes, bins, field_sem.at[1]),
    ]
    for copy in field_copies:
        copy.start()
    for copy in field_copies:
        copy.wait()
    for r in range(0, row_count, SUBLANES):
        span = pl.ds(r, SUBLANES)
        rows_out[span, species + 1, :] = bins[span, :].astype(F32)
    shape = rows_out.shape[1:]
    lane = lanes_of(shape)
    low = jnp.zeros(shape, F32)
    high = jnp.zeros(shape, F32)
    for plane in range(planes):
        span = pl.ds(plane * width, width)
        pltpu.make_async_copy(
            cells.at[:, span], rows_out.at[pl.ds(0, species), pl.ds(0, width), :], sem.at[plane]
        ).wait()
        for r in range(plane * width, (plane + 1) * width):
            turned = pltpu.roll(rows_out[r], r, axis=1) if r else rows_out[r]
            low = jnp.where(lane == r, turned, low)
            high = jnp.where(lane == (r - 1) % depth, turned, high)
    high = pltpu.roll(high, 1, axis=1)
    own_z[0] = low
    own_z[1] = high
    for axis, both in zip(("gx", "gy", "sec"), has_b):
        even = lax.axis_index(axis) % 2 == 0
        for side in range(1 + both):
            out = faces.pop(0)
            upper = even if side == 0 else jnp.logical_not(even)
            if axis == "gx":
                first = jnp.where(upper, row_count - width, 0)
                for y in range(width):
                    out[y] = rows_out[first + y]
            elif axis == "gy":
                first = jnp.where(upper, width - 1, 0)
                for x in range(planes):
                    out[x] = rows_out[first + x * width]
            else:
                out[...] = own_z[jnp.where(upper, 1, 0)]


def inner_kernel(
    planes, cells, mixing, thermal, weights, jacobian, advanced, station_sums, coefs, square
):
    row_count, rows, depth = cells.shape
    species = jacobian.shape[0]
    width = row_count // planes
    shape = (row_count, depth)
    lane, row = lanes_of(shape), rows_of(shape)
    mix = mixing[...]
    up = 0.5 * (mix + pltpu.roll(mix, depth - 1, axis=1))
    up = jnp.where(lane == depth - 1, 0.0, up)
    coefs[0] = up
    down = pltpu.roll(up, 1, axis=1)
    coefs[1] = down
    total = up + down
    up = 0.5 * (mix + pltpu.roll(mix, row_count - 1, axis=0))
    up = jnp.where(row % width == width - 1, 0.0, up)
    coefs[2] = up
    down = pltpu.roll(up, 1, axis=0)
    coefs[3] = down
    total = total + (up + down)
    edge = jnp.zeros((width, depth), F32)
    up = jnp.concatenate([0.5 * (mix[: row_count - width] + mix[width:]), edge], axis=0)
    coefs[4] = up
    down = jnp.concatenate([edge, up[: row_count - width]], axis=0)
    coefs[5] = down
    coefs[6] = total + (up + down)
    coefs[7] = (4.0 * DT) * jnp.exp(-2.0 / thermal[...])

    square[...] = jnp.zeros_like(square)
    matrix = jacobian[...]
    matrix_high = matrix.astype(BF16).astype(F32)
    square[:species, :species] = matrix_high
    square[:species, rows : rows + species] = matrix_high
    square[rows : rows + species, :species] = matrix - matrix_high
    left = square[...].astype(BF16)

    weight = jnp.broadcast_to(weight_column(weights, rows), (rows, depth))
    ones = rows_of((rows, depth)) >= species
    station_sums[...] = jnp.zeros_like(station_sums)

    for x in range(planes):
        base = x * width
        below = max(x - 1, 0) * width
        above = min(x + 1, planes - 1) * width
        made = jnp.zeros((2 * rows, NB), F32)
        for first in range(0, width, 2):
            pair = (first, first + 1)
            here = [cells[base + y] for y in pair]
            mixed = folded(
                jnp.dot(
                    left,
                    jnp.concatenate([halves(c) for c in here], axis=1),
                    preferred_element_type=F32,
                )
            )
            values, classes = [], []
            for i, y in enumerate(pair):
                r = base + y
                c = here[i]
                at = lambda n: coefs[n, pl.ds(r, 1), :]
                flux = at(0) * pltpu.roll(c, depth - 1, axis=1)
                flux += at(1) * pltpu.roll(c, 1, axis=1)
                if y < width - 1:
                    flux += at(2) * cells[r + 1]
                if y > 0:
                    flux += at(3) * cells[r - 1]
                if x < planes - 1:
                    flux += at(4) * cells[above + y]
                if x > 0:
                    flux += at(5) * cells[below + y]
                flux -= at(6) * c
                new = c + weight * flux + at(7) * mixed[:, i * depth : (i + 1) * depth]
                new = jnp.where(ones, 1.0, new)
                advanced[r] = new
                values.append(halves(new))
                classes.append(cells[r, species + 1 : species + 2, :])
            made += binned(jnp.concatenate(values, axis=1), jnp.concatenate(classes, axis=1))
        station_sums[(x + 1) // 2] += folded(made)


def edge_kernel(planes, has_b, cells, own_z, sums, weights, positions, *refs):
    halos = list(refs[: 3 + sum(has_b)])
    window, dx, dy, dz, station_sums = refs[3 + sum(has_b) :]
    row_count, rows, depth = cells.shape
    species = weights.shape[1]
    width = row_count // planes
    weight = jnp.broadcast_to(weight_column(weights, rows), (rows, depth))
    received = {}
    for axis, both in zip(("gx", "gy", "sec"), has_b):
        received[axis] = [halos.pop(0), halos.pop(0) if both else None]
    evens = {axis: lax.axis_index(axis) % 2 == 0 for axis in received}

    def added(c, halo):
        if halo is None:
            return weight * (0.5 * c[species : species + 1]) * (0.0 - c)
        d = 0.5 * (c[species : species + 1] + halo[species : species + 1])
        return weight * d * (halo - c)

    station_sums[...] = sums[...]
    for side in range(2):
        upper = evens["gx"] if side == 0 else jnp.logical_not(evens["gx"])
        plane = jnp.where(upper, planes - 1, 0)
        halo = received["gx"][side]
        made = jnp.zeros((2 * rows, NB), F32)
        for first in range(0, width, 2):
            values, classes = [], []
            for y in (first, first + 1):
                r = plane * width + y
                delta = added(cells[r], None if halo is None else halo[y])
                dx[side, y] = delta
                values.append(halves(delta))
                classes.append(cells[r, species + 1 : species + 2, :])
            made += binned(jnp.concatenate(values, axis=1), jnp.concatenate(classes, axis=1))
        station_sums[(plane + 1) // 2] += folded(made)
    for side in range(2):
        upper = evens["gy"] if side == 0 else jnp.logical_not(evens["gy"])
        place = jnp.where(upper, width - 1, 0)
        halo = received["gy"][side]
        for x in range(planes):
            r = place + x * width
            delta = added(cells[r], None if halo is None else halo[x])
            dy[side, x] = delta
            station_sums[(x + 1) // 2] += folded(
                binned(halves(delta), cells[r, species + 1 : species + 2, :])
            )
    stations = planes // 2 + 1
    lane = lanes_of((1, row_count))
    station = ((lane // width + 1) // 2).astype(F32)
    for side in range(2):
        upper = evens["sec"] if side == 0 else jnp.logical_not(evens["sec"])
        c = own_z[jnp.where(upper, 1, 0)]
        halo = received["sec"][side]
        delta = added(c, None if halo is None else halo[...])
        dz[side] = delta
        value = halves(delta)
        classes = c[species + 1 : species + 2]
        for j in range(stations):
            station_sums[j] += folded(binned(value, jnp.where(station == j, classes, -1.0)))
    shift = jnp.broadcast_to(positions[0:1, 0:1], (rows, NB))
    per_device = planes // 2
    for s in range(0, 2 * per_device, 2):
        parts = []
        for slot in (s, s + 1):
            part = jnp.zeros((rows, NB), F32)
            for j in range(stations):
                if 0 <= slot - j < per_device:
                    part += jnp.where(shift == slot - j, station_sums[j], 0.0)
            parts.append(part)
        window[s // 2] = jnp.concatenate(parts, axis=1)


def finish_kernel(planes, advanced, dx, dy, dz, out, total, sem):
    row_count, rows, depth = advanced.shape
    species = out.shape[0]
    width = row_count // planes
    total[...] = advanced[...]
    evens = {axis: lax.axis_index(axis) % 2 == 0 for axis in ("gx", "gy", "sec")}
    for side in range(2):
        upper = evens["gx"] if side == 0 else jnp.logical_not(evens["gx"])
        first = jnp.where(upper, row_count - width, 0)
        for y in range(width):
            total[first + y] += dx[side, y]
    for side in range(2):
        upper = evens["gy"] if side == 0 else jnp.logical_not(evens["gy"])
        place = jnp.where(upper, width - 1, 0)
        for x in range(planes):
            total[place + x * width] += dy[side, x]
    shape = (rows, depth)
    lane = lanes_of(shape)
    even = jnp.broadcast_to(evens["sec"], shape)
    high = jnp.where(even, dz[0], dz[1])
    low = jnp.where(even, dz[1], dz[0])
    high = pltpu.roll(high, depth - 1, axis=1)
    for plane in range(planes):
        for r in range(plane * width, (plane + 1) * width):
            turned = depth - r if r else 0
            a = pltpu.roll(low, turned, axis=1) if r else low
            b = pltpu.roll(high, turned, axis=1) if r else high
            total[r] += jnp.where(lane == 0, a, jnp.where(lane == depth - 1, b, 0.0))
        span = pl.ds(plane * width, width)
        for k in range(species):
            pltpu.make_async_copy(
                total.at[span, k, :], out.at[k, span], sem.at[plane]
            ).start()
    for plane in range(planes):
        span = pl.ds(plane * width, width)
        pltpu.make_async_copy(
            total.at[pl.ds(0, species), pl.ds(0, width), :], out.at[:, span], sem.at[plane]
        ).wait()


def means_kernel(own, received, out):
    species, per_device, bins = out.shape
    even = lax.axis_index("sec") % 2 == 0
    for s in range(0, per_device, 2):
        block = jnp.where(jnp.broadcast_to(even, own.shape[1:]), received[s // 2], own[s // 2])
        means = block / jnp.maximum(block[species + 1 : species + 2], 1.0)
        out[:, s, :] = means[:species, :bins]
        out[:, s + 1, :] = means[:species, bins:]


def struct(*shape):
    return jax.ShapeDtypeStruct(shape, F32)


def call(kernel, name, out_shape, n_in, out_specs, in_specs=None, scratch=(), flops=0, moved=0):
    return pl.pallas_call(
        kernel,
        out_shape=out_shape,
        in_specs=in_specs or [VMEM] * n_in,
        out_specs=out_specs,
        scratch_shapes=list(scratch),
        name=name,
        compiler_params=pltpu.CompilerParams(vmem_limit_bytes=32 * 1024 * 1024),
        cost_estimate=pl.CostEstimate(flops=flops, bytes_accessed=moved, transcendentals=0),
    )


def swapped(block, axis, side):
    count = lax.axis_size(axis)
    pairs = []
    for i in range(side, count - 1, 2):
        pairs += [(i, i + 1), (i + 1, i)]
    return lax.ppermute(block, axis, pairs)


def on_odd(block, axis, move):
    deep = lax.axis_size("sec")
    count = lax.axis_size(axis)
    if axis == "sec":
        return lax.ppermute(block, axis, [(i, move(i)) for i in range(1, deep, 2)])
    pairs = [(s * count + i, s * count + move(i)) for s in range(1, deep, 2) for i in range(count)]
    return lax.ppermute(block, ("sec", axis), pairs)


def summed(block):
    deep, gx, gy = (lax.axis_size(axis) for axis in ("sec", "gx", "gy"))
    half = block.shape[0] // 2
    block = block + lax.ppermute(block, "sec", [(i, i + 1) for i in range(0, deep, 2)])
    block = block[:half] + on_odd(block[half:], "gx", lambda i: (i + 1) % gx)
    step = 2
    while step < deep:
        block = block + on_odd(block, "sec", lambda i: i ^ step)
        step *= 2
    step = 1
    while step < gy:
        block = block + on_odd(block, "gy", lambda i: i ^ step)
        step *= 2
    return block, lax.ppermute(block, "sec", [(i + 1, i) for i in range(0, deep, 2)])


def on_device(
    composition_matrix,
    local_mixing_coefficient,
    thermal_field,
    component_mixing_weight,
    kinetics_jacobian,
    mixture_classes,
    streamwise_positions,
):
    species, planes, width, depth = composition_matrix.shape
    row_count = planes * width
    rows = padded_rows(species)
    cells = composition_matrix.reshape(species, row_count, depth)
    mixing = local_mixing_coefficient.reshape(row_count, depth)
    thermal = thermal_field.reshape(row_count, depth)
    classes = mixture_classes.reshape(row_count, depth)
    weights = component_mixing_weight.reshape(1, species)
    positions = streamwise_positions.reshape(1, -1)
    per_device = planes // 2
    has_b = tuple(lax.axis_size(axis) > 2 for axis in ("gx", "gy", "sec"))
    shapes = {"gx": (width, rows, depth), "gy": (planes, rows, depth), "sec": (rows, row_count)}
    sides = [
        (axis, side)
        for axis, both in zip(("gx", "gy", "sec"), has_b)
        for side in range(1 + both)
    ]
    face_shapes = [struct(*shapes[axis]) for axis, _ in sides]

    packed = call(
        functools.partial(pack_kernel, planes, has_b),
        "faces",
        [struct(row_count, rows, depth), struct(2, rows, row_count), *face_shapes],
        3,
        [VMEM] * (2 + len(sides)),
        in_specs=[ANY] * 3,
        scratch=[
            pltpu.VMEM((row_count, depth), jnp.int32),
            pltpu.SemaphoreType.DMA((planes,)),
            pltpu.SemaphoreType.DMA((2,)),
        ],
    )(*[pltpu.with_memory_space_constraint(x, pltpu.HBM) for x in (cells, mixing, classes)])
    rows_in, own_z, faces = packed[0], packed[1], packed[2:]
    halos = [swapped(face, axis, side) for face, (axis, side) in zip(faces, sides)]

    inner, sums = call(
        functools.partial(inner_kernel, planes),
        "inside",
        [struct(row_count, rows, depth), struct(per_device + 1, rows, NB)],
        5,
        [VMEM] * 2,
        scratch=[
            pltpu.VMEM((8, row_count, depth), F32),
            pltpu.VMEM((2 * rows, 2 * rows), F32),
        ],
        flops=10_000_000,
        moved=4_000_000,
    )(rows_in, mixing, thermal, weights, kinetics_jacobian)

    window, dx, dy, dz = call(
        functools.partial(edge_kernel, planes, has_b),
        "edges",
        [
            struct(per_device, rows, 2 * NB),
            struct(2, width, rows, depth),
            struct(2, planes, rows, depth),
            struct(2, rows, row_count),
        ],
        5 + len(halos),
        [VMEM] * 4,
        scratch=[pltpu.VMEM((per_device + 1, rows, NB), F32)],
    )(rows_in, own_z, sums, weights, positions, *halos)

    own, received = summed(window)
    advanced = call(
        functools.partial(finish_kernel, planes),
        "advance",
        struct(species, row_count, depth),
        4,
        ANY,
        scratch=[
            pltpu.VMEM((row_count, rows, depth), F32),
            pltpu.SemaphoreType.DMA((planes,)),
        ],
        flops=1_000_000,
        moved=3_000_000,
    )(inner, dx, dy, dz)
    cond_means = call(means_kernel, "means", struct(species, per_device, NB), 2, VMEM)(
        own, received
    )
    return advanced.reshape(composition_matrix.shape), cond_means


def solution(mesh):
    in_specs = (
        P(None, "gx", "gy", "sec"),
        P("gx", "gy", "sec"),
        P("gx", "gy", "sec"),
        P(),
        P(),
        P("gx", "gy", "sec"),
        P(),
    )
    out_specs = (P(None, "gx", "gy", "sec"), P(None, "gx", None))
    return jax.shard_map(
        on_device, mesh=mesh, in_specs=in_specs, out_specs=out_specs, check_vma=False
    )
```

```python
import functools

import jax
import jax.numpy as jnp
from jax import lax
from jax.experimental import pallas as pl
from jax.experimental.pallas import tpu as pltpu
from jax.sharding import PartitionSpec as P

NB = 64
SUBLANES = 8
LANES = 128
F32 = jnp.float32
BF16 = jnp.bfloat16
VMEM = pl.BlockSpec(memory_space=pltpu.VMEM)
ANY = pl.BlockSpec(memory_space=pl.ANY)
DT = 0.05


def padded_rows(species):
    return -(-(species + 2) // SUBLANES) * SUBLANES


def lanes_of(shape):
    return lax.broadcasted_iota(jnp.int32, shape, len(shape) - 1)


def rows_of(shape):
    return lax.broadcasted_iota(jnp.int32, shape, len(shape) - 2)


def halves(block):
    high = block.astype(BF16).astype(F32)
    return jnp.concatenate([high, block - high], axis=0).astype(BF16)


def weight_column(weights_ref, rows):
    species = weights_ref.shape[1]
    shape = (rows, species)
    spread = jnp.where(rows_of(shape) == lanes_of(shape), weights_ref[...], 0.0)
    return DT * jnp.sum(spread, axis=1, keepdims=True)


def binned(values, classes):
    shape = (NB, values.shape[1])
    hits = (classes == rows_of(shape).astype(F32)).astype(F32).astype(BF16)
    return lax.dot_general(
        values, hits, (((1,), (1,)), ((), ())), preferred_element_type=F32
    )


def folded(product):
    rows = product.shape[0] // 2
    return product[:rows] + product[rows:]


def pack_kernel(planes, has_b, cells, mixing, classes, *refs):
    outs, (bins, sem, field_sem) = refs[:-3], refs[-3:]
    rows_out, own_z = outs[0], outs[1]
    faces = list(outs[2:])
    species, row_count, depth = cells.shape
    width = row_count // planes
    field_copies = [
        pltpu.make_async_copy(mixing, rows_out.at[:, species, :], field_sem.at[0]),
        pltpu.make_async_copy(classes, bins, field_sem.at[1]),
    ]
    for copy in field_copies:
        copy.start()
    for plane in range(planes):
        span = pl.ds(plane * width, width)
        for k in range(species):
            pltpu.make_async_copy(
                cells.at[k, span], rows_out.at[span, k, :], sem.at[plane]
            ).start()
    for copy in field_copies:
        copy.wait()
    for r in range(0, row_count, SUBLANES):
        span = pl.ds(r, SUBLANES)
        rows_out[span, species + 1, :] = bins[span, :].astype(F32)
    shape = rows_out.shape[1:]
    lane = lanes_of(shape)
    low = jnp.zeros(shape, F32)
    high = jnp.zeros(shape, F32)
    for plane in range(planes):
        span = pl.ds(plane * width, width)
        pltpu.make_async_copy(
            cells.at[:, span], rows_out.at[pl.ds(0, species), pl.ds(0, width), :], sem.at[plane]
        ).wait()
        for r in range(plane * width, (plane + 1) * width):
            turned = pltpu.roll(rows_out[r], r, axis=1) if r else rows_out[r]
            low = jnp.where(lane == r, turned, low)
            high = jnp.where(lane == (r - 1) % depth, turned, high)
    high = pltpu.roll(high, 1, axis=1)
    own_z[0] = low
    own_z[1] = high
    for axis, both in zip(("gx", "gy", "sec"), has_b):
        even = lax.axis_index(axis) % 2 == 0
        for side in range(1 + both):
            out = faces.pop(0)
            upper = even if side == 0 else jnp.logical_not(even)
            if axis == "gx":
                first = jnp.where(upper, row_count - width, 0)
                for y in range(width):
                    out[y] = rows_out[first + y]
            elif axis == "gy":
                first = jnp.where(upper, width - 1, 0)
                for x in range(planes):
                    out[x] = rows_out[first + x * width]
            else:
                out[...] = own_z[jnp.where(upper, 1, 0)]


def inner_kernel(
    planes, cells, mixing, thermal, weights, jacobian, advanced, station_sums, coefs, square
):
    row_count, rows, depth = cells.shape
    species = jacobian.shape[0]
    width = row_count // planes
    shape = (row_count, depth)
    lane, row = lanes_of(shape), rows_of(shape)
    mix = mixing[...]
    up = 0.5 * (mix + pltpu.roll(mix, depth - 1, axis=1))
    up = jnp.where(lane == depth - 1, 0.0, up)
    coefs[0] = up
    down = pltpu.roll(up, 1, axis=1)
    coefs[1] = down
    total = up + down
    up = 0.5 * (mix + pltpu.roll(mix, row_count - 1, axis=0))
    up = jnp.where(row % width == width - 1, 0.0, up)
    coefs[2] = up
    down = pltpu.roll(up, 1, axis=0)
    coefs[3] = down
    total = total + (up + down)
    edge = jnp.zeros((width, depth), F32)
    up = jnp.concatenate([0.5 * (mix[: row_count - width] + mix[width:]), edge], axis=0)
    coefs[4] = up
    down = jnp.concatenate([edge, up[: row_count - width]], axis=0)
    coefs[5] = down
    coefs[6] = total + (up + down)
    coefs[7] = (4.0 * DT) * jnp.exp(-2.0 / thermal[...])

    square[...] = jnp.zeros_like(square)
    matrix = jacobian[...]
    matrix_high = matrix.astype(BF16).astype(F32)
    square[:species, :species] = matrix_high
    square[:species, rows : rows + species] = matrix_high
    square[rows : rows + species, :species] = matrix - matrix_high
    left = square[...].astype(BF16)

    weight = jnp.broadcast_to(weight_column(weights, rows), (rows, depth))
    ones = rows_of((rows, depth)) >= species
    station_sums[...] = jnp.zeros_like(station_sums)

    for x in range(planes):
        base = x * width
        below = max(x - 1, 0) * width
        above = min(x + 1, planes - 1) * width
        made = jnp.zeros((2 * rows, NB), F32)
        for first in range(0, width, 2):
            pair = (first, first + 1)
            here = [cells[base + y] for y in pair]
            mixed = folded(
                jnp.dot(
                    left,
                    jnp.concatenate([halves(c) for c in here], axis=1),
                    preferred_element_type=F32,
                )
            )
            values, classes = [], []
            for i, y in enumerate(pair):
                r = base + y
                c = here[i]
                at = lambda n: coefs[n, pl.ds(r, 1), :]
                flux = at(0) * pltpu.roll(c, depth - 1, axis=1)
                flux += at(1) * pltpu.roll(c, 1, axis=1)
                if y < width - 1:
                    flux += at(2) * cells[r + 1]
                if y > 0:
                    flux += at(3) * cells[r - 1]
                if x < planes - 1:
                    flux += at(4) * cells[above + y]
                if x > 0:
                    flux += at(5) * cells[below + y]
                flux -= at(6) * c
                new = c + weight * flux + at(7) * mixed[:, i * depth : (i + 1) * depth]
                new = jnp.where(ones, 1.0, new)
                advanced[r] = new
                values.append(halves(new))
                classes.append(cells[r, species + 1 : species + 2, :])
            made += binned(jnp.concatenate(values, axis=1), jnp.concatenate(classes, axis=1))
        station_sums[(x + 1) // 2] += folded(made)


def edge_kernel(planes, has_b, cells, own_z, sums, weights, positions, *refs):
    halos = list(refs[: 3 + sum(has_b)])
    window, dx, dy, dz, station_sums = refs[3 + sum(has_b) :]
    row_count, rows, depth = cells.shape
    species = weights.shape[1]
    width = row_count // planes
    weight = jnp.broadcast_to(weight_column(weights, rows), (rows, depth))
    received = {}
    for axis, both in zip(("gx", "gy", "sec"), has_b):
        received[axis] = [halos.pop(0), halos.pop(0) if both else None]
    evens = {axis: lax.axis_index(axis) % 2 == 0 for axis in received}

    inside = {}
    for axis in received:
        place, upper = lax.axis_index(axis), jnp.logical_not(evens[axis])
        edge = jnp.where(upper, lax.axis_size(axis) - 1, 0)
        inside[axis] = jnp.broadcast_to(place != edge, (rows, depth))

    def added(c, axis, side, part):
        halo = received[axis][side]
        if halo is None:
            return weight * (0.5 * c[species : species + 1]) * (0.0 - c)
        halo = halo[part]
        if side:
            halo = jnp.where(inside[axis], halo, 0.0)
        d = 0.5 * (c[species : species + 1] + halo[species : species + 1])
        return weight * d * (halo - c)

    station_sums[...] = sums[...]
    for side in range(2):
        upper = evens["gx"] if side == 0 else jnp.logical_not(evens["gx"])
        plane = jnp.where(upper, planes - 1, 0)
        made = jnp.zeros((2 * rows, NB), F32)
        for first in range(0, width, 2):
            values, classes = [], []
            for y in (first, first + 1):
                r = plane * width + y
                delta = added(cells[r], "gx", side, y)
                dx[side, y] = delta
                values.append(halves(delta))
                classes.append(cells[r, species + 1 : species + 2, :])
            made += binned(jnp.concatenate(values, axis=1), jnp.concatenate(classes, axis=1))
        station_sums[(plane + 1) // 2] += folded(made)
    for side in range(2):
        upper = evens["gy"] if side == 0 else jnp.logical_not(evens["gy"])
        place = jnp.where(upper, width - 1, 0)
        for x in range(planes):
            r = place + x * width
            delta = added(cells[r], "gy", side, x)
            dy[side, x] = delta
            station_sums[(x + 1) // 2] += folded(
                binned(halves(delta), cells[r, species + 1 : species + 2, :])
            )
    stations = planes // 2 + 1
    lane = lanes_of((1, row_count))
    station = ((lane // width + 1) // 2).astype(F32)
    for side in range(2):
        upper = evens["sec"] if side == 0 else jnp.logical_not(evens["sec"])
        c = own_z[jnp.where(upper, 1, 0)]
        delta = added(c, "sec", side, slice(None))
        dz[side] = delta
        value = halves(delta)
        classes = c[species + 1 : species + 2]
        for j in range(stations):
            station_sums[j] += folded(binned(value, jnp.where(station == j, classes, -1.0)))
    shift = jnp.broadcast_to(positions[0:1, 0:1], (rows, NB))
    per_device = planes // 2
    for s in range(0, 2 * per_device, 2):
        parts = []
        for slot in (s, s + 1):
            part = jnp.zeros((rows, NB), F32)
            for j in range(stations):
                if 0 <= slot - j < per_device:
                    part += jnp.where(shift == slot - j, station_sums[j], 0.0)
            parts.append(part)
        window[s // 2] = jnp.concatenate(parts, axis=1)


def finish_kernel(planes, advanced, dx, dy, dz, out, total, sem):
    row_count, rows, depth = advanced.shape
    species = out.shape[0]
    width = row_count // planes
    total[...] = advanced[...]
    evens = {axis: lax.axis_index(axis) % 2 == 0 for axis in ("gx", "gy", "sec")}
    for side in range(2):
        upper = evens["gx"] if side == 0 else jnp.logical_not(evens["gx"])
        first = jnp.where(upper, row_count - width, 0)
        for y in range(width):
            total[first + y] += dx[side, y]
    for side in range(2):
        upper = evens["gy"] if side == 0 else jnp.logical_not(evens["gy"])
        place = jnp.where(upper, width - 1, 0)
        for x in range(planes):
            total[place + x * width] += dy[side, x]
    shape = (rows, depth)
    lane = lanes_of(shape)
    even = jnp.broadcast_to(evens["sec"], shape)
    high = jnp.where(even, dz[0], dz[1])
    low = jnp.where(even, dz[1], dz[0])
    high = pltpu.roll(high, depth - 1, axis=1)
    for plane in range(planes):
        for r in range(plane * width, (plane + 1) * width):
            turned = depth - r if r else 0
            a = pltpu.roll(low, turned, axis=1) if r else low
            b = pltpu.roll(high, turned, axis=1) if r else high
            total[r] += jnp.where(lane == 0, a, jnp.where(lane == depth - 1, b, 0.0))
        span = pl.ds(plane * width, width)
        for k in range(species):
            pltpu.make_async_copy(
                total.at[span, k, :], out.at[k, span], sem.at[plane]
            ).start()
    for plane in range(planes):
        span = pl.ds(plane * width, width)
        pltpu.make_async_copy(
            total.at[pl.ds(0, species), pl.ds(0, width), :], out.at[:, span], sem.at[plane]
        ).wait()


def means_kernel(own, received, out):
    species, per_device, bins = out.shape
    for s in range(0, per_device, 2):
        block = own[s // 2] + received[s // 2]
        means = block / jnp.maximum(block[species + 1 : species + 2], 1.0)
        out[:, s, :] = means[:species, :bins]
        out[:, s + 1, :] = means[:species, bins:]


def struct(*shape):
    return jax.ShapeDtypeStruct(shape, F32)


def call(kernel, name, out_shape, n_in, out_specs, in_specs=None, scratch=(), flops=0, moved=0):
    return pl.pallas_call(
        kernel,
        out_shape=out_shape,
        in_specs=in_specs or [VMEM] * n_in,
        out_specs=out_specs,
        scratch_shapes=list(scratch),
        name=name,
        compiler_params=pltpu.CompilerParams(vmem_limit_bytes=32 * 1024 * 1024),
        cost_estimate=pl.CostEstimate(flops=flops, bytes_accessed=moved, transcendentals=0),
    )


def swapped(block, axis, side):
    count = lax.axis_size(axis)
    pairs = []
    for i in range(side, count, 2):
        j = (i + 1) % count
        pairs += [(i, j), (j, i)]
    return lax.ppermute(block, axis, pairs)


def crossed(block, axis, move):
    deep = lax.axis_size("sec")
    count = lax.axis_size(axis)
    if axis == "sec":
        return lax.ppermute(block, axis, [(i, move(i) ^ 1) for i in range(deep)])
    pairs = [(s * count + i, (s ^ 1) * count + move(i)) for s in range(deep) for i in range(count)]
    return lax.ppermute(block, ("sec", axis), pairs)


def summed(block):
    deep, gx, gy = (lax.axis_size(axis) for axis in ("sec", "gx", "gy"))
    half = block.shape[0] // 2
    block = block + lax.ppermute(block, "sec", [(i, i ^ 1) for i in range(deep)])
    block = block[:half] + crossed(block[half:], "gx", lambda i: (i + 1) % gx)
    steps = [("sec", 1 << n) for n in range(1, deep.bit_length() - 1)]
    steps += [("gy", 1 << n) for n in range(gy.bit_length() - 1)]
    for axis, step in steps:
        last = crossed(block, axis, lambda i: i ^ step)
        if (axis, step) == steps[-1]:
            return block, last
        block = block + last


def on_device(
    composition_matrix,
    local_mixing_coefficient,
    thermal_field,
    component_mixing_weight,
    kinetics_jacobian,
    mixture_classes,
    streamwise_positions,
):
    species, planes, width, depth = composition_matrix.shape
    row_count = planes * width
    rows = padded_rows(species)
    cells = composition_matrix.reshape(species, row_count, depth)
    mixing = local_mixing_coefficient.reshape(row_count, depth)
    thermal = thermal_field.reshape(row_count, depth)
    classes = mixture_classes.reshape(row_count, depth)
    weights = component_mixing_weight.reshape(1, species)
    positions = streamwise_positions.reshape(1, -1)
    per_device = planes // 2
    has_b = tuple(lax.axis_size(axis) > 2 for axis in ("gx", "gy", "sec"))
    shapes = {"gx": (width, rows, depth), "gy": (planes, rows, depth), "sec": (rows, row_count)}
    sides = [
        (axis, side)
        for axis, both in zip(("gx", "gy", "sec"), has_b)
        for side in range(1 + both)
    ]
    face_shapes = [struct(*shapes[axis]) for axis, _ in sides]

    packed = call(
        functools.partial(pack_kernel, planes, has_b),
        "faces",
        [struct(row_count, rows, depth), struct(2, rows, row_count), *face_shapes],
        3,
        [VMEM] * (2 + len(sides)),
        in_specs=[ANY] * 3,
        scratch=[
            pltpu.VMEM((row_count, depth), jnp.int32),
            pltpu.SemaphoreType.DMA((planes,)),
            pltpu.SemaphoreType.DMA((2,)),
        ],
    )(*[pltpu.with_memory_space_constraint(x, pltpu.HBM) for x in (cells, mixing, classes)])
    rows_in, own_z, faces = packed[0], packed[1], packed[2:]
    halos = [swapped(face, axis, side) for face, (axis, side) in zip(faces, sides)]

    inner, sums = call(
        functools.partial(inner_kernel, planes),
        "inside",
        [struct(row_count, rows, depth), struct(per_device + 1, rows, NB)],
        5,
        [VMEM] * 2,
        scratch=[
            pltpu.VMEM((8, row_count, depth), F32),
            pltpu.VMEM((2 * rows, 2 * rows), F32),
        ],
        flops=10_000_000,
        moved=4_000_000,
    )(rows_in, mixing, thermal, weights, kinetics_jacobian)

    window, dx, dy, dz = call(
        functools.partial(edge_kernel, planes, has_b),
        "edges",
        [
            struct(per_device, rows, 2 * NB),
            struct(2, width, rows, depth),
            struct(2, planes, rows, depth),
            struct(2, rows, row_count),
        ],
        5 + len(halos),
        [VMEM] * 4,
        scratch=[pltpu.VMEM((per_device + 1, rows, NB), F32)],
    )(rows_in, own_z, sums, weights, positions, *halos)

    own, received = summed(window)
    advanced = call(
        functools.partial(finish_kernel, planes),
        "advance",
        struct(species, row_count, depth),
        4,
        ANY,
        scratch=[
            pltpu.VMEM((row_count, rows, depth), F32),
            pltpu.SemaphoreType.DMA((planes,)),
        ],
        flops=1_000_000,
        moved=3_000_000,
    )(inner, dx, dy, dz)
    cond_means = call(means_kernel, "means", struct(species, per_device, NB), 2, VMEM)(
        own, received
    )
    return advanced.reshape(composition_matrix.shape), cond_means


def solution(mesh):
    in_specs = (
        P(None, "gx", "gy", "sec"),
        P("gx", "gy", "sec"),
        P("gx", "gy", "sec"),
        P(),
        P(),
        P("gx", "gy", "sec"),
        P(),
    )
    out_specs = (P(None, "gx", "gy", "sec"), P(None, "gx", None))
    return jax.shard_map(
        on_device, mesh=mesh, in_specs=in_specs, out_specs=out_specs, check_vma=False
    )
```

```python
import functools

import jax
import jax.numpy as jnp
from jax import lax
from jax.experimental import pallas as pl
from jax.experimental.pallas import tpu as pltpu
from jax.sharding import PartitionSpec as P

NB = 64
SUBLANES = 8
LANES = 128
F32 = jnp.float32
BF16 = jnp.bfloat16
VMEM = pl.BlockSpec(memory_space=pltpu.VMEM)
ANY = pl.BlockSpec(memory_space=pl.ANY)
DT = 0.05


def padded_rows(species):
    return -(-(species + 2) // SUBLANES) * SUBLANES


def lanes_of(shape):
    return lax.broadcasted_iota(jnp.int32, shape, len(shape) - 1)


def rows_of(shape):
    return lax.broadcasted_iota(jnp.int32, shape, len(shape) - 2)


def halves(block):
    high = block.astype(BF16).astype(F32)
    return jnp.concatenate([high, block - high], axis=0).astype(BF16)


def weight_column(weights_ref, rows):
    species = weights_ref.shape[1]
    shape = (rows, species)
    spread = jnp.where(rows_of(shape) == lanes_of(shape), weights_ref[...], 0.0)
    return DT * jnp.sum(spread, axis=1, keepdims=True)


def binned(values, classes):
    shape = (NB, values.shape[1])
    hits = (classes == rows_of(shape).astype(F32)).astype(F32).astype(BF16)
    return lax.dot_general(
        values, hits, (((1,), (1,)), ((), ())), preferred_element_type=F32
    )


def folded(product):
    rows = product.shape[0] // 2
    return product[:rows] + product[rows:]


def pack_kernel(planes, has_b, cells, mixing, classes, *refs):
    outs, (bins, sem, field_sem) = refs[:-3], refs[-3:]
    rows_out, own_z = outs[0], outs[1]
    faces = list(outs[2:])
    species, row_count, depth = cells.shape
    rows = rows_out.shape[1]
    width = row_count // planes
    chunk = row_count // sem.shape[0]
    field_copies = [
        pltpu.make_async_copy(mixing, rows_out.at[:, species, :], field_sem.at[0]),
        pltpu.make_async_copy(classes, bins, field_sem.at[1]),
    ]
    for copy in field_copies:
        copy.start()
    for n in range(sem.shape[0]):
        span = pl.ds(n * chunk, chunk)
        for k in range(species):
            pltpu.make_async_copy(
                cells.at[k, span], rows_out.at[span, k, :], sem.at[n]
            ).start()

    lane = lanes_of((SUBLANES, depth))
    zero = jnp.zeros((SUBLANES, depth), F32)

    def gathered(groups, span, low, high):
        low, high = list(low), list(high)
        for r in span:
            at, before = lane == r, lane == (r - 1) % depth
            for i, g in enumerate(groups):
                block = rows_out[r, pl.ds(g, SUBLANES), :]
                turned = pltpu.roll(block, r, axis=1) if r else block
                low[i] = jnp.where(at, turned, low[i])
                high[i] = jnp.where(before, turned, high[i])
        return low, high

    whole = species // SUBLANES * SUBLANES
    first = range(0, whole, SUBLANES)
    rest = range(whole, rows, SUBLANES)
    low, high = [zero] * len(first), [zero] * len(first)
    for n in range(sem.shape[0]):
        arrived = rows_out.at[pl.ds(n * chunk, chunk), pl.ds(0, species), :]
        pltpu.make_async_copy(arrived, arrived, sem.at[n]).wait()
        low, high = gathered(first, range(n * chunk, (n + 1) * chunk), low, high)
    for copy in field_copies:
        copy.wait()
    for r in range(0, row_count, SUBLANES):
        span = pl.ds(r, SUBLANES)
        rows_out[span, species + 1, :] = bins[span, :].astype(F32)
    lows, highs = gathered(rest, range(row_count), [zero] * len(rest), [zero] * len(rest))
    for i, g in enumerate([*first, *rest]):
        own_z[0, pl.ds(g, SUBLANES), :] = (low + lows)[i]
        own_z[1, pl.ds(g, SUBLANES), :] = pltpu.roll((high + highs)[i], 1, axis=1)
    for axis, both in zip(("gx", "gy", "sec"), has_b):
        even = lax.axis_index(axis) % 2 == 0
        for side in range(1 + both):
            out = faces.pop(0)
            upper = even if side == 0 else jnp.logical_not(even)
            if axis == "gx":
                start = jnp.where(upper, row_count - width, 0)
                for y in range(width):
                    out[y] = rows_out[start + y]
            elif axis == "gy":
                start = jnp.where(upper, width - 1, 0)
                for x in range(planes):
                    out[x] = rows_out[start + x * width]
            else:
                out[...] = own_z[jnp.where(upper, 1, 0)]


def inner_kernel(
    planes, cells, mixing, thermal, weights, jacobian, advanced, station_sums, coefs, square
):
    row_count, rows, depth = cells.shape
    species = jacobian.shape[0]
    width = row_count // planes
    shape = (row_count, depth)
    lane, row = lanes_of(shape), rows_of(shape)
    mix = mixing[...]
    up = 0.5 * (mix + pltpu.roll(mix, depth - 1, axis=1))
    up = jnp.where(lane == depth - 1, 0.0, up)
    coefs[0] = up
    down = pltpu.roll(up, 1, axis=1)
    coefs[1] = down
    total = up + down
    up = 0.5 * (mix + pltpu.roll(mix, row_count - 1, axis=0))
    up = jnp.where(row % width == width - 1, 0.0, up)
    coefs[2] = up
    down = pltpu.roll(up, 1, axis=0)
    coefs[3] = down
    total = total + (up + down)
    edge = jnp.zeros((width, depth), F32)
    up = jnp.concatenate([0.5 * (mix[: row_count - width] + mix[width:]), edge], axis=0)
    coefs[4] = up
    down = jnp.concatenate([edge, up[: row_count - width]], axis=0)
    coefs[5] = down
    coefs[6] = total + (up + down)
    coefs[7] = (4.0 * DT) * jnp.exp(-2.0 / thermal[...])

    square[...] = jnp.zeros_like(square)
    matrix = jacobian[...]
    matrix_high = matrix.astype(BF16).astype(F32)
    square[:species, :species] = matrix_high
    square[:species, rows : rows + species] = matrix_high
    square[rows : rows + species, :species] = matrix - matrix_high
    left = square[...].astype(BF16)

    weight = jnp.broadcast_to(weight_column(weights, rows), (rows, depth))
    ones = rows_of((rows, depth)) >= species
    station_sums[...] = jnp.zeros_like(station_sums)

    for x in range(planes):
        base = x * width
        below = max(x - 1, 0) * width
        above = min(x + 1, planes - 1) * width
        made = jnp.zeros((2 * rows, NB), F32)
        for first in range(0, width, 2):
            pair = (first, first + 1)
            here = [cells[base + y] for y in pair]
            mixed = folded(
                jnp.dot(
                    left,
                    jnp.concatenate([halves(c) for c in here], axis=1),
                    preferred_element_type=F32,
                )
            )
            values, classes = [], []
            for i, y in enumerate(pair):
                r = base + y
                c = here[i]
                at = lambda n: coefs[n, pl.ds(r, 1), :]
                flux = at(0) * pltpu.roll(c, depth - 1, axis=1)
                flux += at(1) * pltpu.roll(c, 1, axis=1)
                if y < width - 1:
                    flux += at(2) * cells[r + 1]
                if y > 0:
                    flux += at(3) * cells[r - 1]
                if x < planes - 1:
                    flux += at(4) * cells[above + y]
                if x > 0:
                    flux += at(5) * cells[below + y]
                flux -= at(6) * c
                new = c + weight * flux + at(7) * mixed[:, i * depth : (i + 1) * depth]
                new = jnp.where(ones, 1.0, new)
                advanced[r] = new
                values.append(halves(new))
                classes.append(cells[r, species + 1 : species + 2, :])
            made += binned(jnp.concatenate(values, axis=1), jnp.concatenate(classes, axis=1))
        station_sums[(x + 1) // 2] += folded(made)


def edge_kernel(planes, has_b, cells, own_z, sums, weights, positions, *refs):
    halos = list(refs[: 3 + sum(has_b)])
    window, dx, dy, dz, station_sums = refs[3 + sum(has_b) :]
    row_count, rows, depth = cells.shape
    species = weights.shape[1]
    width = row_count // planes
    weight = jnp.broadcast_to(weight_column(weights, rows), (rows, depth))
    received = {}
    for axis, both in zip(("gx", "gy", "sec"), has_b):
        received[axis] = [halos.pop(0), halos.pop(0) if both else None]
    evens = {axis: lax.axis_index(axis) % 2 == 0 for axis in received}

    inside = {}
    for axis in received:
        place, upper = lax.axis_index(axis), jnp.logical_not(evens[axis])
        edge = jnp.where(upper, lax.axis_size(axis) - 1, 0)
        inside[axis] = jnp.broadcast_to(place != edge, (rows, depth))

    def added(c, axis, side, part):
        halo = received[axis][side]
        if halo is None:
            return weight * (0.5 * c[species : species + 1]) * (0.0 - c)
        halo = halo[part]
        if side:
            halo = jnp.where(inside[axis], halo, 0.0)
        d = 0.5 * (c[species : species + 1] + halo[species : species + 1])
        return weight * d * (halo - c)

    station_sums[...] = sums[...]
    for side in range(2):
        upper = evens["gx"] if side == 0 else jnp.logical_not(evens["gx"])
        plane = jnp.where(upper, planes - 1, 0)
        made = jnp.zeros((2 * rows, NB), F32)
        for first in range(0, width, 2):
            values, classes = [], []
            for y in (first, first + 1):
                r = plane * width + y
                delta = added(cells[r], "gx", side, y)
                dx[side, y] = delta
                values.append(halves(delta))
                classes.append(cells[r, species + 1 : species + 2, :])
            made += binned(jnp.concatenate(values, axis=1), jnp.concatenate(classes, axis=1))
        station_sums[(plane + 1) // 2] += folded(made)
    for side in range(2):
        upper = evens["gy"] if side == 0 else jnp.logical_not(evens["gy"])
        place = jnp.where(upper, width - 1, 0)
        for x in range(planes):
            r = place + x * width
            delta = added(cells[r], "gy", side, x)
            dy[side, x] = delta
            station_sums[(x + 1) // 2] += folded(
                binned(halves(delta), cells[r, species + 1 : species + 2, :])
            )
    stations = planes // 2 + 1
    lane = lanes_of((1, row_count))
    station = ((lane // width + 1) // 2).astype(F32)
    for side in range(2):
        upper = evens["sec"] if side == 0 else jnp.logical_not(evens["sec"])
        c = own_z[jnp.where(upper, 1, 0)]
        delta = added(c, "sec", side, slice(None))
        dz[side] = delta
        value = halves(delta)
        classes = c[species + 1 : species + 2]
        for j in range(stations):
            station_sums[j] += folded(binned(value, jnp.where(station == j, classes, -1.0)))
    shift = jnp.broadcast_to(positions[0:1, 0:1], (rows, NB))
    per_device = planes // 2
    for s in range(0, 2 * per_device, 2):
        parts = []
        for slot in (s, s + 1):
            part = jnp.zeros((rows, NB), F32)
            for j in range(stations):
                if 0 <= slot - j < per_device:
                    part += jnp.where(shift == slot - j, station_sums[j], 0.0)
            parts.append(part)
        window[s // 2] = jnp.concatenate(parts, axis=1)


def finish_kernel(planes, advanced, dx, dy, dz, out, total, sem):
    row_count, rows, depth = advanced.shape
    species = out.shape[0]
    width = row_count // planes
    total[...] = advanced[...]
    evens = {axis: lax.axis_index(axis) % 2 == 0 for axis in ("gx", "gy", "sec")}
    for side in range(2):
        upper = evens["gx"] if side == 0 else jnp.logical_not(evens["gx"])
        first = jnp.where(upper, row_count - width, 0)
        for y in range(width):
            total[first + y] += dx[side, y]
    for side in range(2):
        upper = evens["gy"] if side == 0 else jnp.logical_not(evens["gy"])
        place = jnp.where(upper, width - 1, 0)
        for x in range(planes):
            total[place + x * width] += dy[side, x]
    shape = (rows, depth)
    lane = lanes_of(shape)
    even = jnp.broadcast_to(evens["sec"], shape)
    high = jnp.where(even, dz[0], dz[1])
    low = jnp.where(even, dz[1], dz[0])
    high = pltpu.roll(high, depth - 1, axis=1)
    for plane in range(planes):
        for r in range(plane * width, (plane + 1) * width):
            turned = depth - r if r else 0
            a = pltpu.roll(low, turned, axis=1) if r else low
            b = pltpu.roll(high, turned, axis=1) if r else high
            total[r] += jnp.where(lane == 0, a, jnp.where(lane == depth - 1, b, 0.0))
        span = pl.ds(plane * width, width)
        for k in range(species):
            pltpu.make_async_copy(
                total.at[span, k, :], out.at[k, span], sem.at[plane]
            ).start()
    for plane in range(planes):
        span = pl.ds(plane * width, width)
        pltpu.make_async_copy(
            total.at[pl.ds(0, species), pl.ds(0, width), :], out.at[:, span], sem.at[plane]
        ).wait()


def means_kernel(*refs):
    terms, out = refs[:-1], refs[-1]
    species, per_device, bins = out.shape
    for s in range(0, per_device, 2):
        block = sum((term[s // 2] for term in terms[1:]), terms[0][s // 2])
        means = block / jnp.maximum(block[species + 1 : species + 2], 1.0)
        out[:, s, :] = means[:species, :bins]
        out[:, s + 1, :] = means[:species, bins:]


def struct(*shape):
    return jax.ShapeDtypeStruct(shape, F32)


def call(kernel, name, out_shape, n_in, out_specs, in_specs=None, scratch=(), flops=0, moved=0):
    return pl.pallas_call(
        kernel,
        out_shape=out_shape,
        in_specs=in_specs or [VMEM] * n_in,
        out_specs=out_specs,
        scratch_shapes=list(scratch),
        name=name,
        compiler_params=pltpu.CompilerParams(vmem_limit_bytes=32 * 1024 * 1024),
        cost_estimate=pl.CostEstimate(flops=flops, bytes_accessed=moved, transcendentals=0),
    )


def joint(block, axis, source):
    deep, count = lax.axis_size("sec"), lax.axis_size(axis)
    pairs = []
    for s in range(deep):
        for i in range(count):
            t, j = source(s, i)
            pairs.append((t * count + j, s * count + i))
    return lax.ppermute(block, ("sec", axis), pairs)


def swapped(block, axis, side):
    count = lax.axis_size(axis)
    if side == 0:
        return lax.ppermute(block, axis, [(i, i ^ 1) for i in range(count)])
    if axis == "sec":
        pairs = [(i, ((i + 1) ^ 1) - 1) for i in range(1, count - 1)]
        return lax.ppermute(block, axis, [*pairs, (0, count - 1), (count - 1, 0)])
    return joint(
        block,
        axis,
        lambda s, i: (s, ((i + 1) ^ 1) - 1) if 0 < i < count - 1 else (s ^ 1, i),
    )


def summed(block):
    deep, gx, gy = (lax.axis_size(axis) for axis in ("sec", "gx", "gy"))
    half = block.shape[0] // 2
    block = block + lax.ppermute(block, "sec", [(i, i ^ 1) for i in range(deep)])
    block = block[:half] + joint(block[half:], "gx", lambda s, i: (s ^ 1, (i - 1) % gx))
    steps = [(1 << n, 0) for n in range(1, deep.bit_length() - 1)]
    steps += [(0, 1 << n) for n in range(gy.bit_length() - 1)]
    terms = [block]
    while steps:
        (a, b), (c, d) = steps.pop(0), steps.pop(0) if steps else (0, 0)
        block = sum(terms[1:], terms[0])
        terms = [block]
        for e, f in dict.fromkeys([(a, b), (c, d), (a ^ c, b ^ d)]):
            if e or f:
                terms.append(joint(block, "gy", lambda s, i: (s ^ 1 ^ e, i ^ f)))
    return terms


def on_device(
    composition_matrix,
    local_mixing_coefficient,
    thermal_field,
    component_mixing_weight,
    kinetics_jacobian,
    mixture_classes,
    streamwise_positions,
):
    species, planes, width, depth = composition_matrix.shape
    row_count = planes * width
    rows = padded_rows(species)
    cells = composition_matrix.reshape(species, row_count, depth)
    mixing = local_mixing_coefficient.reshape(row_count, depth)
    thermal = thermal_field.reshape(row_count, depth)
    classes = mixture_classes.reshape(row_count, depth)
    weights = component_mixing_weight.reshape(1, species)
    positions = streamwise_positions.reshape(1, -1)
    per_device = planes // 2
    has_b = tuple(lax.axis_size(axis) > 2 for axis in ("gx", "gy", "sec"))
    shapes = {"gx": (width, rows, depth), "gy": (planes, rows, depth), "sec": (rows, row_count)}
    sides = [
        (axis, side)
        for axis, both in zip(("gx", "gy", "sec"), has_b)
        for side in range(1 + both)
    ]
    face_shapes = [struct(*shapes[axis]) for axis, _ in sides]

    packed = call(
        functools.partial(pack_kernel, planes, has_b),
        "faces",
        [struct(row_count, rows, depth), struct(2, rows, row_count), *face_shapes],
        3,
        [VMEM] * (2 + len(sides)),
        in_specs=[ANY] * 3,
        scratch=[
            pltpu.VMEM((row_count, depth), jnp.int32),
            pltpu.SemaphoreType.DMA((planes // 2,)),
            pltpu.SemaphoreType.DMA((2,)),
        ],
    )(*[pltpu.with_memory_space_constraint(x, pltpu.HBM) for x in (cells, mixing, classes)])
    rows_in, own_z, faces = packed[0], packed[1], packed[2:]
    halos = [swapped(face, axis, side) for face, (axis, side) in zip(faces, sides)]

    inner, sums = call(
        functools.partial(inner_kernel, planes),
        "inside",
        [struct(row_count, rows, depth), struct(per_device + 1, rows, NB)],
        5,
        [VMEM] * 2,
        scratch=[
            pltpu.VMEM((8, row_count, depth), F32),
            pltpu.VMEM((2 * rows, 2 * rows), F32),
        ],
        flops=10_000_000,
        moved=4_000_000,
    )(rows_in, mixing, thermal, weights, kinetics_jacobian)

    window, dx, dy, dz = call(
        functools.partial(edge_kernel, planes, has_b),
        "edges",
        [
            struct(per_device, rows, 2 * NB),
            struct(2, width, rows, depth),
            struct(2, planes, rows, depth),
            struct(2, rows, row_count),
        ],
        5 + len(halos),
        [VMEM] * 4,
        scratch=[pltpu.VMEM((per_device + 1, rows, NB), F32)],
    )(rows_in, own_z, sums, weights, positions, *halos)

    terms = summed(window)
    advanced = call(
        functools.partial(finish_kernel, planes),
        "advance",
        struct(species, row_count, depth),
        4,
        ANY,
        scratch=[
            pltpu.VMEM((row_count, rows, depth), F32),
            pltpu.SemaphoreType.DMA((planes,)),
        ],
        flops=1_000_000,
        moved=3_000_000,
    )(inner, dx, dy, dz)
    cond_means = call(
        means_kernel, "means", struct(species, per_device, NB), len(terms), VMEM
    )(*terms)
    return advanced.reshape(composition_matrix.shape), cond_means


def solution(mesh):
    in_specs = (
        P(None, "gx", "gy", "sec"),
        P("gx", "gy", "sec"),
        P("gx", "gy", "sec"),
        P(),
        P(),
        P("gx", "gy", "sec"),
        P(),
    )
    out_specs = (P(None, "gx", "gy", "sec"), P(None, "gx", None))
    return jax.shard_map(
        on_device, mesh=mesh, in_specs=in_specs, out_specs=out_specs, check_vma=False
    )
```

```python
import functools

import jax
import jax.numpy as jnp
from jax import lax
from jax.experimental import pallas as pl
from jax.experimental.pallas import tpu as pltpu
from jax.sharding import PartitionSpec as P

NB = 64
SUBLANES = 8
LANES = 128
F32 = jnp.float32
BF16 = jnp.bfloat16
VMEM = pl.BlockSpec(memory_space=pltpu.VMEM)
ANY = pl.BlockSpec(memory_space=pl.ANY)
DT = 0.05


def padded_rows(species):
    return -(-(species + 2) // SUBLANES) * SUBLANES


def lanes_of(shape):
    return lax.broadcasted_iota(jnp.int32, shape, len(shape) - 1)


def rows_of(shape):
    return lax.broadcasted_iota(jnp.int32, shape, len(shape) - 2)


def halves(block):
    high = block.astype(BF16).astype(F32)
    return jnp.concatenate([high, block - high], axis=0).astype(BF16)


def weight_column(weights_ref, rows):
    species = weights_ref.shape[1]
    shape = (rows, species)
    spread = jnp.where(rows_of(shape) == lanes_of(shape), weights_ref[...], 0.0)
    return DT * jnp.sum(spread, axis=1, keepdims=True)


def binned(values, classes):
    shape = (NB, values.shape[1])
    hits = (classes == rows_of(shape).astype(F32)).astype(F32).astype(BF16)
    return lax.dot_general(
        values, hits, (((1,), (1,)), ((), ())), preferred_element_type=F32
    )


def folded(product):
    rows = product.shape[0] // 2
    return product[:rows] + product[rows:]


def gx_face_kernel(planes, both, cells, mixing, *refs):
    faces, sem = refs[:-1], refs[-1]
    species, row_count, _ = cells.shape
    width = row_count // planes
    even = lax.axis_index("gx") % 2 == 0
    for side in range(1 + both):
        upper = even if side == 0 else jnp.logical_not(even)
        start = pl.multiple_of(jnp.where(upper, row_count - width, 0), width)
        span = pl.ds(start, width)
        for k in range(species):
            pltpu.make_async_copy(
                cells.at[k, span], faces[side].at[:, k, :], sem.at[side]
            ).start()
        pltpu.make_async_copy(
            mixing.at[span], faces[side].at[:, species, :], sem.at[side]
        ).start()
    for side in range(1 + both):
        arrived = faces[side].at[:, pl.ds(0, species + 1), :]
        pltpu.make_async_copy(arrived, arrived, sem.at[side]).wait()


def rows_kernel(planes, has_b, cells, mixing, classes, rows_out, own_z, *refs):
    faces, (bins, sem) = list(refs[:-2]), refs[-2:]
    species, row_count, depth = cells.shape
    rows = rows_out.shape[1]
    width = row_count // planes
    copies = [
        pltpu.make_async_copy(mixing, rows_out.at[:, species, :], sem.at[0]),
        pltpu.make_async_copy(classes, bins, sem.at[1]),
    ]
    for copy in copies:
        copy.start()
    flat = cells.reshape(species * row_count, depth)
    lane = lanes_of((SUBLANES, depth))
    groups = range(0, rows, SUBLANES)
    low = [jnp.zeros((SUBLANES, depth), F32)] * len(groups)
    high = list(low)

    def gather(i, r, block):
        turned = pltpu.roll(block, r, axis=1) if r else block
        low[i] = jnp.where(lane == r, turned, low[i])
        high[i] = jnp.where(lane == (r - 1) % depth, turned, high[i])

    for r in range(row_count):
        for i, g in enumerate(groups):
            count = max(0, min(SUBLANES, species - g))
            if count:
                block = flat[pl.ds(g * row_count + r, count, stride=row_count), :]
                rows_out[r, pl.ds(g, count), :] = block
            if count == SUBLANES:
                gather(i, r, block)
    for copy in copies:
        copy.wait()
    for r in range(0, row_count, SUBLANES):
        span = pl.ds(r, SUBLANES)
        rows_out[span, species + 1, :] = bins[span, :].astype(F32)
    for i, g in enumerate(groups):
        if species - g < SUBLANES:
            for r in range(row_count):
                gather(i, r, rows_out[r, pl.ds(g, SUBLANES), :])
    for i, g in enumerate(groups):
        own_z[0, pl.ds(g, SUBLANES), :] = low[i]
        own_z[1, pl.ds(g, SUBLANES), :] = pltpu.roll(high[i], 1, axis=1)
    for axis, both in zip(("gy", "sec"), has_b):
        even = lax.axis_index(axis) % 2 == 0
        for side in range(1 + both):
            out = faces.pop(0)
            upper = even if side == 0 else jnp.logical_not(even)
            if axis == "gy":
                start = jnp.where(upper, width - 1, 0)
                for x in range(planes):
                    out[x] = rows_out[start + x * width]
            else:
                out[...] = own_z[jnp.where(upper, 1, 0)]


def inner_kernel(
    planes, cells, mixing, thermal, weights, jacobian, advanced, station_sums, coefs, square
):
    row_count, rows, depth = cells.shape
    species = jacobian.shape[0]
    width = row_count // planes
    shape = (row_count, depth)
    lane, row = lanes_of(shape), rows_of(shape)
    mix = mixing[...]
    up = 0.5 * (mix + pltpu.roll(mix, depth - 1, axis=1))
    up = jnp.where(lane == depth - 1, 0.0, up)
    coefs[0] = up
    down = pltpu.roll(up, 1, axis=1)
    coefs[1] = down
    total = up + down
    up = 0.5 * (mix + pltpu.roll(mix, row_count - 1, axis=0))
    up = jnp.where(row % width == width - 1, 0.0, up)
    coefs[2] = up
    down = pltpu.roll(up, 1, axis=0)
    coefs[3] = down
    total = total + (up + down)
    edge = jnp.zeros((width, depth), F32)
    up = jnp.concatenate([0.5 * (mix[: row_count - width] + mix[width:]), edge], axis=0)
    coefs[4] = up
    down = jnp.concatenate([edge, up[: row_count - width]], axis=0)
    coefs[5] = down
    coefs[6] = total + (up + down)
    coefs[7] = (4.0 * DT) * jnp.exp(-2.0 / thermal[...])

    square[...] = jnp.zeros_like(square)
    matrix = jacobian[...]
    matrix_high = matrix.astype(BF16).astype(F32)
    square[:species, :species] = matrix_high
    square[:species, rows : rows + species] = matrix_high
    square[rows : rows + species, :species] = matrix - matrix_high
    left = square[...].astype(BF16)

    weight = jnp.broadcast_to(weight_column(weights, rows), (rows, depth))
    ones = rows_of((rows, depth)) >= species
    station_sums[...] = jnp.zeros_like(station_sums)

    for x in range(planes):
        base = x * width
        below = max(x - 1, 0) * width
        above = min(x + 1, planes - 1) * width
        made = jnp.zeros((2 * rows, NB), F32)
        for first in range(0, width, 2):
            pair = (first, first + 1)
            here = [cells[base + y] for y in pair]
            mixed = folded(
                jnp.dot(
                    left,
                    jnp.concatenate([halves(c) for c in here], axis=1),
                    preferred_element_type=F32,
                )
            )
            values, classes = [], []
            for i, y in enumerate(pair):
                r = base + y
                c = here[i]
                at = lambda n: coefs[n, pl.ds(r, 1), :]
                flux = at(0) * pltpu.roll(c, depth - 1, axis=1)
                flux += at(1) * pltpu.roll(c, 1, axis=1)
                if y < width - 1:
                    flux += at(2) * cells[r + 1]
                if y > 0:
                    flux += at(3) * cells[r - 1]
                if x < planes - 1:
                    flux += at(4) * cells[above + y]
                if x > 0:
                    flux += at(5) * cells[below + y]
                flux -= at(6) * c
                new = c + weight * flux + at(7) * mixed[:, i * depth : (i + 1) * depth]
                new = jnp.where(ones, 1.0, new)
                advanced[r] = new
                values.append(halves(new))
                classes.append(cells[r, species + 1 : species + 2, :])
            made += binned(jnp.concatenate(values, axis=1), jnp.concatenate(classes, axis=1))
        station_sums[(x + 1) // 2] += folded(made)


def edge_kernel(planes, has_b, cells, own_z, sums, weights, positions, *refs):
    halos = list(refs[: 3 + sum(has_b)])
    window, dx, dy, dz, station_sums = refs[3 + sum(has_b) :]
    row_count, rows, depth = cells.shape
    species = weights.shape[1]
    width = row_count // planes
    weight = jnp.broadcast_to(weight_column(weights, rows), (rows, depth))
    received = {}
    for axis, both in zip(("gx", "gy", "sec"), has_b):
        received[axis] = [halos.pop(0), halos.pop(0) if both else None]
    evens = {axis: lax.axis_index(axis) % 2 == 0 for axis in received}

    inside = {}
    for axis in received:
        place, upper = lax.axis_index(axis), jnp.logical_not(evens[axis])
        edge = jnp.where(upper, lax.axis_size(axis) - 1, 0)
        inside[axis] = jnp.broadcast_to(place != edge, (rows, depth))

    def added(c, axis, side, part):
        halo = received[axis][side]
        if halo is None:
            return weight * (0.5 * c[species : species + 1]) * (0.0 - c)
        halo = halo[part]
        if side:
            halo = jnp.where(inside[axis], halo, 0.0)
        d = 0.5 * (c[species : species + 1] + halo[species : species + 1])
        return weight * d * (halo - c)

    station_sums[...] = sums[...]
    for side in range(2):
        upper = evens["gx"] if side == 0 else jnp.logical_not(evens["gx"])
        plane = jnp.where(upper, planes - 1, 0)
        made = jnp.zeros((2 * rows, NB), F32)
        for first in range(0, width, 2):
            values, classes = [], []
            for y in (first, first + 1):
                r = plane * width + y
                delta = added(cells[r], "gx", side, y)
                dx[side, y] = delta
                values.append(halves(delta))
                classes.append(cells[r, species + 1 : species + 2, :])
            made += binned(jnp.concatenate(values, axis=1), jnp.concatenate(classes, axis=1))
        station_sums[(plane + 1) // 2] += folded(made)
    for side in range(2):
        upper = evens["gy"] if side == 0 else jnp.logical_not(evens["gy"])
        place = jnp.where(upper, width - 1, 0)
        for x in range(planes):
            r = place + x * width
            delta = added(cells[r], "gy", side, x)
            dy[side, x] = delta
            station_sums[(x + 1) // 2] += folded(
                binned(halves(delta), cells[r, species + 1 : species + 2, :])
            )
    stations = planes // 2 + 1
    lane = lanes_of((1, row_count))
    station = ((lane // width + 1) // 2).astype(F32)
    for side in range(2):
        upper = evens["sec"] if side == 0 else jnp.logical_not(evens["sec"])
        c = own_z[jnp.where(upper, 1, 0)]
        delta = added(c, "sec", side, slice(None))
        dz[side] = delta
        value = halves(delta)
        classes = c[species + 1 : species + 2]
        for j in range(stations):
            station_sums[j] += folded(binned(value, jnp.where(station == j, classes, -1.0)))
    shift = jnp.broadcast_to(positions[0:1, 0:1], (rows, NB))
    per_device = planes // 2
    for s in range(0, 2 * per_device, 2):
        parts = []
        for slot in (s, s + 1):
            part = jnp.zeros((rows, NB), F32)
            for j in range(stations):
                if 0 <= slot - j < per_device:
                    part += jnp.where(shift == slot - j, station_sums[j], 0.0)
            parts.append(part)
        window[s // 2] = jnp.concatenate(parts, axis=1)


def finish_kernel(planes, advanced, dx, dy, dz, out, total, sem):
    row_count, rows, depth = advanced.shape
    species = out.shape[0]
    width = row_count // planes
    total[...] = advanced[...]
    evens = {axis: lax.axis_index(axis) % 2 == 0 for axis in ("gx", "gy", "sec")}
    for side in range(2):
        upper = evens["gx"] if side == 0 else jnp.logical_not(evens["gx"])
        first = jnp.where(upper, row_count - width, 0)
        for y in range(width):
            total[first + y] += dx[side, y]
    for side in range(2):
        upper = evens["gy"] if side == 0 else jnp.logical_not(evens["gy"])
        place = jnp.where(upper, width - 1, 0)
        for x in range(planes):
            total[place + x * width] += dy[side, x]
    shape = (rows, depth)
    lane = lanes_of(shape)
    even = jnp.broadcast_to(evens["sec"], shape)
    high = jnp.where(even, dz[0], dz[1])
    low = jnp.where(even, dz[1], dz[0])
    high = pltpu.roll(high, depth - 1, axis=1)
    for plane in range(planes):
        for r in range(plane * width, (plane + 1) * width):
            turned = depth - r if r else 0
            a = pltpu.roll(low, turned, axis=1) if r else low
            b = pltpu.roll(high, turned, axis=1) if r else high
            total[r] += jnp.where(lane == 0, a, jnp.where(lane == depth - 1, b, 0.0))
        span = pl.ds(plane * width, width)
        for k in range(species):
            pltpu.make_async_copy(
                total.at[span, k, :], out.at[k, span], sem.at[plane]
            ).start()
    for plane in range(planes):
        span = pl.ds(plane * width, width)
        pltpu.make_async_copy(
            total.at[pl.ds(0, species), pl.ds(0, width), :], out.at[:, span], sem.at[plane]
        ).wait()


def means_kernel(*refs):
    terms, out = refs[:-1], refs[-1]
    species, per_device, bins = out.shape
    for s in range(0, per_device, 2):
        block = sum((term[s // 2] for term in terms[1:]), terms[0][s // 2])
        means = block / jnp.maximum(block[species + 1 : species + 2], 1.0)
        out[:, s, :] = means[:species, :bins]
        out[:, s + 1, :] = means[:species, bins:]


def struct(*shape):
    return jax.ShapeDtypeStruct(shape, F32)


def call(kernel, name, out_shape, n_in, out_specs, in_specs=None, scratch=(), flops=0, moved=0):
    return pl.pallas_call(
        kernel,
        out_shape=out_shape,
        in_specs=in_specs or [VMEM] * n_in,
        out_specs=out_specs,
        scratch_shapes=list(scratch),
        name=name,
        compiler_params=pltpu.CompilerParams(vmem_limit_bytes=32 * 1024 * 1024),
        cost_estimate=pl.CostEstimate(flops=flops, bytes_accessed=moved, transcendentals=0),
    )


def joint(block, axis, source):
    deep, count = lax.axis_size("sec"), lax.axis_size(axis)
    pairs = []
    for s in range(deep):
        for i in range(count):
            t, j = source(s, i)
            pairs.append((t * count + j, s * count + i))
    return lax.ppermute(block, ("sec", axis), pairs)


def swapped(block, axis, side):
    count = lax.axis_size(axis)
    if side == 0:
        return lax.ppermute(block, axis, [(i, i ^ 1) for i in range(count)])
    if axis == "sec":
        pairs = [(i, ((i + 1) ^ 1) - 1) for i in range(1, count - 1)]
        return lax.ppermute(block, axis, [*pairs, (0, count - 1), (count - 1, 0)])
    return joint(
        block,
        axis,
        lambda s, i: (s, ((i + 1) ^ 1) - 1) if 0 < i < count - 1 else (s ^ 1, i),
    )


def summed(block):
    deep, gx, gy = (lax.axis_size(axis) for axis in ("sec", "gx", "gy"))
    half = block.shape[0] // 2
    block = block + lax.ppermute(block, "sec", [(i, i ^ 1) for i in range(deep)])
    block = block[:half] + joint(block[half:], "gx", lambda s, i: (s ^ 1, (i - 1) % gx))
    steps = [(1 << n, 0) for n in range(1, deep.bit_length() - 1)]
    steps += [(0, 1 << n) for n in range(gy.bit_length() - 1)]
    terms = [block]
    while steps:
        (a, b), (c, d) = steps.pop(0), steps.pop(0) if steps else (0, 0)
        block = sum(terms[1:], terms[0])
        terms = [block]
        for e, f in dict.fromkeys([(a, b), (c, d), (a ^ c, b ^ d)]):
            if e or f:
                terms.append(joint(block, "gy", lambda s, i: (s ^ 1 ^ e, i ^ f)))
    return terms


def on_device(
    composition_matrix,
    local_mixing_coefficient,
    thermal_field,
    component_mixing_weight,
    kinetics_jacobian,
    mixture_classes,
    streamwise_positions,
):
    species, planes, width, depth = composition_matrix.shape
    row_count = planes * width
    rows = padded_rows(species)
    cells = composition_matrix.reshape(species, row_count, depth)
    mixing = local_mixing_coefficient.reshape(row_count, depth)
    thermal = thermal_field.reshape(row_count, depth)
    classes = mixture_classes.reshape(row_count, depth)
    weights = component_mixing_weight.reshape(1, species)
    positions = streamwise_positions.reshape(1, -1)
    per_device = planes // 2
    has_b = tuple(lax.axis_size(axis) > 2 for axis in ("gx", "gy", "sec"))
    shapes = {"gx": (width, rows, depth), "gy": (planes, rows, depth), "sec": (rows, row_count)}
    sides = [
        (axis, side)
        for axis, both in zip(("gx", "gy", "sec"), has_b)
        for side in range(1 + both)
    ]
    face_shapes = [struct(*shapes[axis]) for axis, _ in sides]

    in_hbm = [pltpu.with_memory_space_constraint(x, pltpu.HBM) for x in (cells, mixing)]
    gx_faces = call(
        functools.partial(gx_face_kernel, planes, has_b[0]),
        "outer_planes",
        [shape for shape, (axis, _) in zip(face_shapes, sides) if axis == "gx"],
        2,
        [VMEM] * (1 + has_b[0]),
        in_specs=[ANY] * 2,
        scratch=[pltpu.SemaphoreType.DMA((2,))],
    )(*in_hbm)
    rows_in, own_z, *faces = call(
        functools.partial(rows_kernel, planes, has_b[1:]),
        "rows",
        [
            struct(row_count, rows, depth),
            struct(2, rows, row_count),
            *[shape for shape, (axis, _) in zip(face_shapes, sides) if axis != "gx"],
        ],
        3,
        [VMEM] * (2 + len(sides) - len(gx_faces)),
        in_specs=[VMEM, ANY, ANY],
        scratch=[
            pltpu.VMEM((row_count, depth), jnp.int32),
            pltpu.SemaphoreType.DMA((2,)),
        ],
        flops=4_000_000,
        moved=3_000_000,
    )(cells, in_hbm[1], pltpu.with_memory_space_constraint(classes, pltpu.HBM))
    faces = [*gx_faces, *faces]
    halos = [swapped(face, axis, side) for face, (axis, side) in zip(faces, sides)]

    inner, sums = call(
        functools.partial(inner_kernel, planes),
        "inside",
        [struct(row_count, rows, depth), struct(per_device + 1, rows, NB)],
        5,
        [VMEM] * 2,
        scratch=[
            pltpu.VMEM((8, row_count, depth), F32),
            pltpu.VMEM((2 * rows, 2 * rows), F32),
        ],
        flops=10_000_000,
        moved=4_000_000,
    )(rows_in, mixing, thermal, weights, kinetics_jacobian)

    window, dx, dy, dz = call(
        functools.partial(edge_kernel, planes, has_b),
        "edges",
        [
            struct(per_device, rows, 2 * NB),
            struct(2, width, rows, depth),
            struct(2, planes, rows, depth),
            struct(2, rows, row_count),
        ],
        5 + len(halos),
        [VMEM] * 4,
        scratch=[pltpu.VMEM((per_device + 1, rows, NB), F32)],
    )(rows_in, own_z, sums, weights, positions, *halos)

    terms = summed(window)
    advanced = call(
        functools.partial(finish_kernel, planes),
        "advance",
        struct(species, row_count, depth),
        4,
        ANY,
        scratch=[
            pltpu.VMEM((row_count, rows, depth), F32),
            pltpu.SemaphoreType.DMA((planes,)),
        ],
        flops=1_000_000,
        moved=3_000_000,
    )(inner, dx, dy, dz)
    cond_means = call(
        means_kernel, "means", struct(species, per_device, NB), len(terms), VMEM
    )(*terms)
    return advanced.reshape(composition_matrix.shape), cond_means


def solution(mesh):
    in_specs = (
        P(None, "gx", "gy", "sec"),
        P("gx", "gy", "sec"),
        P("gx", "gy", "sec"),
        P(),
        P(),
        P("gx", "gy", "sec"),
        P(),
    )
    out_specs = (P(None, "gx", "gy", "sec"), P(None, "gx", None))
    return jax.shard_map(
        on_device, mesh=mesh, in_specs=in_specs, out_specs=out_specs, check_vma=False
    )
```

```python
import functools

import jax
import jax.numpy as jnp
from jax import lax
from jax.experimental import pallas as pl
from jax.experimental.pallas import tpu as pltpu
from jax.sharding import PartitionSpec as P

NB = 64
SUBLANES = 8
LANES = 128
F32 = jnp.float32
BF16 = jnp.bfloat16
VMEM = pl.BlockSpec(memory_space=pltpu.VMEM)
ANY = pl.BlockSpec(memory_space=pl.ANY)
DT = 0.05
AHEAD = 2


def padded_rows(species):
    return -(-(species + 2) // SUBLANES) * SUBLANES


def lanes_of(shape):
    return lax.broadcasted_iota(jnp.int32, shape, len(shape) - 1)


def rows_of(shape):
    return lax.broadcasted_iota(jnp.int32, shape, len(shape) - 2)


def halves(block):
    high = block.astype(BF16).astype(F32)
    return jnp.concatenate([high, block - high], axis=0).astype(BF16)


def weight_column(weights_ref, rows):
    species = weights_ref.shape[1]
    shape = (rows, species)
    spread = jnp.where(rows_of(shape) == lanes_of(shape), weights_ref[...], 0.0)
    return DT * jnp.sum(spread, axis=1, keepdims=True)


def hits(classes):
    shape = (NB, classes.shape[1])
    bins = jnp.broadcast_to(classes.astype(BF16), shape)
    found = bins == rows_of(shape).astype(F32).astype(BF16)
    return jnp.where(found, jnp.ones((), BF16), jnp.zeros((), BF16))


def binned(values, hit):
    return lax.dot_general(
        values, hit, (((1,), (1,)), ((), ())), preferred_element_type=F32
    )


def folded(product):
    rows = product.shape[0] // 2
    return product[:rows] + product[rows:]


def gx_face_kernel(planes, both, cells, mixing, classes, mixing_out, classes_out, *refs):
    faces, sem, field_sem = refs[:-2], refs[-2], refs[-1]
    species, row_count, _ = cells.shape
    width = row_count // planes
    even = lax.axis_index("gx") % 2 == 0
    for side in range(1 + both):
        upper = even if side == 0 else jnp.logical_not(even)
        start = pl.multiple_of(jnp.where(upper, row_count - width, 0), width)
        span = pl.ds(start, width)
        for k in range(species):
            pltpu.make_async_copy(
                cells.at[k, span], faces[side].at[:, k, :], sem.at[side]
            ).start()
        pltpu.make_async_copy(
            mixing.at[span], faces[side].at[:, species, :], sem.at[side]
        ).start()
    field_copies = [
        pltpu.make_async_copy(mixing, mixing_out, field_sem.at[0]),
        pltpu.make_async_copy(classes, classes_out, field_sem.at[1]),
    ]
    for copy in field_copies:
        copy.start()
    for side in range(1 + both):
        arrived = faces[side].at[:, pl.ds(0, species + 1), :]
        pltpu.make_async_copy(arrived, arrived, sem.at[side]).wait()
    for copy in field_copies:
        copy.wait()


def rows_kernel(planes, has_b, cells, mixing, classes, rows_out, own_z, *faces):
    faces = list(faces)
    species, row_count, depth = cells.shape
    rows = rows_out.shape[1]
    width = row_count // planes
    for r in range(0, row_count, SUBLANES):
        span = pl.ds(r, SUBLANES)
        rows_out[span, species, :] = mixing[span, :]
        rows_out[span, species + 1, :] = classes[span, :].astype(F32)
    flat = cells.reshape(species * row_count, depth)
    lane = lanes_of((SUBLANES, depth))
    groups = range(0, rows, SUBLANES)
    low = [jnp.zeros((SUBLANES, depth), F32)] * len(groups)
    high = list(low)
    for r in range(row_count):
        at, before = lane == r, lane == (r - 1) % depth
        for i, g in enumerate(groups):
            count = max(0, min(SUBLANES, species - g))
            if count:
                block = flat[pl.ds(g * row_count + r, count, stride=row_count), :]
                rows_out[r, pl.ds(g, count), :] = block
            if count < SUBLANES:
                block = rows_out[r, pl.ds(g, SUBLANES), :]
            turned = pltpu.roll(block, r, axis=1) if r else block
            low[i] = jnp.where(at, turned, low[i])
            high[i] = jnp.where(before, turned, high[i])
    for i, g in enumerate(groups):
        own_z[0, pl.ds(g, SUBLANES), :] = low[i]
        own_z[1, pl.ds(g, SUBLANES), :] = pltpu.roll(high[i], 1, axis=1)
    for axis, both in zip(("gy", "sec"), has_b):
        even = lax.axis_index(axis) % 2 == 0
        for side in range(1 + both):
            out = faces.pop(0)
            upper = even if side == 0 else jnp.logical_not(even)
            if axis == "gy":
                start = jnp.where(upper, width - 1, 0)
                for x in range(planes):
                    out[x] = rows_out[start + x * width]
            else:
                out[...] = own_z[jnp.where(upper, 1, 0)]


def inner_kernel(
    planes, cells, mixing, thermal, weights, jacobian, advanced, station_sums, coefs, square
):
    row_count, rows, depth = cells.shape
    species = jacobian.shape[0]
    width = row_count // planes
    shape = (row_count, depth)
    lane, row = lanes_of(shape), rows_of(shape)
    mix = mixing[...]
    up = 0.5 * (mix + pltpu.roll(mix, depth - 1, axis=1))
    up = jnp.where(lane == depth - 1, 0.0, up)
    coefs[0] = up
    down = pltpu.roll(up, 1, axis=1)
    coefs[1] = down
    total = up + down
    up = 0.5 * (mix + pltpu.roll(mix, row_count - 1, axis=0))
    up = jnp.where(row % width == width - 1, 0.0, up)
    coefs[2] = up
    down = pltpu.roll(up, 1, axis=0)
    coefs[3] = down
    total = total + (up + down)
    edge = jnp.zeros((width, depth), F32)
    up = jnp.concatenate([0.5 * (mix[: row_count - width] + mix[width:]), edge], axis=0)
    coefs[4] = up
    down = jnp.concatenate([edge, up[: row_count - width]], axis=0)
    coefs[5] = down
    coefs[6] = total + (up + down)
    coefs[7] = (4.0 * DT) * jnp.exp(-2.0 / thermal[...])

    square[...] = jnp.zeros_like(square)
    matrix = jacobian[...]
    matrix_high = matrix.astype(BF16).astype(F32)
    square[:species, :species] = matrix_high
    square[:species, rows : rows + species] = matrix_high
    square[rows : rows + species, :species] = matrix - matrix_high
    left = square[...].astype(BF16)

    weight = jnp.broadcast_to(weight_column(weights, rows), (rows, depth))
    whole = species // SUBLANES * SUBLANES
    ones = rows_of((rows - whole, depth)) >= species - whole
    station_sums[...] = jnp.zeros_like(station_sums)

    def kinetics(pair):
        wide = jnp.concatenate([halves(cells[r]) for r in pair], axis=1)
        return folded(jnp.dot(left, wide, preferred_element_type=F32))

    def advance(pair, mixed):
        values, found = [], []
        for i, r in enumerate(pair):
            x, y = divmod(r, width)
            c = cells[r]
            at = lambda n: coefs[n, pl.ds(r, 1), :]
            flux = at(0) * pltpu.roll(c, depth - 1, axis=1)
            flux += at(1) * pltpu.roll(c, 1, axis=1)
            if y < width - 1:
                flux += at(2) * cells[r + 1]
            if y > 0:
                flux += at(3) * cells[r - 1]
            if x < planes - 1:
                flux += at(4) * cells[r + width]
            if x > 0:
                flux += at(5) * cells[r - width]
            flux -= at(6) * c
            new = c + weight * flux + at(7) * mixed[:, i * depth : (i + 1) * depth]
            new = jnp.concatenate([new[:whole], jnp.where(ones, 1.0, new[whole:])], axis=0)
            advanced[r] = new
            values.append(halves(new))
            found.append(hits(cells[r, species + 1 : species + 2, :]))
        return jnp.concatenate(values, axis=1), jnp.concatenate(found, axis=1)

    pairs = [(r, r + 1) for r in range(0, row_count, 2)]
    mixed, values, made = {}, {}, 0.0
    for t in range(len(pairs) + 2 * AHEAD):
        if t < len(pairs):
            mixed[t] = kinetics(pairs[t])
        now = t - AHEAD
        if 0 <= now < len(pairs):
            values[now] = advance(pairs[now], mixed.pop(now))
        last = now - AHEAD
        if 0 <= last < len(pairs):
            made += binned(*values.pop(last))
            x, y = divmod(pairs[last][1], width)
            if y == width - 1:
                station_sums[(x + 1) // 2] += folded(made)
                made = 0.0


def edge_kernel(planes, has_b, cells, own_z, sums, weights, positions, *refs):
    halos = list(refs[: 3 + sum(has_b)])
    window, dx, dy, dz, station_sums = refs[3 + sum(has_b) :]
    row_count, rows, depth = cells.shape
    species = weights.shape[1]
    width = row_count // planes
    weight = jnp.broadcast_to(weight_column(weights, rows), (rows, depth))
    received = {}
    for axis, both in zip(("gx", "gy", "sec"), has_b):
        received[axis] = [halos.pop(0), halos.pop(0) if both else None]
    evens = {axis: lax.axis_index(axis) % 2 == 0 for axis in received}

    inside = {}
    for axis in received:
        place, upper = lax.axis_index(axis), jnp.logical_not(evens[axis])
        edge = jnp.where(upper, lax.axis_size(axis) - 1, 0)
        inside[axis] = jnp.broadcast_to(place != edge, (rows, depth))

    def added(c, axis, side, part):
        halo = received[axis][side]
        if halo is None:
            return weight * (0.5 * c[species : species + 1]) * (0.0 - c)
        halo = halo[part]
        if side:
            halo = jnp.where(inside[axis], halo, 0.0)
        d = 0.5 * (c[species : species + 1] + halo[species : species + 1])
        return weight * d * (halo - c)

    station_sums[...] = sums[...]
    for side in range(2):
        upper = evens["gx"] if side == 0 else jnp.logical_not(evens["gx"])
        plane = jnp.where(upper, planes - 1, 0)
        made = jnp.zeros((2 * rows, NB), F32)
        for first in range(0, width, 2):
            values, classes = [], []
            for y in (first, first + 1):
                r = plane * width + y
                delta = added(cells[r], "gx", side, y)
                dx[side, y] = delta
                values.append(halves(delta))
                classes.append(cells[r, species + 1 : species + 2, :])
            made += binned(jnp.concatenate(values, axis=1), hits(jnp.concatenate(classes, axis=1)))
        station_sums[(plane + 1) // 2] += folded(made)
    for side in range(2):
        upper = evens["gy"] if side == 0 else jnp.logical_not(evens["gy"])
        place = jnp.where(upper, width - 1, 0)
        for x in range(planes):
            r = place + x * width
            delta = added(cells[r], "gy", side, x)
            dy[side, x] = delta
            station_sums[(x + 1) // 2] += folded(
                binned(halves(delta), hits(cells[r, species + 1 : species + 2, :]))
            )
    stations = planes // 2 + 1
    lane = lanes_of((1, row_count))
    station = ((lane // width + 1) // 2).astype(F32)
    for side in range(2):
        upper = evens["sec"] if side == 0 else jnp.logical_not(evens["sec"])
        c = own_z[jnp.where(upper, 1, 0)]
        delta = added(c, "sec", side, slice(None))
        dz[side] = delta
        value = halves(delta)
        classes = c[species + 1 : species + 2]
        for j in range(stations):
            station_sums[j] += folded(binned(value, hits(jnp.where(station == j, classes, -1.0))))
    shift = jnp.broadcast_to(positions[0:1, 0:1], (rows, NB))
    per_device = planes // 2
    for s in range(0, 2 * per_device, 2):
        parts = []
        for slot in (s, s + 1):
            part = jnp.zeros((rows, NB), F32)
            for j in range(stations):
                if 0 <= slot - j < per_device:
                    part += jnp.where(shift == slot - j, station_sums[j], 0.0)
            parts.append(part)
        window[s // 2] = jnp.concatenate(parts, axis=1)


def finish_kernel(planes, advanced, dx, dy, dz, out, total, sem):
    row_count, rows, depth = advanced.shape
    species = out.shape[0]
    width = row_count // planes
    total[...] = advanced[...]
    evens = {axis: lax.axis_index(axis) % 2 == 0 for axis in ("gx", "gy", "sec")}
    for side in range(2):
        upper = evens["gx"] if side == 0 else jnp.logical_not(evens["gx"])
        first = jnp.where(upper, row_count - width, 0)
        for y in range(width):
            total[first + y] += dx[side, y]
    for side in range(2):
        upper = evens["gy"] if side == 0 else jnp.logical_not(evens["gy"])
        place = jnp.where(upper, width - 1, 0)
        for x in range(planes):
            total[place + x * width] += dy[side, x]
    shape = (rows, depth)
    lane = lanes_of(shape)
    even = jnp.broadcast_to(evens["sec"], shape)
    high = jnp.where(even, dz[0], dz[1])
    low = jnp.where(even, dz[1], dz[0])
    high = pltpu.roll(high, depth - 1, axis=1)
    for plane in range(planes):
        for r in range(plane * width, (plane + 1) * width):
            turned = depth - r if r else 0
            a = pltpu.roll(low, turned, axis=1) if r else low
            b = pltpu.roll(high, turned, axis=1) if r else high
            total[r] += jnp.where(lane == 0, a, jnp.where(lane == depth - 1, b, 0.0))
        span = pl.ds(plane * width, width)
        for k in range(species):
            pltpu.make_async_copy(
                total.at[span, k, :], out.at[k, span], sem.at[plane]
            ).start()
    for plane in range(planes):
        span = pl.ds(plane * width, width)
        pltpu.make_async_copy(
            total.at[pl.ds(0, species), pl.ds(0, width), :], out.at[:, span], sem.at[plane]
        ).wait()


def means_kernel(*refs):
    terms, out = refs[:-1], refs[-1]
    species, per_device, bins = out.shape
    for s in range(0, per_device, 2):
        block = sum((term[s // 2] for term in terms[1:]), terms[0][s // 2])
        means = block / jnp.maximum(block[species + 1 : species + 2], 1.0)
        out[:, s, :] = means[:species, :bins]
        out[:, s + 1, :] = means[:species, bins:]


def struct(*shape):
    return jax.ShapeDtypeStruct(shape, F32)


def call(kernel, name, out_shape, n_in, out_specs, in_specs=None, scratch=(), flops=0, moved=0):
    return pl.pallas_call(
        kernel,
        out_shape=out_shape,
        in_specs=in_specs or [VMEM] * n_in,
        out_specs=out_specs,
        scratch_shapes=list(scratch),
        name=name,
        compiler_params=pltpu.CompilerParams(vmem_limit_bytes=32 * 1024 * 1024),
        cost_estimate=pl.CostEstimate(flops=flops, bytes_accessed=moved, transcendentals=0),
    )


def joint(block, axis, source):
    deep, count = lax.axis_size("sec"), lax.axis_size(axis)
    pairs = []
    for s in range(deep):
        for i in range(count):
            t, j = source(s, i)
            pairs.append((t * count + j, s * count + i))
    return lax.ppermute(block, ("sec", axis), pairs)


def swapped(block, axis, side):
    count = lax.axis_size(axis)
    if side == 0:
        return lax.ppermute(block, axis, [(i, i ^ 1) for i in range(count)])
    if axis == "sec":
        pairs = [(i, ((i + 1) ^ 1) - 1) for i in range(1, count - 1)]
        return lax.ppermute(block, axis, [*pairs, (0, count - 1), (count - 1, 0)])
    return joint(
        block,
        axis,
        lambda s, i: (s, ((i + 1) ^ 1) - 1) if 0 < i < count - 1 else (s ^ 1, i),
    )


def summed(block):
    deep, gx, gy = (lax.axis_size(axis) for axis in ("sec", "gx", "gy"))
    half = block.shape[0] // 2
    block = block + lax.ppermute(block, "sec", [(i, i ^ 1) for i in range(deep)])
    block = block[:half] + joint(block[half:], "gx", lambda s, i: (s ^ 1, (i - 1) % gx))
    steps = [(1 << n, 0) for n in range(1, deep.bit_length() - 1)]
    steps += [(0, 1 << n) for n in range(gy.bit_length() - 1)]
    terms = [block]
    while steps:
        (a, b), (c, d) = steps.pop(0), steps.pop(0) if steps else (0, 0)
        block = sum(terms[1:], terms[0])
        terms = [block]
        for e, f in dict.fromkeys([(a, b), (c, d), (a ^ c, b ^ d)]):
            if e or f:
                terms.append(joint(block, "gy", lambda s, i: (s ^ 1 ^ e, i ^ f)))
    return terms


def on_device(
    composition_matrix,
    local_mixing_coefficient,
    thermal_field,
    component_mixing_weight,
    kinetics_jacobian,
    mixture_classes,
    streamwise_positions,
):
    species, planes, width, depth = composition_matrix.shape
    row_count = planes * width
    rows = padded_rows(species)
    cells = composition_matrix.reshape(species, row_count, depth)
    mixing = local_mixing_coefficient.reshape(row_count, depth)
    thermal = thermal_field.reshape(row_count, depth)
    classes = mixture_classes.reshape(row_count, depth)
    weights = component_mixing_weight.reshape(1, species)
    positions = streamwise_positions.reshape(1, -1)
    per_device = planes // 2
    has_b = tuple(lax.axis_size(axis) > 2 for axis in ("gx", "gy", "sec"))
    shapes = {"gx": (width, rows, depth), "gy": (planes, rows, depth), "sec": (rows, row_count)}
    sides = [
        (axis, side)
        for axis, both in zip(("gx", "gy", "sec"), has_b)
        for side in range(1 + both)
    ]
    face_shapes = [struct(*shapes[axis]) for axis, _ in sides]

    in_hbm = [pltpu.with_memory_space_constraint(x, pltpu.HBM) for x in (cells, mixing, classes)]
    mixing, classes, *gx_faces = call(
        functools.partial(gx_face_kernel, planes, has_b[0]),
        "outer_planes",
        [
            struct(row_count, depth),
            jax.ShapeDtypeStruct((row_count, depth), jnp.int32),
            *[shape for shape, (axis, _) in zip(face_shapes, sides) if axis == "gx"],
        ],
        3,
        [VMEM] * (3 + has_b[0]),
        in_specs=[ANY] * 3,
        scratch=[pltpu.SemaphoreType.DMA((2,)), pltpu.SemaphoreType.DMA((2,))],
    )(*in_hbm)
    rows_in, own_z, *faces = call(
        functools.partial(rows_kernel, planes, has_b[1:]),
        "rows",
        [
            struct(row_count, rows, depth),
            struct(2, rows, row_count),
            *[shape for shape, (axis, _) in zip(face_shapes, sides) if axis != "gx"],
        ],
        3,
        [VMEM] * (2 + len(sides) - len(gx_faces)),
        flops=4_000_000,
        moved=3_000_000,
    )(cells, mixing, classes)
    faces = [*gx_faces, *faces]
    halos = [swapped(face, axis, side) for face, (axis, side) in zip(faces, sides)]

    inner, sums = call(
        functools.partial(inner_kernel, planes),
        "inside",
        [struct(row_count, rows, depth), struct(per_device + 1, rows, NB)],
        5,
        [VMEM] * 2,
        scratch=[
            pltpu.VMEM((8, row_count, depth), F32),
            pltpu.VMEM((2 * rows, 2 * rows), F32),
        ],
        flops=10_000_000,
        moved=4_000_000,
    )(rows_in, mixing, thermal, weights, kinetics_jacobian)

    window, dx, dy, dz = call(
        functools.partial(edge_kernel, planes, has_b),
        "edges",
        [
            struct(per_device, rows, 2 * NB),
            struct(2, width, rows, depth),
            struct(2, planes, rows, depth),
            struct(2, rows, row_count),
        ],
        5 + len(halos),
        [VMEM] * 4,
        scratch=[pltpu.VMEM((per_device + 1, rows, NB), F32)],
    )(rows_in, own_z, sums, weights, positions, *halos)

    terms = summed(window)
    advanced = call(
        functools.partial(finish_kernel, planes),
        "advance",
        struct(species, row_count, depth),
        4,
        ANY,
        scratch=[
            pltpu.VMEM((row_count, rows, depth), F32),
            pltpu.SemaphoreType.DMA((planes,)),
        ],
        flops=1_000_000,
        moved=3_000_000,
    )(inner, dx, dy, dz)
    cond_means = call(
        means_kernel, "means", struct(species, per_device, NB), len(terms), VMEM
    )(*terms)
    return advanced.reshape(composition_matrix.shape), cond_means


def solution(mesh):
    in_specs = (
        P(None, "gx", "gy", "sec"),
        P("gx", "gy", "sec"),
        P("gx", "gy", "sec"),
        P(),
        P(),
        P("gx", "gy", "sec"),
        P(),
    )
    out_specs = (P(None, "gx", "gy", "sec"), P(None, "gx", None))
    return jax.shard_map(
        on_device, mesh=mesh, in_specs=in_specs, out_specs=out_specs, check_vma=False
    )
```

```python
import functools

import jax
import jax.numpy as jnp
from jax import lax
from jax.experimental import pallas as pl
from jax.experimental.pallas import tpu as pltpu
from jax.sharding import PartitionSpec as P

NB = 64
SUBLANES = 8
LANES = 128
F32 = jnp.float32
BF16 = jnp.bfloat16
VMEM = pl.BlockSpec(memory_space=pltpu.VMEM)
ANY = pl.BlockSpec(memory_space=pl.ANY)
DT = 0.05
AHEAD = 2


def padded_rows(species):
    return -(-(species + 2) // SUBLANES) * SUBLANES


def lanes_of(shape):
    return lax.broadcasted_iota(jnp.int32, shape, len(shape) - 1)


def rows_of(shape):
    return lax.broadcasted_iota(jnp.int32, shape, len(shape) - 2)


def halves(block):
    high = block.astype(BF16).astype(F32)
    return jnp.concatenate([high, block - high], axis=0).astype(BF16)


def weight_column(weights_ref, rows):
    species = weights_ref.shape[1]
    shape = (rows, species)
    spread = jnp.where(rows_of(shape) == lanes_of(shape), weights_ref[...], 0.0)
    return DT * jnp.sum(spread, axis=1, keepdims=True)


def hits(classes):
    shape = (NB, classes.shape[1])
    bins = jnp.broadcast_to(classes.astype(BF16), shape)
    found = bins == rows_of(shape).astype(F32).astype(BF16)
    return jnp.where(found, jnp.ones((), BF16), jnp.zeros((), BF16))


def binned(values, hit):
    return lax.dot_general(
        values, hit, (((1,), (1,)), ((), ())), preferred_element_type=F32
    )


def folded(product):
    rows = product.shape[0] // 2
    return product[:rows] + product[rows:]


def upper_of(axis, side):
    even = lax.axis_index(axis) % 2 == 0
    return even if side == 0 else jnp.logical_not(even)


def has_neighbour(axis, side):
    if side == 0:
        return True
    edge = jnp.where(upper_of(axis, 1), lax.axis_size(axis) - 1, 0)
    return lax.axis_index(axis) != edge


def face_rows(axis, upper, planes, width):
    if axis == "gx":
        return jnp.where(upper, (planes - 1) * width, 0), 1, width
    return jnp.where(upper, width - 1, 0), width, planes


def pack_kernel(planes, has_b, cells, mixing, classes, *refs):
    outs, (bins, sem, field_sem) = refs[:-3], refs[-3:]
    rows_out, own_z = outs[0], outs[1]
    faces = list(outs[2:])
    species, row_count, depth = cells.shape
    rows = rows_out.shape[1]
    width = row_count // planes
    chunk = row_count // sem.shape[0]
    field_copies = [
        pltpu.make_async_copy(mixing, rows_out.at[:, species, :], field_sem.at[0]),
        pltpu.make_async_copy(classes, bins, field_sem.at[1]),
    ]
    for copy in field_copies:
        copy.start()
    for n in range(sem.shape[0]):
        span = pl.ds(n * chunk, chunk)
        for k in range(species):
            pltpu.make_async_copy(
                cells.at[k, span], rows_out.at[span, k, :], sem.at[n]
            ).start()

    lane = lanes_of((SUBLANES, depth))
    zero = jnp.zeros((SUBLANES, depth), F32)

    def gathered(groups, span, low, high):
        low, high = list(low), list(high)
        for r in span:
            at, before = lane == r, lane == (r - 1) % depth
            for i, g in enumerate(groups):
                block = rows_out[r, pl.ds(g, SUBLANES), :]
                turned = pltpu.roll(block, r, axis=1) if r else block
                low[i] = jnp.where(at, turned, low[i])
                high[i] = jnp.where(before, turned, high[i])
        return low, high

    whole = species // SUBLANES * SUBLANES
    first = range(0, whole, SUBLANES)
    rest = range(whole, rows, SUBLANES)
    low, high = [zero] * len(first), [zero] * len(first)
    for n in range(sem.shape[0]):
        arrived = rows_out.at[pl.ds(n * chunk, chunk), pl.ds(0, species), :]
        pltpu.make_async_copy(arrived, arrived, sem.at[n]).wait()
        low, high = gathered(first, range(n * chunk, (n + 1) * chunk), low, high)
    for copy in field_copies:
        copy.wait()
    for r in range(0, row_count, SUBLANES):
        span = pl.ds(r, SUBLANES)
        rows_out[span, species + 1, :] = bins[span, :].astype(F32)
    lows, highs = gathered(rest, range(row_count), [zero] * len(rest), [zero] * len(rest))
    for i, g in enumerate([*first, *rest]):
        own_z[0, pl.ds(g, SUBLANES), :] = (low + lows)[i]
        own_z[1, pl.ds(g, SUBLANES), :] = pltpu.roll((high + highs)[i], 1, axis=1)
    for axis, both in zip(("gx", "gy", "sec"), has_b):
        for side in range(1 + both):
            out = faces.pop(0)
            upper = upper_of(axis, side)
            if axis == "sec":
                out[...] = own_z[jnp.where(upper, 1, 0)]
                continue
            start, step, count = face_rows(axis, upper, planes, width)
            for i in range(count):
                r = start + i * step
                out[pl.ds(i, 1), :] = rows_out[r, pl.ds(species, 1), :]
                out[pl.ds(count + i, 1), :] = rows_out[r, pl.ds(species + 1, 1), :]


def wide_face_kernel(planes, has_b, cells, held, *faces):
    faces = list(faces)
    width = cells.shape[0] // planes
    for axis, both in zip(("gx", "gy"), has_b):
        for side in range(1 + both):
            out = faces.pop(0)
            start, step, count = face_rows(axis, upper_of(axis, side), planes, width)
            for i in range(count):
                out[i] = cells[start + i * step]


def inner_kernel(
    planes, cells, mixing, thermal, weights, jacobian, advanced, station_sums, coefs, square
):
    row_count, rows, depth = cells.shape
    species = jacobian.shape[0]
    width = row_count // planes
    shape = (row_count, depth)
    lane, row = lanes_of(shape), rows_of(shape)
    mix = mixing[...]
    up = 0.5 * (mix + pltpu.roll(mix, depth - 1, axis=1))
    up = jnp.where(lane == depth - 1, 0.0, up)
    coefs[0] = up
    down = pltpu.roll(up, 1, axis=1)
    coefs[1] = down
    total = up + down
    up = 0.5 * (mix + pltpu.roll(mix, row_count - 1, axis=0))
    up = jnp.where(row % width == width - 1, 0.0, up)
    coefs[2] = up
    down = pltpu.roll(up, 1, axis=0)
    coefs[3] = down
    total = total + (up + down)
    edge = jnp.zeros((width, depth), F32)
    up = jnp.concatenate([0.5 * (mix[: row_count - width] + mix[width:]), edge], axis=0)
    coefs[4] = up
    down = jnp.concatenate([edge, up[: row_count - width]], axis=0)
    coefs[5] = down
    coefs[6] = total + (up + down)
    coefs[7] = (4.0 * DT) * jnp.exp(-2.0 / thermal[...])

    square[...] = jnp.zeros_like(square)
    matrix = jacobian[...]
    matrix_high = matrix.astype(BF16).astype(F32)
    square[:species, :species] = matrix_high
    square[:species, rows : rows + species] = matrix_high
    square[rows : rows + species, :species] = matrix - matrix_high
    left = square[...].astype(BF16)

    weight = jnp.broadcast_to(weight_column(weights, rows), (rows, depth))
    whole = species // SUBLANES * SUBLANES
    ones = rows_of((rows - whole, depth)) >= species - whole
    station_sums[...] = jnp.zeros_like(station_sums)

    def kinetics(pair):
        wide = jnp.concatenate([halves(cells[r]) for r in pair], axis=1)
        return folded(jnp.dot(left, wide, preferred_element_type=F32))

    def advance(pair, mixed):
        values, found = [], []
        for i, r in enumerate(pair):
            x, y = divmod(r, width)
            c = cells[r]
            at = lambda n: coefs[n, pl.ds(r, 1), :]
            flux = at(0) * pltpu.roll(c, depth - 1, axis=1)
            flux += at(1) * pltpu.roll(c, 1, axis=1)
            if y < width - 1:
                flux += at(2) * cells[r + 1]
            if y > 0:
                flux += at(3) * cells[r - 1]
            if x < planes - 1:
                flux += at(4) * cells[r + width]
            if x > 0:
                flux += at(5) * cells[r - width]
            flux -= at(6) * c
            new = c + weight * flux + at(7) * mixed[:, i * depth : (i + 1) * depth]
            new = jnp.concatenate([new[:whole], jnp.where(ones, 1.0, new[whole:])], axis=0)
            advanced[r] = new
            values.append(halves(new))
            found.append(hits(cells[r, species + 1 : species + 2, :]))
        return jnp.concatenate(values, axis=1), jnp.concatenate(found, axis=1)

    pairs = [(r, r + 1) for r in range(0, row_count, 2)]
    mixed, values, made = {}, {}, 0.0
    for t in range(len(pairs) + 2 * AHEAD):
        if t < len(pairs):
            mixed[t] = kinetics(pairs[t])
        now = t - AHEAD
        if 0 <= now < len(pairs):
            values[now] = advance(pairs[now], mixed.pop(now))
        last = now - AHEAD
        if 0 <= last < len(pairs):
            made += binned(*values.pop(last))
            x, y = divmod(pairs[last][1], width)
            if y == width - 1:
                station_sums[(x + 1) // 2] += folded(made)
                made = 0.0


def edge_kernel(planes, has_b, cells, own_z, sums, weights, positions, *refs):
    halos = list(refs[: 3 + sum(has_b)])
    window, dz, station_sums = refs[3 + sum(has_b) :]
    row_count, rows, depth = cells.shape
    species = weights.shape[1]
    width = row_count // planes
    weight = jnp.broadcast_to(weight_column(weights, rows), (rows, depth))
    received = {}
    for axis, both in zip(("gx", "gy", "sec"), has_b):
        received[axis] = [halos.pop(0), halos.pop(0) if both else None]
    station_sums[...] = sums[...]

    for axis in ("gx", "gy"):
        for side in range(2):
            halo = received[axis][side]
            start, step, count = face_rows(axis, upper_of(axis, side), planes, width)
            there = jnp.zeros((2 * count, depth), F32)
            there = there if halo is None else halo[...]
            if side and halo is not None:
                inside = jnp.broadcast_to(has_neighbour(axis, side), there.shape)
                outside = jnp.where(rows_of(there.shape) < count, 0.0, -1.0)
                there = jnp.where(inside, there, outside)
            if halo is None:
                there = jnp.where(rows_of(there.shape) < count, 0.0, -1.0)
            made = jnp.zeros((2 * rows, NB), F32)
            for first in range(0, count, 2):
                values, found = [], []
                for i in (first, first + 1):
                    c = cells[start + i * step]
                    d = 0.5 * (c[species : species + 1] + there[i : i + 1])
                    values.append(halves(weight * d * c))
                    found.append(
                        hits(there[count + i : count + i + 1]) - hits(c[species + 1 : species + 2])
                    )
                if axis == "gx":
                    made += binned(
                        jnp.concatenate(values, axis=1), jnp.concatenate(found, axis=1)
                    )
                else:
                    for i, value, hit in zip((first, first + 1), values, found):
                        station_sums[(i + 1) // 2] += folded(binned(value, hit))
            if axis == "gx":
                plane = jnp.where(upper_of(axis, side), planes - 1, 0)
                station_sums[(plane + 1) // 2] += folded(made)

    stations = planes // 2 + 1
    lane = lanes_of((1, row_count))
    station = ((lane // width + 1) // 2).astype(F32)
    for side in range(2):
        c = own_z[jnp.where(upper_of("sec", side), 1, 0)]
        halo = received["sec"][side]
        if halo is None:
            halo = jnp.zeros_like(c)
        else:
            halo = jnp.where(
                jnp.broadcast_to(has_neighbour("sec", side), halo.shape), halo[...], 0.0
            )
        d = 0.5 * (c[species : species + 1] + halo[species : species + 1])
        delta = weight * d * (halo - c)
        dz[side] = delta
        value = halves(delta)
        classes = c[species + 1 : species + 2]
        for j in range(stations):
            station_sums[j] += folded(binned(value, hits(jnp.where(station == j, classes, -1.0))))
    shift = jnp.broadcast_to(positions[0:1, 0:1], (rows, NB))
    per_device = planes // 2
    for s in range(0, 2 * per_device, 2):
        parts = []
        for slot in (s, s + 1):
            part = jnp.zeros((rows, NB), F32)
            for j in range(stations):
                if 0 <= slot - j < per_device:
                    part += jnp.where(shift == slot - j, station_sums[j], 0.0)
            parts.append(part)
        window[s // 2] = jnp.concatenate(parts, axis=1)


def finish_kernel(planes, has_b, cells, advanced, dz, weights, *refs):
    halos = list(refs[: 2 + sum(has_b)])
    out, finished, total, sem = refs[2 + sum(has_b) :]
    finished[...] = jnp.zeros_like(finished)
    row_count, rows, depth = advanced.shape
    species = out.shape[0]
    width = row_count // planes
    weight = jnp.broadcast_to(weight_column(weights, rows), (rows, depth))
    total[...] = advanced[...]
    for axis, both in zip(("gx", "gy"), has_b):
        for side in range(2):
            halo = halos.pop(0) if side <= both else None
            start, step, count = face_rows(axis, upper_of(axis, side), planes, width)
            inside = jnp.broadcast_to(has_neighbour(axis, side), (rows, depth))
            for i in range(count):
                r = start + i * step
                c = cells[r]
                there = jnp.zeros_like(c) if halo is None else halo[i]
                if side:
                    there = jnp.where(inside, there, 0.0)
                d = 0.5 * (c[species : species + 1] + there[species : species + 1])
                total[r] += weight * d * (there - c)
    shape = (rows, depth)
    lane = lanes_of(shape)
    even = jnp.broadcast_to(upper_of("sec", 0), shape)
    high = jnp.where(even, dz[0], dz[1])
    low = jnp.where(even, dz[1], dz[0])
    high = pltpu.roll(high, depth - 1, axis=1)
    for plane in range(planes):
        for r in range(plane * width, (plane + 1) * width):
            turned = depth - r if r else 0
            a = pltpu.roll(low, turned, axis=1) if r else low
            b = pltpu.roll(high, turned, axis=1) if r else high
            total[r] += jnp.where(lane == 0, a, jnp.where(lane == depth - 1, b, 0.0))
        span = pl.ds(plane * width, width)
        for k in range(species):
            pltpu.make_async_copy(
                total.at[span, k, :], out.at[k, span], sem.at[plane]
            ).start()
    for plane in range(planes):
        span = pl.ds(plane * width, width)
        pltpu.make_async_copy(
            total.at[pl.ds(0, species), pl.ds(0, width), :], out.at[:, span], sem.at[plane]
        ).wait()


def means_kernel(after, *refs):
    terms, out = refs[:-1], refs[-1]
    species, per_device, bins = out.shape
    for s in range(0, per_device, 2):
        block = sum((term[s // 2] for term in terms[1:]), terms[0][s // 2])
        means = block / jnp.maximum(block[species + 1 : species + 2], 1.0)
        out[:, s, :] = means[:species, :bins]
        out[:, s + 1, :] = means[:species, bins:]


def struct(*shape):
    return jax.ShapeDtypeStruct(shape, F32)


def call(kernel, name, out_shape, n_in, out_specs, in_specs=None, scratch=(), flops=0, moved=0):
    return pl.pallas_call(
        kernel,
        out_shape=out_shape,
        in_specs=in_specs or [VMEM] * n_in,
        out_specs=out_specs,
        scratch_shapes=list(scratch),
        name=name,
        compiler_params=pltpu.CompilerParams(vmem_limit_bytes=32 * 1024 * 1024),
        cost_estimate=pl.CostEstimate(flops=flops, bytes_accessed=moved, transcendentals=0),
    )


def joint(block, axis, source):
    deep, count = lax.axis_size("sec"), lax.axis_size(axis)
    pairs = []
    for s in range(deep):
        for i in range(count):
            t, j = source(s, i)
            pairs.append((t * count + j, s * count + i))
    return lax.ppermute(block, ("sec", axis), pairs)


def swapped(block, axis, side):
    count = lax.axis_size(axis)
    if side == 0:
        return lax.ppermute(block, axis, [(i, i ^ 1) for i in range(count)])
    if axis == "sec":
        pairs = [(i, ((i + 1) ^ 1) - 1) for i in range(1, count - 1)]
        return lax.ppermute(block, axis, [*pairs, (0, count - 1), (count - 1, 0)])
    return joint(
        block,
        axis,
        lambda s, i: (s, ((i + 1) ^ 1) - 1) if 0 < i < count - 1 else (s ^ 1, i),
    )


def summed(block):
    deep, gx, gy = (lax.axis_size(axis) for axis in ("sec", "gx", "gy"))
    half = block.shape[0] // 2
    block = block[:half] + joint(block[half:], "gx", lambda s, i: (s ^ 1, (i - 1) % gx))
    steps = [(1 << n, 0) for n in range(1, deep.bit_length() - 1)]
    steps += [(0, 1 << n) for n in range(gy.bit_length() - 1)]
    terms = [block]
    for e, f in steps:
        block = sum(terms[1:], terms[0])
        terms = [block, joint(block, "gy", lambda s, i: (s ^ 1 ^ e, i ^ f))]
    return terms


def on_device(
    composition_matrix,
    local_mixing_coefficient,
    thermal_field,
    component_mixing_weight,
    kinetics_jacobian,
    mixture_classes,
    streamwise_positions,
):
    species, planes, width, depth = composition_matrix.shape
    row_count = planes * width
    rows = padded_rows(species)
    cells = composition_matrix.reshape(species, row_count, depth)
    mixing = local_mixing_coefficient.reshape(row_count, depth)
    thermal = thermal_field.reshape(row_count, depth)
    classes = mixture_classes.reshape(row_count, depth)
    weights = component_mixing_weight.reshape(1, species)
    positions = streamwise_positions.reshape(1, -1)
    per_device = planes // 2
    has_b = tuple(lax.axis_size(axis) > 2 for axis in ("gx", "gy", "sec"))
    sides = [
        (axis, side)
        for axis, both in zip(("gx", "gy", "sec"), has_b)
        for side in range(1 + both)
    ]
    narrow = {
        "gx": struct(2 * width, depth),
        "gy": struct(2 * planes, depth),
        "sec": struct(rows, row_count),
    }
    wide = {"gx": struct(width, rows, depth), "gy": struct(planes, rows, depth)}

    rows_in, own_z, *faces = call(
        functools.partial(pack_kernel, planes, has_b),
        "faces",
        [
            struct(row_count, rows, depth),
            struct(2, rows, row_count),
            *[narrow[axis] for axis, _ in sides],
        ],
        3,
        [VMEM] * (2 + len(sides)),
        in_specs=[ANY] * 3,
        scratch=[
            pltpu.VMEM((row_count, depth), jnp.int32),
            pltpu.SemaphoreType.DMA((planes // 2,)),
            pltpu.SemaphoreType.DMA((2,)),
        ],
    )(*[pltpu.with_memory_space_constraint(x, pltpu.HBM) for x in (cells, mixing, classes)])
    halos = [swapped(face, axis, side) for face, (axis, side) in zip(faces, sides)]

    inner, sums = call(
        functools.partial(inner_kernel, planes),
        "inside",
        [struct(row_count, rows, depth), struct(per_device + 1, rows, NB)],
        5,
        [VMEM] * 2,
        scratch=[
            pltpu.VMEM((8, row_count, depth), F32),
            pltpu.VMEM((2 * rows, 2 * rows), F32),
        ],
        flops=10_000_000,
        moved=4_000_000,
    )(rows_in, mixing, thermal, weights, kinetics_jacobian)

    window, dz = call(
        functools.partial(edge_kernel, planes, has_b),
        "edges",
        [struct(per_device, rows, 2 * NB), struct(2, rows, row_count)],
        5 + len(halos),
        [VMEM] * 2,
        scratch=[pltpu.VMEM((per_device + 1, rows, NB), F32)],
    )(rows_in, own_z, sums, weights, positions, *halos)

    deep = lax.axis_size("sec")
    window = window + lax.ppermute(window, "sec", [(i, i ^ 1) for i in range(deep)])
    terms = summed(window)

    wide_sides = [(axis, side) for axis, side in sides if axis != "sec"]
    wide_faces = call(
        functools.partial(wide_face_kernel, planes, has_b),
        "wide_faces",
        [wide[axis] for axis, _ in wide_sides],
        2,
        [VMEM] * len(wide_sides),
    )(rows_in, window)
    wide_halos = [swapped(face, axis, side) for face, (axis, side) in zip(wide_faces, wide_sides)]
    advanced, finished = call(
        functools.partial(finish_kernel, planes, has_b[:2]),
        "advance",
        [struct(species, row_count, depth), struct(SUBLANES, LANES)],
        4 + len(wide_halos),
        [ANY, VMEM],
        scratch=[
            pltpu.VMEM((row_count, rows, depth), F32),
            pltpu.SemaphoreType.DMA((planes,)),
        ],
        flops=1_000_000,
        moved=3_000_000,
    )(rows_in, inner, dz, weights, *wide_halos)
    cond_means = call(
        means_kernel, "means", struct(species, per_device, NB), 1 + len(terms), VMEM
    )(finished, *terms)
    return advanced.reshape(composition_matrix.shape), cond_means


def solution(mesh):
    in_specs = (
        P(None, "gx", "gy", "sec"),
        P("gx", "gy", "sec"),
        P("gx", "gy", "sec"),
        P(),
        P(),
        P("gx", "gy", "sec"),
        P(),
    )
    out_specs = (P(None, "gx", "gy", "sec"), P(None, "gx", None))
    return jax.shard_map(
        on_device, mesh=mesh, in_specs=in_specs, out_specs=out_specs, check_vma=False
    )
```

```python
import functools

import jax
import jax.numpy as jnp
from jax import lax
from jax.experimental import pallas as pl
from jax.experimental.pallas import tpu as pltpu
from jax.sharding import PartitionSpec as P

NB = 64
SUBLANES = 8
LANES = 128
F32 = jnp.float32
BF16 = jnp.bfloat16
VMEM = pl.BlockSpec(memory_space=pltpu.VMEM)
ANY = pl.BlockSpec(memory_space=pl.ANY)
DT = 0.05
AHEAD = 2


def padded_rows(species):
    return -(-(species + 2) // SUBLANES) * SUBLANES


def lanes_of(shape):
    return lax.broadcasted_iota(jnp.int32, shape, len(shape) - 1)


def rows_of(shape):
    return lax.broadcasted_iota(jnp.int32, shape, len(shape) - 2)


def halves(block):
    high = block.astype(BF16).astype(F32)
    return jnp.concatenate([high, block - high], axis=0).astype(BF16)


def weight_column(weights_ref, rows):
    species = weights_ref.shape[1]
    shape = (rows, species)
    spread = jnp.where(rows_of(shape) == lanes_of(shape), weights_ref[...], 0.0)
    return DT * jnp.sum(spread, axis=1, keepdims=True)


def hits(classes):
    shape = (NB, classes.shape[1])
    bins = jnp.broadcast_to(classes.astype(BF16), shape)
    found = bins == rows_of(shape).astype(F32).astype(BF16)
    return jnp.where(found, jnp.ones((), BF16), jnp.zeros((), BF16))


def binned(values, hit):
    return lax.dot_general(
        values, hit, (((1,), (1,)), ((), ())), preferred_element_type=F32
    )


def folded(product):
    rows = product.shape[0] // 2
    return product[:rows] + product[rows:]


def upper_of(axis, side):
    even = lax.axis_index(axis) % 2 == 0
    return even if side == 0 else jnp.logical_not(even)


def has_neighbour(axis, side):
    if side == 0:
        return True
    edge = jnp.where(upper_of(axis, 1), lax.axis_size(axis) - 1, 0)
    return lax.axis_index(axis) != edge


def face_rows(axis, upper, planes, width):
    if axis == "gx":
        return jnp.where(upper, (planes - 1) * width, 0), 1, width
    return jnp.where(upper, width - 1, 0), width, planes


def pack_kernel(planes, has_b, cells, mixing, classes, *refs):
    outs, (bins, sem, field_sem) = refs[:-3], refs[-3:]
    rows_out, own_z = outs[0], outs[1]
    faces = list(outs[2:])
    species, row_count, depth = cells.shape
    rows = rows_out.shape[1]
    width = row_count // planes
    chunk = row_count // sem.shape[0]
    field_copies = [
        pltpu.make_async_copy(mixing, rows_out.at[:, species, :], field_sem.at[0]),
        pltpu.make_async_copy(classes, bins, field_sem.at[1]),
    ]
    for copy in field_copies:
        copy.start()
    for n in range(sem.shape[0]):
        span = pl.ds(n * chunk, chunk)
        for k in range(species):
            pltpu.make_async_copy(
                cells.at[k, span], rows_out.at[span, k, :], sem.at[n]
            ).start()

    lane = lanes_of((SUBLANES, depth))
    zero = jnp.zeros((SUBLANES, depth), F32)

    def gathered(groups, span, low, high):
        low, high = list(low), list(high)
        for r in span:
            at, before = lane == r, lane == (r - 1) % depth
            for i, g in enumerate(groups):
                block = rows_out[r, pl.ds(g, SUBLANES), :]
                turned = pltpu.roll(block, r, axis=1) if r else block
                low[i] = jnp.where(at, turned, low[i])
                high[i] = jnp.where(before, turned, high[i])
        return low, high

    whole = species // SUBLANES * SUBLANES
    first = range(0, whole, SUBLANES)
    rest = range(whole, rows, SUBLANES)
    low, high = [zero] * len(first), [zero] * len(first)
    for n in range(sem.shape[0]):
        arrived = rows_out.at[pl.ds(n * chunk, chunk), pl.ds(0, species), :]
        pltpu.make_async_copy(arrived, arrived, sem.at[n]).wait()
        low, high = gathered(first, range(n * chunk, (n + 1) * chunk), low, high)
    for copy in field_copies:
        copy.wait()
    for r in range(0, row_count, SUBLANES):
        span = pl.ds(r, SUBLANES)
        rows_out[span, species + 1, :] = bins[span, :].astype(F32)
    lows, highs = gathered(rest, range(row_count), [zero] * len(rest), [zero] * len(rest))
    for i, g in enumerate([*first, *rest]):
        own_z[0, pl.ds(g, SUBLANES), :] = (low + lows)[i]
        own_z[1, pl.ds(g, SUBLANES), :] = pltpu.roll((high + highs)[i], 1, axis=1)
    for axis, both in zip(("gx", "gy", "sec"), has_b):
        for side in range(1 + both):
            out = faces.pop(0)
            upper = upper_of(axis, side)
            if axis == "sec":
                out[pl.ds(0, rows), :] = own_z[jnp.where(upper, 1, 0)]
                continue
            start, step, count = face_rows(axis, upper, planes, width)
            for i in range(count):
                r = start + i * step
                if axis == "gy":
                    out[i] = rows_out[r]
                else:
                    out[pl.ds(i, 1), :] = rows_out[r, pl.ds(species, 1), :]
                    out[pl.ds(count + i, 1), :] = rows_out[r, pl.ds(species + 1, 1), :]


def plane_kernel(planes, cells, held, *faces):
    width = cells.shape[0] // planes
    for side, out in enumerate(faces):
        start, step, count = face_rows("gx", upper_of("gx", side), planes, width)
        for i in range(count):
            out[i] = cells[start + i * step]


def inner_kernel(
    planes, cells, mixing, thermal, weights, jacobian, advanced, station_sums, coefs, square
):
    row_count, rows, depth = cells.shape
    species = jacobian.shape[0]
    width = row_count // planes
    shape = (row_count, depth)
    lane, row = lanes_of(shape), rows_of(shape)
    mix = mixing[...]
    up = 0.5 * (mix + pltpu.roll(mix, depth - 1, axis=1))
    up = jnp.where(lane == depth - 1, 0.0, up)
    coefs[0] = up
    down = pltpu.roll(up, 1, axis=1)
    coefs[1] = down
    total = up + down
    up = 0.5 * (mix + pltpu.roll(mix, row_count - 1, axis=0))
    up = jnp.where(row % width == width - 1, 0.0, up)
    coefs[2] = up
    down = pltpu.roll(up, 1, axis=0)
    coefs[3] = down
    total = total + (up + down)
    edge = jnp.zeros((width, depth), F32)
    up = jnp.concatenate([0.5 * (mix[: row_count - width] + mix[width:]), edge], axis=0)
    coefs[4] = up
    down = jnp.concatenate([edge, up[: row_count - width]], axis=0)
    coefs[5] = down
    coefs[6] = total + (up + down)
    coefs[7] = (4.0 * DT) * jnp.exp(-2.0 / thermal[...])

    square[...] = jnp.zeros_like(square)
    matrix = jacobian[...]
    matrix_high = matrix.astype(BF16).astype(F32)
    square[:species, :species] = matrix_high
    square[:species, rows : rows + species] = matrix_high
    square[rows : rows + species, :species] = matrix - matrix_high
    left = square[...].astype(BF16)

    weight = jnp.broadcast_to(weight_column(weights, rows), (rows, depth))
    whole = species // SUBLANES * SUBLANES
    ones = rows_of((rows - whole, depth)) >= species - whole
    station_sums[...] = jnp.zeros_like(station_sums)

    def kinetics(pair):
        wide = jnp.concatenate([halves(cells[r]) for r in pair], axis=1)
        return folded(jnp.dot(left, wide, preferred_element_type=F32))

    def advance(pair, mixed):
        values, found = [], []
        for i, r in enumerate(pair):
            x, y = divmod(r, width)
            c = cells[r]
            at = lambda n: coefs[n, pl.ds(r, 1), :]
            flux = at(0) * pltpu.roll(c, depth - 1, axis=1)
            flux += at(1) * pltpu.roll(c, 1, axis=1)
            if y < width - 1:
                flux += at(2) * cells[r + 1]
            if y > 0:
                flux += at(3) * cells[r - 1]
            if x < planes - 1:
                flux += at(4) * cells[r + width]
            if x > 0:
                flux += at(5) * cells[r - width]
            flux -= at(6) * c
            new = c + weight * flux + at(7) * mixed[:, i * depth : (i + 1) * depth]
            new = jnp.concatenate([new[:whole], jnp.where(ones, 1.0, new[whole:])], axis=0)
            advanced[r] = new
            values.append(halves(new))
            found.append(hits(cells[r, species + 1 : species + 2, :]))
        return jnp.concatenate(values, axis=1), jnp.concatenate(found, axis=1)

    pairs = [(r, r + 1) for r in range(0, row_count, 2)]
    mixed, values, made = {}, {}, 0.0
    for t in range(len(pairs) + 2 * AHEAD):
        if t < len(pairs):
            mixed[t] = kinetics(pairs[t])
        now = t - AHEAD
        if 0 <= now < len(pairs):
            values[now] = advance(pairs[now], mixed.pop(now))
        last = now - AHEAD
        if 0 <= last < len(pairs):
            made += binned(*values.pop(last))
            x, y = divmod(pairs[last][1], width)
            if y == width - 1:
                station_sums[(x + 1) // 2] += folded(made)
                made = 0.0


def edge_kernel(planes, has_b, cells, own_z, sums, weights, positions, *refs):
    halos = list(refs[: 3 + sum(has_b)])
    window, dz, station_sums = refs[3 + sum(has_b) :]
    row_count, rows, depth = cells.shape
    species = weights.shape[1]
    width = row_count // planes
    weight = jnp.broadcast_to(weight_column(weights, rows), (rows, depth))
    received = {}
    for axis, both in zip(("gx", "gy", "sec"), has_b):
        received[axis] = [halos.pop(0), halos.pop(0) if both else None]
    station_sums[...] = sums[...]

    for axis in ("gx", "gy"):
        for side in range(2):
            halo = received[axis][side]
            start, step, count = face_rows(axis, upper_of(axis, side), planes, width)
            inside = jnp.broadcast_to(has_neighbour(axis, side), (1, depth))

            def there(i):
                if halo is None:
                    return jnp.zeros((1, depth), F32), jnp.full((1, depth), -1.0, F32)
                if axis == "gx":
                    d, bins = halo[pl.ds(i, 1), :], halo[pl.ds(count + i, 1), :]
                else:
                    d = halo[i, pl.ds(species, 1), :]
                    bins = halo[i, pl.ds(species + 1, 1), :]
                if side:
                    d, bins = jnp.where(inside, d, 0.0), jnp.where(inside, bins, -1.0)
                return d, bins

            made = jnp.zeros((2 * rows, NB), F32)
            for first in range(0, count, 2):
                values, found = [], []
                for i in (first, first + 1):
                    c = cells[start + i * step]
                    d, bins = there(i)
                    d = 0.5 * (c[species : species + 1] + d)
                    values.append(halves(weight * d * c))
                    found.append(hits(bins) - hits(c[species + 1 : species + 2]))
                if axis == "gx":
                    made += binned(
                        jnp.concatenate(values, axis=1), jnp.concatenate(found, axis=1)
                    )
                else:
                    for i, value, hit in zip((first, first + 1), values, found):
                        station_sums[(i + 1) // 2] += folded(binned(value, hit))
            if axis == "gx":
                plane = jnp.where(upper_of(axis, side), planes - 1, 0)
                station_sums[(plane + 1) // 2] += folded(made)

    stations = planes // 2 + 1
    lane = lanes_of((1, row_count))
    station = ((lane // width + 1) // 2).astype(F32)
    for side in range(2):
        c = own_z[jnp.where(upper_of("sec", side), 1, 0)]
        halo = received["sec"][side]
        if halo is None:
            halo = jnp.zeros_like(c)
        else:
            inside = jnp.broadcast_to(has_neighbour("sec", side), c.shape)
            halo = jnp.where(inside, halo[pl.ds(0, rows), :], 0.0)
        d = 0.5 * (c[species : species + 1] + halo[species : species + 1])
        delta = weight * d * (halo - c)
        dz[side] = delta
        value = halves(delta)
        classes = c[species + 1 : species + 2]
        for j in range(stations):
            station_sums[j] += folded(binned(value, hits(jnp.where(station == j, classes, -1.0))))
    shift = jnp.broadcast_to(positions[0:1, 0:1], (rows, NB))
    per_device = planes // 2
    for s in range(0, 2 * per_device, 2):
        parts = []
        for slot in (s, s + 1):
            part = jnp.zeros((rows, NB), F32)
            for j in range(stations):
                if 0 <= slot - j < per_device:
                    part += jnp.where(shift == slot - j, station_sums[j], 0.0)
            parts.append(part)
        window[s // 2] = jnp.concatenate(parts, axis=1)


def interior_kernel(planes, advanced, dz, total, out, sem):
    row_count, rows, depth = advanced.shape
    species = out.shape[0]
    width = row_count // planes
    shape = (rows, depth)
    lane = lanes_of(shape)
    even = jnp.broadcast_to(upper_of("sec", 0), shape)
    high = jnp.where(even, dz[0], dz[1])
    low = jnp.where(even, dz[1], dz[0])
    high = pltpu.roll(high, depth - 1, axis=1)
    for plane in range(planes):
        for r in range(plane * width, (plane + 1) * width):
            turned = depth - r if r else 0
            a = pltpu.roll(low, turned, axis=1) if r else low
            b = pltpu.roll(high, turned, axis=1) if r else high
            total[r] = advanced[r] + jnp.where(
                lane == 0, a, jnp.where(lane == depth - 1, b, 0.0)
            )
        span = pl.ds(plane * width, width)
        for k in range(species):
            pltpu.make_async_copy(
                total.at[span, k, :], out.at[k, span], sem.at[plane]
            ).start()
    for plane in range(planes):
        span = pl.ds(plane * width, width)
        pltpu.make_async_copy(
            total.at[pl.ds(0, species), pl.ds(0, width), :], out.at[:, span], sem.at[plane]
        ).wait()


def last_kernel(planes, has_b, n_terms, cells, total, weights, first_out, *refs):
    halos, terms = list(refs[: 2 + sum(has_b)]), refs[2 + sum(has_b) :][:n_terms]
    out, means_out, changed, means, sem = refs[2 + sum(has_b) + n_terms :]
    row_count, rows, depth = total.shape
    species = out.shape[0]
    width = row_count // planes
    per_device, bins = means.shape[1:]
    for s in range(0, per_device, 2):
        block = sum((term[s // 2] for term in terms[1:]), terms[0][s // 2])
        block = block / jnp.maximum(block[species + 1 : species + 2], 1.0)
        means[:, s, :] = block[:species, :bins]
        means[:, s + 1, :] = block[:species, bins:]
    copies = [pltpu.make_async_copy(means, means_out, sem.at[0])]
    copies[0].start()

    weight = jnp.broadcast_to(weight_column(weights, rows), (rows, depth))
    received = {}
    for axis, both in zip(("gx", "gy"), has_b):
        received[axis] = [halos.pop(0), halos.pop(0) if both else None]

    def share(axis, upper, c, i):
        first, second = received[axis]
        is_first = jnp.broadcast_to(upper_of(axis, 0) if upper else upper_of(axis, 1), c.shape)
        inside = jnp.broadcast_to(has_neighbour(axis, 1), c.shape)
        other = jnp.zeros_like(c) if second is None else jnp.where(inside, second[i], 0.0)
        there = jnp.where(is_first, first[i], other)
        d = 0.5 * (c[species : species + 1] + there[species : species + 1])
        return weight * d * (there - c)

    n = 0
    for x in (0, planes - 1):
        for y in range(width):
            r = x * width + y
            c = cells[r]
            new = total[r] + share("gx", x > 0, c, y)
            if y in (0, width - 1):
                new += share("gy", y > 0, c, x)
            changed[n + y] = new
        for k in range(species):
            copies.append(
                pltpu.make_async_copy(
                    changed.at[pl.ds(n, width), k, :],
                    out.at[k, pl.ds(x * width, width)],
                    sem.at[1],
                )
            )
            copies[-1].start()
        n += width
    planes_changed = changed.at[pl.ds(0, n), pl.ds(0, species), :]
    cells_out = out.reshape(species, planes, width, depth)
    start = n
    for y in (0, width - 1):
        for x in range(1, planes - 1):
            r = x * width + y
            changed[n + x - 1] = total[r] + share("gy", y > 0, cells[r], x)
        for k in range(species):
            copies.append(
                pltpu.make_async_copy(
                    changed.at[pl.ds(n, planes - 2), k, :],
                    cells_out.at[k, pl.ds(1, planes - 2), y, :],
                    sem.at[2],
                )
            )
            copies[-1].start()
        n += planes - 2
    rows_changed = changed.at[pl.ds(start, n - start), pl.ds(0, species), :]
    copies[0].wait()
    pltpu.make_async_copy(planes_changed, planes_changed, sem.at[1]).wait()
    pltpu.make_async_copy(rows_changed, rows_changed, sem.at[2]).wait()


def struct(*shape):
    return jax.ShapeDtypeStruct(shape, F32)


def call(
    kernel, name, out_shape, n_in, out_specs, in_specs=None, scratch=(), flops=0, moved=0, aliases=None
):
    return pl.pallas_call(
        kernel,
        out_shape=out_shape,
        in_specs=in_specs or [VMEM] * n_in,
        out_specs=out_specs,
        scratch_shapes=list(scratch),
        input_output_aliases=aliases or {},
        name=name,
        compiler_params=pltpu.CompilerParams(vmem_limit_bytes=32 * 1024 * 1024),
        cost_estimate=pl.CostEstimate(flops=flops, bytes_accessed=moved, transcendentals=0),
    )


def joint(block, axis, source):
    deep, count = lax.axis_size("sec"), lax.axis_size(axis)
    pairs = []
    for s in range(deep):
        for i in range(count):
            t, j = source(s, i)
            pairs.append((t * count + j, s * count + i))
    return lax.ppermute(block, ("sec", axis), pairs)


def swapped(block, axis, side):
    count = lax.axis_size(axis)
    if side == 0:
        return lax.ppermute(block, axis, [(i, i ^ 1) for i in range(count)])
    if axis == "sec":
        pairs = [(i, ((i + 1) ^ 1) - 1) for i in range(1, count - 1)]
        return lax.ppermute(block, axis, [*pairs, (0, count - 1), (count - 1, 0)])
    return joint(
        block,
        axis,
        lambda s, i: (s, ((i + 1) ^ 1) - 1) if 0 < i < count - 1 else (s ^ 1, i),
    )


def summed(block):
    deep, gx, gy = (lax.axis_size(axis) for axis in ("sec", "gx", "gy"))
    half = block.shape[0] // 2
    block = block[:half] + joint(block[half:], "gx", lambda s, i: (s ^ 1, (i - 1) % gx))
    steps = [(1 << n, 0) for n in range(1, deep.bit_length() - 1)]
    steps += [(0, 1 << n) for n in range(gy.bit_length() - 1)]
    terms = [block]
    while steps:
        (a, b), (c, d) = steps.pop(0), steps.pop(0) if steps else (0, 0)
        block = sum(terms[1:], terms[0])
        terms = [block]
        for e, f in dict.fromkeys([(a, b), (c, d), (a ^ c, b ^ d)]):
            if e or f:
                terms.append(joint(block, "gy", lambda s, i: (s ^ 1 ^ e, i ^ f)))
    return terms


def on_device(
    composition_matrix,
    local_mixing_coefficient,
    thermal_field,
    component_mixing_weight,
    kinetics_jacobian,
    mixture_classes,
    streamwise_positions,
):
    species, planes, width, depth = composition_matrix.shape
    row_count = planes * width
    rows = padded_rows(species)
    cells = composition_matrix.reshape(species, row_count, depth)
    mixing = local_mixing_coefficient.reshape(row_count, depth)
    thermal = thermal_field.reshape(row_count, depth)
    classes = mixture_classes.reshape(row_count, depth)
    weights = component_mixing_weight.reshape(1, species)
    positions = streamwise_positions.reshape(1, -1)
    per_device = planes // 2
    has_b = tuple(lax.axis_size(axis) > 2 for axis in ("gx", "gy", "sec"))
    sides = [
        (axis, side)
        for axis, both in zip(("gx", "gy", "sec"), has_b)
        for side in range(1 + both)
    ]
    shapes = {
        ("gx", 0): struct(2 * width, depth),
        ("gx", 1): struct(2 * width, depth),
        ("gy", 0): struct(planes, rows, depth),
        ("gy", 1): struct(planes, rows, depth),
        ("sec", 0): struct(rows, row_count),
        ("sec", 1): struct(max(rows, 2 * width + SUBLANES), row_count),
    }

    rows_in, own_z, *faces = call(
        functools.partial(pack_kernel, planes, has_b),
        "faces",
        [
            struct(row_count, rows, depth),
            struct(2, rows, row_count),
            *[shapes[side] for side in sides],
        ],
        3,
        [VMEM] * (2 + len(sides)),
        in_specs=[ANY] * 3,
        scratch=[
            pltpu.VMEM((row_count, depth), jnp.int32),
            pltpu.SemaphoreType.DMA((planes // 2,)),
            pltpu.SemaphoreType.DMA((2,)),
        ],
    )(*[pltpu.with_memory_space_constraint(x, pltpu.HBM) for x in (cells, mixing, classes)])
    halos = [swapped(face, axis, side) for face, (axis, side) in zip(faces, sides)]

    inner, sums = call(
        functools.partial(inner_kernel, planes),
        "inside",
        [struct(row_count, rows, depth), struct(per_device + 1, rows, NB)],
        5,
        [VMEM] * 2,
        scratch=[
            pltpu.VMEM((8, row_count, depth), F32),
            pltpu.VMEM((2 * rows, 2 * rows), F32),
        ],
        flops=10_000_000,
        moved=4_000_000,
    )(rows_in, mixing, thermal, weights, kinetics_jacobian)

    window, dz = call(
        functools.partial(edge_kernel, planes, has_b),
        "edges",
        [struct(per_device, rows, 2 * NB), struct(2, rows, row_count)],
        5 + len(halos),
        [VMEM] * 2,
        scratch=[pltpu.VMEM((per_device + 1, rows, NB), F32)],
    )(rows_in, own_z, sums, weights, positions, *halos)

    deep = lax.axis_size("sec")
    window = window + lax.ppermute(window, "sec", [(i, i ^ 1) for i in range(deep)])
    terms = summed(window)

    outer_planes = call(
        functools.partial(plane_kernel, planes),
        "planes",
        [struct(width, rows, depth)] * (1 + has_b[0]),
        2,
        [VMEM] * (1 + has_b[0]),
    )(rows_in, window)
    wide_halos = [swapped(face, "gx", side) for side, face in enumerate(outer_planes)]
    wide_halos += [halo for halo, (axis, _) in zip(halos, sides) if axis == "gy"]

    total, advanced = call(
        functools.partial(interior_kernel, planes),
        "interior",
        [struct(row_count, rows, depth), struct(species, row_count, depth)],
        2,
        [VMEM, ANY],
        scratch=[pltpu.SemaphoreType.DMA((planes,))],
        flops=1_000_000,
        moved=3_000_000,
    )(inner, dz)
    ins = [rows_in, total, weights, advanced, *wide_halos, *terms]
    specs = [VMEM] * len(ins)
    specs[3] = ANY
    advanced, cond_means = call(
        functools.partial(last_kernel, planes, has_b[:2], len(terms)),
        "last",
        [struct(species, row_count, depth), struct(species, per_device, NB)],
        len(ins),
        [ANY, ANY],
        in_specs=specs,
        scratch=[
            pltpu.VMEM((2 * (width + planes - 2), rows, depth), F32),
            pltpu.VMEM((species, per_device, NB), F32),
            pltpu.SemaphoreType.DMA((3,)),
        ],
        aliases={3: 0},
    )(*ins)
    return advanced.reshape(composition_matrix.shape), cond_means


def solution(mesh):
    in_specs = (
        P(None, "gx", "gy", "sec"),
        P("gx", "gy", "sec"),
        P("gx", "gy", "sec"),
        P(),
        P(),
        P("gx", "gy", "sec"),
        P(),
    )
    out_specs = (P(None, "gx", "gy", "sec"), P(None, "gx", None))
    return jax.shard_map(
        on_device, mesh=mesh, in_specs=in_specs, out_specs=out_specs, check_vma=False
    )
```

```python
import functools

import jax
import jax.numpy as jnp
from jax import lax
from jax.experimental import pallas as pl
from jax.experimental.pallas import tpu as pltpu
from jax.sharding import PartitionSpec as P

NB = 64
SUBLANES = 8
LANES = 128
F32 = jnp.float32
BF16 = jnp.bfloat16
VMEM = pl.BlockSpec(memory_space=pltpu.VMEM)
ANY = pl.BlockSpec(memory_space=pl.ANY)
DT = 0.05
AHEAD = 2


def padded_rows(species):
    return -(-(species + 2) // SUBLANES) * SUBLANES


def lanes_of(shape):
    return lax.broadcasted_iota(jnp.int32, shape, len(shape) - 1)


def rows_of(shape):
    return lax.broadcasted_iota(jnp.int32, shape, len(shape) - 2)


def halves(block):
    high = block.astype(BF16).astype(F32)
    return jnp.concatenate([high, block - high], axis=0).astype(BF16)


def weight_column(weights_ref, rows):
    species = weights_ref.shape[1]
    shape = (rows, species)
    spread = jnp.where(rows_of(shape) == lanes_of(shape), weights_ref[...], 0.0)
    return DT * jnp.sum(spread, axis=1, keepdims=True)


def hits(classes):
    shape = (NB, classes.shape[1])
    bins = jnp.broadcast_to(classes.astype(BF16), shape)
    found = bins == rows_of(shape).astype(F32).astype(BF16)
    return jnp.where(found, jnp.ones((), BF16), jnp.zeros((), BF16))


def binned(values, hit):
    return lax.dot_general(
        values, hit, (((1,), (1,)), ((), ())), preferred_element_type=F32
    )


def folded(product):
    rows = product.shape[0] // 2
    return product[:rows] + product[rows:]


def upper_of(axis, side):
    even = lax.axis_index(axis) % 2 == 0
    return even if side == 0 else jnp.logical_not(even)


def has_neighbour(axis, side):
    if side == 0:
        return True
    edge = jnp.where(upper_of(axis, 1), lax.axis_size(axis) - 1, 0)
    return lax.axis_index(axis) != edge


def face_rows(axis, upper, planes, width):
    if axis == "gx":
        return jnp.where(upper, (planes - 1) * width, 0), 1, width
    return jnp.where(upper, width - 1, 0), width, planes


def pack_kernel(planes, has_b, cells, mixing, classes, *refs):
    outs, (bins, sem, field_sem) = refs[:-3], refs[-3:]
    rows_out, own_z = outs[0], outs[1]
    faces = list(outs[2:])
    species, row_count, depth = cells.shape
    rows = rows_out.shape[1]
    width = row_count // planes
    chunk = row_count // sem.shape[0]
    field_copies = [
        pltpu.make_async_copy(mixing, rows_out.at[:, species, :], field_sem.at[0]),
        pltpu.make_async_copy(classes, bins, field_sem.at[1]),
    ]
    for copy in field_copies:
        copy.start()
    for n in range(sem.shape[0]):
        span = pl.ds(n * chunk, chunk)
        for k in range(species):
            pltpu.make_async_copy(
                cells.at[k, span], rows_out.at[span, k, :], sem.at[n]
            ).start()

    lane = lanes_of((SUBLANES, depth))
    zero = jnp.zeros((SUBLANES, depth), F32)

    def gathered(groups, span, low, high):
        low, high = list(low), list(high)
        for r in span:
            at, before = lane == r, lane == (r - 1) % depth
            for i, g in enumerate(groups):
                block = rows_out[r, pl.ds(g, SUBLANES), :]
                turned = pltpu.roll(block, r, axis=1) if r else block
                low[i] = jnp.where(at, turned, low[i])
                high[i] = jnp.where(before, turned, high[i])
        return low, high

    whole = species // SUBLANES * SUBLANES
    first = range(0, whole, SUBLANES)
    rest = range(whole, rows, SUBLANES)
    low, high = [zero] * len(first), [zero] * len(first)
    for n in range(sem.shape[0]):
        arrived = rows_out.at[pl.ds(n * chunk, chunk), pl.ds(0, species), :]
        pltpu.make_async_copy(arrived, arrived, sem.at[n]).wait()
        low, high = gathered(first, range(n * chunk, (n + 1) * chunk), low, high)
    for copy in field_copies:
        copy.wait()
    for r in range(0, row_count, SUBLANES):
        span = pl.ds(r, SUBLANES)
        rows_out[span, species + 1, :] = bins[span, :].astype(F32)
    lows, highs = gathered(rest, range(row_count), [zero] * len(rest), [zero] * len(rest))
    for i, g in enumerate([*first, *rest]):
        own_z[0, pl.ds(g, SUBLANES), :] = (low + lows)[i]
        own_z[1, pl.ds(g, SUBLANES), :] = pltpu.roll((high + highs)[i], 1, axis=1)
    for axis, both in zip(("gx", "gy", "sec"), has_b):
        for side in range(1 + both):
            out = faces.pop(0)
            upper = upper_of(axis, side)
            if axis == "sec":
                out[pl.ds(0, rows), :] = own_z[jnp.where(upper, 1, 0)]
                continue
            start, step, count = face_rows(axis, upper, planes, width)
            for i in range(count):
                r = start + i * step
                if axis == "gy":
                    out[i] = rows_out[r]
                else:
                    out[pl.ds(i, 1), :] = rows_out[r, pl.ds(species, 1), :]
                    out[pl.ds(count + i, 1), :] = rows_out[r, pl.ds(species + 1, 1), :]


def plane_kernel(planes, cells, held, *faces):
    width = cells.shape[0] // planes
    for side, out in enumerate(faces):
        start, step, count = face_rows("gx", upper_of("gx", side), planes, width)
        for i in range(count):
            out[i] = cells[start + i * step]


def inner_kernel(
    planes, cells, mixing, thermal, weights, jacobian, advanced, station_sums, coefs, square
):
    row_count, rows, depth = cells.shape
    species = jacobian.shape[0]
    width = row_count // planes
    shape = (row_count, depth)
    lane, row = lanes_of(shape), rows_of(shape)
    mix = mixing[...]
    up = 0.5 * (mix + pltpu.roll(mix, depth - 1, axis=1))
    up = jnp.where(lane == depth - 1, 0.0, up)
    coefs[0] = up
    down = pltpu.roll(up, 1, axis=1)
    coefs[1] = down
    total = up + down
    up = 0.5 * (mix + pltpu.roll(mix, row_count - 1, axis=0))
    up = jnp.where(row % width == width - 1, 0.0, up)
    coefs[2] = up
    down = pltpu.roll(up, 1, axis=0)
    coefs[3] = down
    total = total + (up + down)
    edge = jnp.zeros((width, depth), F32)
    up = jnp.concatenate([0.5 * (mix[: row_count - width] + mix[width:]), edge], axis=0)
    coefs[4] = up
    down = jnp.concatenate([edge, up[: row_count - width]], axis=0)
    coefs[5] = down
    coefs[6] = total + (up + down)
    coefs[7] = (4.0 * DT) * jnp.exp(-2.0 / thermal[...])

    square[...] = jnp.zeros_like(square)
    matrix = jacobian[...]
    matrix_high = matrix.astype(BF16).astype(F32)
    square[:species, :species] = matrix_high
    square[:species, rows : rows + species] = matrix_high
    square[rows : rows + species, :species] = matrix - matrix_high
    left = square[...].astype(BF16)

    weight = jnp.broadcast_to(weight_column(weights, rows), (rows, depth))
    whole = species // SUBLANES * SUBLANES
    ones = rows_of((rows - whole, depth)) >= species - whole
    station_sums[...] = jnp.zeros_like(station_sums)

    def kinetics(pair):
        wide = jnp.concatenate([halves(cells[r]) for r in pair], axis=1)
        return folded(jnp.dot(left, wide, preferred_element_type=F32))

    def advance(pair, mixed):
        values, found = [], []
        for i, r in enumerate(pair):
            x, y = divmod(r, width)
            c = cells[r]
            at = lambda n: coefs[n, pl.ds(r, 1), :]
            flux = at(0) * pltpu.roll(c, depth - 1, axis=1)
            flux += at(1) * pltpu.roll(c, 1, axis=1)
            if y < width - 1:
                flux += at(2) * cells[r + 1]
            if y > 0:
                flux += at(3) * cells[r - 1]
            if x < planes - 1:
                flux += at(4) * cells[r + width]
            if x > 0:
                flux += at(5) * cells[r - width]
            flux -= at(6) * c
            new = c + weight * flux + at(7) * mixed[:, i * depth : (i + 1) * depth]
            new = jnp.concatenate([new[:whole], jnp.where(ones, 1.0, new[whole:])], axis=0)
            advanced[r] = new
            values.append(halves(new))
            found.append(hits(cells[r, species + 1 : species + 2, :]))
        return jnp.concatenate(values, axis=1), jnp.concatenate(found, axis=1)

    pairs = [(r, r + 1) for r in range(0, row_count, 2)]
    mixed, values, made = {}, {}, 0.0
    for t in range(len(pairs) + 2 * AHEAD):
        if t < len(pairs):
            mixed[t] = kinetics(pairs[t])
        now = t - AHEAD
        if 0 <= now < len(pairs):
            values[now] = advance(pairs[now], mixed.pop(now))
        last = now - AHEAD
        if 0 <= last < len(pairs):
            made += binned(*values.pop(last))
            x, y = divmod(pairs[last][1], width)
            if y == width - 1:
                station_sums[(x + 1) // 2] += folded(made)
                made = 0.0


def edge_kernel(planes, has_b, cells, own_z, sums, weights, positions, *refs):
    halos = list(refs[: 3 + sum(has_b)])
    window, dz = refs[3 + sum(has_b) :]
    row_count, rows, depth = cells.shape
    species = weights.shape[1]
    width = row_count // planes
    stations = planes // 2 + 1
    weight = jnp.broadcast_to(weight_column(weights, rows), (rows, depth))
    received = {}
    for axis, both in zip(("gx", "gy", "sec"), has_b):
        received[axis] = [halos.pop(0), halos.pop(0) if both else None]

    def beyond(axis, upper, part, outside):
        first, second = (halo if halo is None else halo[part] for halo in received[axis])
        second = jnp.full_like(first, outside) if second is None else second
        is_first = upper_of(axis, 0) if upper else upper_of(axis, 1)
        edge = lax.axis_size(axis) - 1 if upper else 0
        block = jnp.where(jnp.broadcast_to(is_first, first.shape), first, second)
        inside = jnp.broadcast_to(lax.axis_index(axis) != edge, first.shape)
        return jnp.where(inside, block, outside)

    values = [[] for _ in range(stations)]
    found = [[] for _ in range(stations)]

    def moves(x, y, d, bins):
        c = cells[x * width + y]
        d = 0.5 * (c[species : species + 1] + d)
        values[(x + 1) // 2].append(halves(weight * d * c))
        found[(x + 1) // 2].append(hits(bins) - hits(c[species + 1 : species + 2]))

    for upper in (False, True):
        d_beyond = beyond("gx", upper, pl.ds(0, width), 0.0)
        bins_beyond = beyond("gx", upper, pl.ds(width, width), -1.0)
        for y in range(width):
            moves((planes - 1) * upper, y, d_beyond[y : y + 1], bins_beyond[y : y + 1])
    for upper in (False, True):
        for x in range(planes):
            d = beyond("gy", upper, (x, pl.ds(species, 1)), 0.0)
            bins = beyond("gy", upper, (x, pl.ds(species + 1, 1)), -1.0)
            moves(x, (width - 1) * upper, d, bins)
    station = ((lanes_of((1, row_count)) // width + 1) // 2).astype(F32)
    for upper in (False, True):
        c = own_z[int(upper)]
        halo = beyond("sec", upper, pl.ds(0, rows), 0.0)
        d = 0.5 * (c[species : species + 1] + halo[species : species + 1])
        delta = weight * d * (halo - c)
        dz[int(upper)] = delta
        value = halves(delta)
        for j in range(stations):
            values[j].append(value)
            found[j].append(hits(jnp.where(station == j, c[species + 1 : species + 2], -1.0)))

    station_sums = [
        sums[j]
        + folded(binned(jnp.concatenate(values[j], axis=1), jnp.concatenate(found[j], axis=1)))
        for j in range(stations)
    ]
    shift = jnp.broadcast_to(positions[0:1, 0:1], (rows, NB))
    per_device = planes // 2
    for s in range(0, 2 * per_device, 2):
        parts = []
        for slot in (s, s + 1):
            part = jnp.zeros((rows, NB), F32)
            for j in range(stations):
                if 0 <= slot - j < per_device:
                    part += jnp.where(shift == slot - j, station_sums[j], 0.0)
            parts.append(part)
        window[s // 2] = jnp.concatenate(parts, axis=1)


def interior_kernel(planes, advanced, dz, total, out, sem):
    row_count, rows, depth = advanced.shape
    species = out.shape[0]
    width = row_count // planes
    shape = (rows, depth)
    lane = lanes_of(shape)
    low = dz[0]
    high = pltpu.roll(dz[1], depth - 1, axis=1)
    for plane in range(planes):
        for r in range(plane * width, (plane + 1) * width):
            turned = depth - r if r else 0
            a = pltpu.roll(low, turned, axis=1) if r else low
            b = pltpu.roll(high, turned, axis=1) if r else high
            total[r] = advanced[r] + jnp.where(
                lane == 0, a, jnp.where(lane == depth - 1, b, 0.0)
            )
        span = pl.ds(plane * width, width)
        for k in range(species):
            pltpu.make_async_copy(
                total.at[span, k, :], out.at[k, span], sem.at[plane]
            ).start()
    for plane in range(planes):
        span = pl.ds(plane * width, width)
        pltpu.make_async_copy(
            total.at[pl.ds(0, species), pl.ds(0, width), :], out.at[:, span], sem.at[plane]
        ).wait()


def last_kernel(planes, has_b, n_terms, cells, total, weights, first_out, *refs):
    halos, terms = list(refs[: 2 + sum(has_b)]), refs[2 + sum(has_b) :][:n_terms]
    out, means_out, changed, means, sem = refs[2 + sum(has_b) + n_terms :]
    row_count, rows, depth = total.shape
    species = out.shape[0]
    width = row_count // planes
    per_device, bins = means.shape[1:]
    for s in range(0, per_device, 2):
        block = sum((term[s // 2] for term in terms[1:]), terms[0][s // 2])
        block = block / jnp.maximum(block[species + 1 : species + 2], 1.0)
        means[:, s, :] = block[:species, :bins]
        means[:, s + 1, :] = block[:species, bins:]
    copies = [pltpu.make_async_copy(means, means_out, sem.at[0])]
    copies[0].start()

    weight = jnp.broadcast_to(weight_column(weights, rows), (rows, depth))
    received = {}
    for axis, both in zip(("gx", "gy"), has_b):
        received[axis] = [halos.pop(0), halos.pop(0) if both else None]

    def share(axis, upper, c, i):
        first, second = received[axis]
        is_first = jnp.broadcast_to(upper_of(axis, 0) if upper else upper_of(axis, 1), c.shape)
        inside = jnp.broadcast_to(has_neighbour(axis, 1), c.shape)
        other = jnp.zeros_like(c) if second is None else jnp.where(inside, second[i], 0.0)
        there = jnp.where(is_first, first[i], other)
        d = 0.5 * (c[species : species + 1] + there[species : species + 1])
        return weight * d * (there - c)

    n = 0
    for x in (0, planes - 1):
        for y in range(width):
            r = x * width + y
            c = cells[r]
            new = total[r] + share("gx", x > 0, c, y)
            if y in (0, width - 1):
                new += share("gy", y > 0, c, x)
            changed[n + y] = new
        for k in range(species):
            copies.append(
                pltpu.make_async_copy(
                    changed.at[pl.ds(n, width), k, :],
                    out.at[k, pl.ds(x * width, width)],
                    sem.at[1],
                )
            )
            copies[-1].start()
        n += width
    planes_changed = changed.at[pl.ds(0, n), pl.ds(0, species), :]
    cells_out = out.reshape(species, planes, width, depth)
    start = n
    for y in (0, width - 1):
        for x in range(1, planes - 1):
            r = x * width + y
            changed[n + x - 1] = total[r] + share("gy", y > 0, cells[r], x)
        for k in range(species):
            copies.append(
                pltpu.make_async_copy(
                    changed.at[pl.ds(n, planes - 2), k, :],
                    cells_out.at[k, pl.ds(1, planes - 2), y, :],
                    sem.at[2],
                )
            )
            copies[-1].start()
        n += planes - 2
    rows_changed = changed.at[pl.ds(start, n - start), pl.ds(0, species), :]
    copies[0].wait()
    pltpu.make_async_copy(planes_changed, planes_changed, sem.at[1]).wait()
    pltpu.make_async_copy(rows_changed, rows_changed, sem.at[2]).wait()


def struct(*shape):
    return jax.ShapeDtypeStruct(shape, F32)


def call(
    kernel, name, out_shape, n_in, out_specs, in_specs=None, scratch=(), flops=0, moved=0, aliases=None
):
    return pl.pallas_call(
        kernel,
        out_shape=out_shape,
        in_specs=in_specs or [VMEM] * n_in,
        out_specs=out_specs,
        scratch_shapes=list(scratch),
        input_output_aliases=aliases or {},
        name=name,
        compiler_params=pltpu.CompilerParams(vmem_limit_bytes=32 * 1024 * 1024),
        cost_estimate=pl.CostEstimate(flops=flops, bytes_accessed=moved, transcendentals=0),
    )


def joint(block, axis, source):
    deep, count = lax.axis_size("sec"), lax.axis_size(axis)
    pairs = []
    for s in range(deep):
        for i in range(count):
            t, j = source(s, i)
            pairs.append((t * count + j, s * count + i))
    return lax.ppermute(block, ("sec", axis), pairs)


def swapped(block, axis, side):
    count = lax.axis_size(axis)
    if side == 0:
        return lax.ppermute(block, axis, [(i, i ^ 1) for i in range(count)])
    if axis == "sec":
        pairs = [(i, ((i + 1) ^ 1) - 1) for i in range(1, count - 1)]
        return lax.ppermute(block, axis, [*pairs, (0, count - 1), (count - 1, 0)])
    return joint(
        block,
        axis,
        lambda s, i: (s, ((i + 1) ^ 1) - 1) if 0 < i < count - 1 else (s ^ 1, i),
    )


def summed(block):
    deep, gx, gy = (lax.axis_size(axis) for axis in ("sec", "gx", "gy"))
    half = block.shape[0] // 2
    block = block[:half] + joint(block[half:], "gx", lambda s, i: (s ^ 1, (i - 1) % gx))
    steps = [(1 << n, 0) for n in range(1, deep.bit_length() - 1)]
    steps += [(0, 1 << n) for n in range(gy.bit_length() - 1)]
    terms = [block]
    while steps:
        (a, b), (c, d) = steps.pop(0), steps.pop(0) if steps else (0, 0)
        block = sum(terms[1:], terms[0])
        terms = [block]
        for e, f in dict.fromkeys([(a, b), (a ^ c, b ^ d), (c, d)]):
            if e or f:
                terms.append(joint(block, "gy", lambda s, i: (s ^ 1 ^ e, i ^ f)))
    return terms


def on_device(
    composition_matrix,
    local_mixing_coefficient,
    thermal_field,
    component_mixing_weight,
    kinetics_jacobian,
    mixture_classes,
    streamwise_positions,
):
    species, planes, width, depth = composition_matrix.shape
    row_count = planes * width
    rows = padded_rows(species)
    cells = composition_matrix.reshape(species, row_count, depth)
    mixing = local_mixing_coefficient.reshape(row_count, depth)
    thermal = thermal_field.reshape(row_count, depth)
    classes = mixture_classes.reshape(row_count, depth)
    weights = component_mixing_weight.reshape(1, species)
    positions = streamwise_positions.reshape(1, -1)
    per_device = planes // 2
    has_b = tuple(lax.axis_size(axis) > 2 for axis in ("gx", "gy", "sec"))
    sides = [
        (axis, side)
        for axis, both in zip(("gx", "gy", "sec"), has_b)
        for side in range(1 + both)
    ]
    shapes = {
        ("gx", 0): struct(2 * width, depth),
        ("gx", 1): struct(2 * width, depth),
        ("gy", 0): struct(planes, rows, depth),
        ("gy", 1): struct(planes, rows, depth),
        ("sec", 0): struct(rows, row_count),
        ("sec", 1): struct(max(rows, 2 * width + SUBLANES), row_count),
    }

    rows_in, own_z, *faces = call(
        functools.partial(pack_kernel, planes, has_b),
        "faces",
        [
            struct(row_count, rows, depth),
            struct(2, rows, row_count),
            *[shapes[side] for side in sides],
        ],
        3,
        [VMEM] * (2 + len(sides)),
        in_specs=[ANY] * 3,
        scratch=[
            pltpu.VMEM((row_count, depth), jnp.int32),
            pltpu.SemaphoreType.DMA((planes // 2,)),
            pltpu.SemaphoreType.DMA((2,)),
        ],
    )(*[pltpu.with_memory_space_constraint(x, pltpu.HBM) for x in (cells, mixing, classes)])
    halos = [swapped(face, axis, side) for face, (axis, side) in zip(faces, sides)]

    inner, sums = call(
        functools.partial(inner_kernel, planes),
        "inside",
        [struct(row_count, rows, depth), struct(per_device + 1, rows, NB)],
        5,
        [VMEM] * 2,
        scratch=[
            pltpu.VMEM((8, row_count, depth), F32),
            pltpu.VMEM((2 * rows, 2 * rows), F32),
        ],
        flops=10_000_000,
        moved=4_000_000,
    )(rows_in, mixing, thermal, weights, kinetics_jacobian)

    window, dz = call(
        functools.partial(edge_kernel, planes, has_b),
        "edges",
        [struct(per_device, rows, 2 * NB), struct(2, rows, row_count)],
        5 + len(halos),
        [VMEM] * 2,
    )(rows_in, own_z, sums, weights, positions, *halos)

    deep = lax.axis_size("sec")
    window = window + lax.ppermute(window, "sec", [(i, i ^ 1) for i in range(deep)])
    terms = summed(window)

    outer_planes = call(
        functools.partial(plane_kernel, planes),
        "planes",
        [struct(width, rows, depth)] * (1 + has_b[0]),
        2,
        [VMEM] * (1 + has_b[0]),
    )(rows_in, window)
    wide_halos = [swapped(face, "gx", side) for side, face in enumerate(outer_planes)]
    wide_halos += [halo for halo, (axis, _) in zip(halos, sides) if axis == "gy"]

    total, advanced = call(
        functools.partial(interior_kernel, planes),
        "interior",
        [struct(row_count, rows, depth), struct(species, row_count, depth)],
        2,
        [VMEM, ANY],
        scratch=[pltpu.SemaphoreType.DMA((planes,))],
        flops=1_000_000,
        moved=3_000_000,
    )(inner, dz)
    ins = [rows_in, total, weights, advanced, *wide_halos, *terms]
    specs = [VMEM] * len(ins)
    specs[3] = ANY
    advanced, cond_means = call(
        functools.partial(last_kernel, planes, has_b[:2], len(terms)),
        "last",
        [struct(species, row_count, depth), struct(species, per_device, NB)],
        len(ins),
        [ANY, ANY],
        in_specs=specs,
        scratch=[
            pltpu.VMEM((2 * (width + planes - 2), rows, depth), F32),
            pltpu.VMEM((species, per_device, NB), F32),
            pltpu.SemaphoreType.DMA((3,)),
        ],
        aliases={3: 0},
    )(*ins)
    return advanced.reshape(composition_matrix.shape), cond_means


def solution(mesh):
    in_specs = (
        P(None, "gx", "gy", "sec"),
        P("gx", "gy", "sec"),
        P("gx", "gy", "sec"),
        P(),
        P(),
        P("gx", "gy", "sec"),
        P(),
    )
    out_specs = (P(None, "gx", "gy", "sec"), P(None, "gx", None))
    return jax.shard_map(
        on_device, mesh=mesh, in_specs=in_specs, out_specs=out_specs, check_vma=False
    )
```

```python
import functools

import jax
import jax.numpy as jnp
from jax import lax
from jax.experimental import pallas as pl
from jax.experimental.pallas import tpu as pltpu
from jax.sharding import PartitionSpec as P

NB = 64
SUBLANES = 8
LANES = 128
F32 = jnp.float32
BF16 = jnp.bfloat16
VMEM = pl.BlockSpec(memory_space=pltpu.VMEM)
ANY = pl.BlockSpec(memory_space=pl.ANY)
DT = 0.05
AHEAD = 2


def padded_rows(species):
    return -(-(species + 2) // SUBLANES) * SUBLANES


def lanes_of(shape):
    return lax.broadcasted_iota(jnp.int32, shape, len(shape) - 1)


def rows_of(shape):
    return lax.broadcasted_iota(jnp.int32, shape, len(shape) - 2)


def halves(block):
    high = block.astype(BF16).astype(F32)
    return jnp.concatenate([high, block - high], axis=0).astype(BF16)


def weight_column(weights_ref, rows):
    species = weights_ref.shape[1]
    shape = (rows, species)
    spread = jnp.where(rows_of(shape) == lanes_of(shape), weights_ref[...], 0.0)
    return DT * jnp.sum(spread, axis=1, keepdims=True)


def hits(classes):
    shape = (NB, classes.shape[1])
    bins = jnp.broadcast_to(classes.astype(BF16), shape)
    found = bins == rows_of(shape).astype(F32).astype(BF16)
    return jnp.where(found, jnp.ones((), BF16), jnp.zeros((), BF16))


def binned(values, hit):
    return lax.dot_general(
        values, hit, (((1,), (1,)), ((), ())), preferred_element_type=F32
    )


def folded(product):
    rows = product.shape[0] // 2
    return product[:rows] + product[rows:]


def upper_of(axis, side):
    even = lax.axis_index(axis) % 2 == 0
    return even if side == 0 else jnp.logical_not(even)


def has_neighbour(axis, side):
    if side == 0:
        return True
    edge = jnp.where(upper_of(axis, 1), lax.axis_size(axis) - 1, 0)
    return lax.axis_index(axis) != edge


def face_rows(axis, upper, planes, width):
    if axis == "gx":
        return jnp.where(upper, (planes - 1) * width, 0), 1, width
    return jnp.where(upper, width - 1, 0), width, planes


def pack_kernel(planes, has_b, cells, mixing, classes, *refs):
    outs, (bins, sem, field_sem) = refs[:-3], refs[-3:]
    rows_out, own_z = outs[0], outs[1]
    faces = list(outs[2:])
    species, row_count, depth = cells.shape
    rows = rows_out.shape[1]
    width = row_count // planes
    chunk = row_count // sem.shape[0]
    field_copies = [
        pltpu.make_async_copy(mixing, rows_out.at[:, species, :], field_sem.at[0]),
        pltpu.make_async_copy(classes, bins, field_sem.at[1]),
    ]
    for copy in field_copies:
        copy.start()
    for n in range(sem.shape[0]):
        span = pl.ds(n * chunk, chunk)
        for k in range(species):
            pltpu.make_async_copy(
                cells.at[k, span], rows_out.at[span, k, :], sem.at[n]
            ).start()

    lane = lanes_of((SUBLANES, depth))
    zero = jnp.zeros((SUBLANES, depth), F32)

    def gathered(groups, span, low, high):
        low, high = list(low), list(high)
        for r in span:
            at, before = lane == r, lane == (r - 1) % depth
            for i, g in enumerate(groups):
                block = rows_out[r, pl.ds(g, SUBLANES), :]
                turned = pltpu.roll(block, r, axis=1) if r else block
                low[i] = jnp.where(at, turned, low[i])
                high[i] = jnp.where(before, turned, high[i])
        return low, high

    whole = species // SUBLANES * SUBLANES
    first = range(0, whole, SUBLANES)
    rest = range(whole, rows, SUBLANES)
    low, high = [zero] * len(first), [zero] * len(first)
    for n in range(sem.shape[0]):
        arrived = rows_out.at[pl.ds(n * chunk, chunk), pl.ds(0, species), :]
        pltpu.make_async_copy(arrived, arrived, sem.at[n]).wait()
        low, high = gathered(first, range(n * chunk, (n + 1) * chunk), low, high)
    for copy in field_copies:
        copy.wait()
    for r in range(0, row_count, SUBLANES):
        span = pl.ds(r, SUBLANES)
        rows_out[span, species + 1, :] = bins[span, :].astype(F32)
    lows, highs = gathered(rest, range(row_count), [zero] * len(rest), [zero] * len(rest))
    for i, g in enumerate([*first, *rest]):
        own_z[0, pl.ds(g, SUBLANES), :] = (low + lows)[i]
        own_z[1, pl.ds(g, SUBLANES), :] = pltpu.roll((high + highs)[i], 1, axis=1)
    for axis, both in zip(("gx", "gy", "sec"), has_b):
        for side in range(1 + both):
            out = faces.pop(0)
            upper = upper_of(axis, side)
            if axis == "sec":
                out[pl.ds(0, rows), :] = own_z[jnp.where(upper, 1, 0)]
                continue
            start, step, count = face_rows(axis, upper, planes, width)
            for i in range(count):
                r = start + i * step
                if axis == "gy":
                    out[i] = rows_out[r]
                else:
                    out[pl.ds(i, 1), :] = rows_out[r, pl.ds(species, 1), :]
                    out[pl.ds(count + i, 1), :] = rows_out[r, pl.ds(species + 1, 1), :]


def plane_kernel(planes, cells, held, *faces):
    width = cells.shape[0] // planes
    for side, out in enumerate(faces):
        start, step, count = face_rows("gx", upper_of("gx", side), planes, width)
        for i in range(count):
            out[i] = cells[start + i * step]


def inner_kernel(planes, cells, mixing, thermal, weights, diffused, sums, heated_sums, coefs):
    row_count, rows, depth = cells.shape
    species = weights.shape[1]
    width = row_count // planes
    shape = (row_count, depth)
    lane, row = lanes_of(shape), rows_of(shape)
    mix = mixing[...]
    up = 0.5 * (mix + pltpu.roll(mix, depth - 1, axis=1))
    up = jnp.where(lane == depth - 1, 0.0, up)
    coefs[0] = up
    down = pltpu.roll(up, 1, axis=1)
    coefs[1] = down
    total = up + down
    up = 0.5 * (mix + pltpu.roll(mix, row_count - 1, axis=0))
    up = jnp.where(row % width == width - 1, 0.0, up)
    coefs[2] = up
    down = pltpu.roll(up, 1, axis=0)
    coefs[3] = down
    total = total + (up + down)
    edge = jnp.zeros((width, depth), F32)
    up = jnp.concatenate([0.5 * (mix[: row_count - width] + mix[width:]), edge], axis=0)
    coefs[4] = up
    down = jnp.concatenate([edge, up[: row_count - width]], axis=0)
    coefs[5] = down
    coefs[6] = total + (up + down)
    coefs[7] = rate(thermal)

    weight = jnp.broadcast_to(weight_column(weights, rows), (rows, depth))
    whole = species // SUBLANES * SUBLANES
    ones = rows_of((rows - whole, depth)) >= species - whole
    sums[...] = jnp.zeros_like(sums)
    heated_sums[...] = jnp.zeros_like(heated_sums)

    def advance(pair):
        values, found = [], []
        for r in pair:
            x, y = divmod(r, width)
            c = cells[r]
            at = lambda n: coefs[n, pl.ds(r, 1), :]
            flux = at(0) * pltpu.roll(c, depth - 1, axis=1)
            flux += at(1) * pltpu.roll(c, 1, axis=1)
            if y < width - 1:
                flux += at(2) * cells[r + 1]
            if y > 0:
                flux += at(3) * cells[r - 1]
            if x < planes - 1:
                flux += at(4) * cells[r + width]
            if x > 0:
                flux += at(5) * cells[r - width]
            flux -= at(6) * c
            new = c + weight * flux
            new = jnp.concatenate([new[:whole], jnp.where(ones, 1.0, new[whole:])], axis=0)
            diffused[r] = new
            values.append(jnp.concatenate([halves(new), halves(at(7) * c)], axis=0))
            found.append(hits(cells[r, species + 1 : species + 2, :]))
        return jnp.concatenate(values, axis=1), jnp.concatenate(found, axis=1)

    pairs = [(r, r + 1) for r in range(0, row_count, 2)]
    values, made = {}, 0.0
    for t in range(len(pairs) + AHEAD):
        if t < len(pairs):
            values[t] = advance(pairs[t])
        last = t - AHEAD
        if last >= 0:
            made += binned(*values.pop(last))
            x, y = divmod(pairs[last][1], width)
            if y == width - 1:
                sums[(x + 1) // 2] += folded(made[: 2 * rows])
                heated_sums[(x + 1) // 2] += folded(made[2 * rows :])
                made = 0.0


def rate(thermal):
    return (4.0 * DT) * jnp.exp(-2.0 / thermal[...])


def stacked_square(jacobian, square):
    species, rows = jacobian.shape[0], square.shape[0] // 2
    square[...] = jnp.zeros_like(square)
    matrix = jacobian[...]
    matrix_high = matrix.astype(BF16).astype(F32)
    square[:species, :species] = matrix_high
    square[:species, rows : rows + species] = matrix_high
    square[rows : rows + species, :species] = matrix - matrix_high
    return square[...].astype(BF16)


def kinetics_kernel(cells, diffused, thermal, jacobian, held, advanced, rates, square):
    row_count, rows, depth = cells.shape
    left = stacked_square(jacobian, square)
    rates[...] = rate(thermal)
    pairs = [(r, r + 1) for r in range(0, row_count, 2)]
    mixed = {}
    for t in range(len(pairs) + AHEAD):
        if t < len(pairs):
            wide = jnp.concatenate([halves(cells[r]) for r in pairs[t]], axis=1)
            mixed[t] = folded(jnp.dot(left, wide, preferred_element_type=F32))
        now = t - AHEAD
        if now >= 0:
            product = mixed.pop(now)
            for i, r in enumerate(pairs[now]):
                advanced[r] = (
                    diffused[r]
                    + rates[pl.ds(r, 1), :] * product[:, i * depth : (i + 1) * depth]
                )


def edge_kernel(
    planes, has_b, cells, own_z, sums, heated_sums, weights, jacobian, positions, *refs
):
    halos = list(refs[: 3 + sum(has_b)])
    window, dz, square = refs[3 + sum(has_b) :]
    row_count, rows, depth = cells.shape
    species = weights.shape[1]
    width = row_count // planes
    stations = planes // 2 + 1
    weight = jnp.broadcast_to(weight_column(weights, rows), (rows, depth))
    received = {}
    for axis, both in zip(("gx", "gy", "sec"), has_b):
        received[axis] = [halos.pop(0), halos.pop(0) if both else None]

    def beyond(axis, upper, part, outside):
        first, second = (halo if halo is None else halo[part] for halo in received[axis])
        second = jnp.full_like(first, outside) if second is None else second
        is_first = upper_of(axis, 0) if upper else upper_of(axis, 1)
        edge = lax.axis_size(axis) - 1 if upper else 0
        block = jnp.where(jnp.broadcast_to(is_first, first.shape), first, second)
        inside = jnp.broadcast_to(lax.axis_index(axis) != edge, first.shape)
        return jnp.where(inside, block, outside)

    values = [[] for _ in range(stations)]
    found = [[] for _ in range(stations)]

    def moves(x, y, d, bins):
        c = cells[x * width + y]
        d = 0.5 * (c[species : species + 1] + d)
        values[(x + 1) // 2].append(halves(weight * d * c))
        found[(x + 1) // 2].append(hits(bins) - hits(c[species + 1 : species + 2]))

    for upper in (False, True):
        d_beyond = beyond("gx", upper, pl.ds(0, width), 0.0)
        bins_beyond = beyond("gx", upper, pl.ds(width, width), -1.0)
        for y in range(width):
            moves((planes - 1) * upper, y, d_beyond[y : y + 1], bins_beyond[y : y + 1])
    for upper in (False, True):
        for x in range(planes):
            d = beyond("gy", upper, (x, pl.ds(species, 1)), 0.0)
            bins = beyond("gy", upper, (x, pl.ds(species + 1, 1)), -1.0)
            moves(x, (width - 1) * upper, d, bins)
    station = ((lanes_of((1, row_count)) // width + 1) // 2).astype(F32)
    for upper in (False, True):
        c = own_z[int(upper)]
        halo = beyond("sec", upper, pl.ds(0, rows), 0.0)
        d = 0.5 * (c[species : species + 1] + halo[species : species + 1])
        delta = weight * d * (halo - c)
        dz[int(upper)] = delta
        value = halves(delta)
        for j in range(stations):
            values[j].append(value)
            found[j].append(hits(jnp.where(station == j, c[species + 1 : species + 2], -1.0)))

    left = stacked_square(jacobian, square)
    station_sums = [
        sums[j]
        + folded(jnp.dot(left, halves(heated_sums[j]), preferred_element_type=F32))
        + folded(binned(jnp.concatenate(values[j], axis=1), jnp.concatenate(found[j], axis=1)))
        for j in range(stations)
    ]
    shift = jnp.broadcast_to(positions[0:1, 0:1], (rows, NB))
    per_device = planes // 2
    for s in range(0, 2 * per_device, 2):
        parts = []
        for slot in (s, s + 1):
            part = jnp.zeros((rows, NB), F32)
            for j in range(stations):
                if 0 <= slot - j < per_device:
                    part += jnp.where(shift == slot - j, station_sums[j], 0.0)
            parts.append(part)
        window[s // 2] = jnp.concatenate(parts, axis=1)


def interior_kernel(planes, advanced, dz, total, out, sem):
    row_count, rows, depth = advanced.shape
    species = out.shape[0]
    width = row_count // planes
    shape = (rows, depth)
    lane = lanes_of(shape)
    low = dz[0]
    high = pltpu.roll(dz[1], depth - 1, axis=1)
    for plane in range(planes):
        for r in range(plane * width, (plane + 1) * width):
            turned = depth - r if r else 0
            a = pltpu.roll(low, turned, axis=1) if r else low
            b = pltpu.roll(high, turned, axis=1) if r else high
            total[r] = advanced[r] + jnp.where(
                lane == 0, a, jnp.where(lane == depth - 1, b, 0.0)
            )
        span = pl.ds(plane * width, width)
        for k in range(species):
            pltpu.make_async_copy(
                total.at[span, k, :], out.at[k, span], sem.at[plane]
            ).start()
    for plane in range(planes):
        span = pl.ds(plane * width, width)
        pltpu.make_async_copy(
            total.at[pl.ds(0, species), pl.ds(0, width), :], out.at[:, span], sem.at[plane]
        ).wait()


def last_kernel(planes, has_b, n_terms, cells, total, weights, first_out, *refs):
    halos, terms = list(refs[: 2 + sum(has_b)]), refs[2 + sum(has_b) :][:n_terms]
    out, means_out, changed, means, sem = refs[2 + sum(has_b) + n_terms :]
    row_count, rows, depth = total.shape
    species = out.shape[0]
    width = row_count // planes
    per_device, bins = means.shape[1:]
    for s in range(0, per_device, 2):
        block = sum((term[s // 2] for term in terms[1:]), terms[0][s // 2])
        block = block / jnp.maximum(block[species + 1 : species + 2], 1.0)
        means[:, s, :] = block[:species, :bins]
        means[:, s + 1, :] = block[:species, bins:]
    copies = [pltpu.make_async_copy(means, means_out, sem.at[0])]
    copies[0].start()

    weight = jnp.broadcast_to(weight_column(weights, rows), (rows, depth))
    received = {}
    for axis, both in zip(("gx", "gy"), has_b):
        received[axis] = [halos.pop(0), halos.pop(0) if both else None]

    def share(axis, upper, c, i):
        first, second = received[axis]
        is_first = jnp.broadcast_to(upper_of(axis, 0) if upper else upper_of(axis, 1), c.shape)
        inside = jnp.broadcast_to(has_neighbour(axis, 1), c.shape)
        other = jnp.zeros_like(c) if second is None else jnp.where(inside, second[i], 0.0)
        there = jnp.where(is_first, first[i], other)
        d = 0.5 * (c[species : species + 1] + there[species : species + 1])
        return weight * d * (there - c)

    n = 0
    for x in (0, planes - 1):
        for y in range(width):
            r = x * width + y
            c = cells[r]
            new = total[r] + share("gx", x > 0, c, y)
            if y in (0, width - 1):
                new += share("gy", y > 0, c, x)
            changed[n + y] = new
        for k in range(species):
            copies.append(
                pltpu.make_async_copy(
                    changed.at[pl.ds(n, width), k, :],
                    out.at[k, pl.ds(x * width, width)],
                    sem.at[1],
                )
            )
            copies[-1].start()
        n += width
    planes_changed = changed.at[pl.ds(0, n), pl.ds(0, species), :]
    cells_out = out.reshape(species, planes, width, depth)
    start = n
    for y in (0, width - 1):
        for x in range(1, planes - 1):
            r = x * width + y
            changed[n + x - 1] = total[r] + share("gy", y > 0, cells[r], x)
        for k in range(species):
            copies.append(
                pltpu.make_async_copy(
                    changed.at[pl.ds(n, planes - 2), k, :],
                    cells_out.at[k, pl.ds(1, planes - 2), y, :],
                    sem.at[2],
                )
            )
            copies[-1].start()
        n += planes - 2
    rows_changed = changed.at[pl.ds(start, n - start), pl.ds(0, species), :]
    copies[0].wait()
    pltpu.make_async_copy(planes_changed, planes_changed, sem.at[1]).wait()
    pltpu.make_async_copy(rows_changed, rows_changed, sem.at[2]).wait()


def struct(*shape):
    return jax.ShapeDtypeStruct(shape, F32)


def call(
    kernel, name, out_shape, n_in, out_specs, in_specs=None, scratch=(), flops=0, moved=0, aliases=None
):
    return pl.pallas_call(
        kernel,
        out_shape=out_shape,
        in_specs=in_specs or [VMEM] * n_in,
        out_specs=out_specs,
        scratch_shapes=list(scratch),
        input_output_aliases=aliases or {},
        name=name,
        compiler_params=pltpu.CompilerParams(vmem_limit_bytes=32 * 1024 * 1024),
        cost_estimate=pl.CostEstimate(flops=flops, bytes_accessed=moved, transcendentals=0),
    )


def joint(block, axis, source):
    deep, count = lax.axis_size("sec"), lax.axis_size(axis)
    pairs = []
    for s in range(deep):
        for i in range(count):
            t, j = source(s, i)
            pairs.append((t * count + j, s * count + i))
    return lax.ppermute(block, ("sec", axis), pairs)


def swapped(block, axis, side):
    count = lax.axis_size(axis)
    if side == 0:
        return lax.ppermute(block, axis, [(i, i ^ 1) for i in range(count)])
    if axis == "sec":
        pairs = [(i, ((i + 1) ^ 1) - 1) for i in range(1, count - 1)]
        return lax.ppermute(block, axis, [*pairs, (0, count - 1), (count - 1, 0)])
    return joint(
        block,
        axis,
        lambda s, i: (s, ((i + 1) ^ 1) - 1) if 0 < i < count - 1 else (s ^ 1, i),
    )


def summed(block):
    deep, gx, gy = (lax.axis_size(axis) for axis in ("sec", "gx", "gy"))
    half = block.shape[0] // 2
    block = block[:half] + joint(block[half:], "gx", lambda s, i: (s ^ 1, (i - 1) % gx))
    steps = [(1 << n, 0) for n in range(1, deep.bit_length() - 1)]
    steps += [(0, 1 << n) for n in range(gy.bit_length() - 1)]
    terms = [block]
    while steps:
        (a, b), (c, d) = steps.pop(0), steps.pop(0) if steps else (0, 0)
        block = sum(terms[1:], terms[0])
        terms = [block]
        for e, f in dict.fromkeys([(a, b), (a ^ c, b ^ d), (c, d)]):
            if e or f:
                terms.append(joint(block, "gy", lambda s, i: (s ^ 1 ^ e, i ^ f)))
    return terms


def on_device(
    composition_matrix,
    local_mixing_coefficient,
    thermal_field,
    component_mixing_weight,
    kinetics_jacobian,
    mixture_classes,
    streamwise_positions,
):
    species, planes, width, depth = composition_matrix.shape
    row_count = planes * width
    rows = padded_rows(species)
    cells = composition_matrix.reshape(species, row_count, depth)
    mixing = local_mixing_coefficient.reshape(row_count, depth)
    thermal = thermal_field.reshape(row_count, depth)
    classes = mixture_classes.reshape(row_count, depth)
    weights = component_mixing_weight.reshape(1, species)
    positions = streamwise_positions.reshape(1, -1)
    per_device = planes // 2
    has_b = tuple(lax.axis_size(axis) > 2 for axis in ("gx", "gy", "sec"))
    sides = [
        (axis, side)
        for axis, both in zip(("gx", "gy", "sec"), has_b)
        for side in range(1 + both)
    ]
    shapes = {
        ("gx", 0): struct(2 * width, depth),
        ("gx", 1): struct(2 * width, depth),
        ("gy", 0): struct(planes, rows, depth),
        ("gy", 1): struct(planes, rows, depth),
        ("sec", 0): struct(rows, row_count),
        ("sec", 1): struct(max(rows, 2 * width + SUBLANES), row_count),
    }

    rows_in, own_z, *faces = call(
        functools.partial(pack_kernel, planes, has_b),
        "faces",
        [
            struct(row_count, rows, depth),
            struct(2, rows, row_count),
            *[shapes[side] for side in sides],
        ],
        3,
        [VMEM] * (2 + len(sides)),
        in_specs=[ANY] * 3,
        scratch=[
            pltpu.VMEM((row_count, depth), jnp.int32),
            pltpu.SemaphoreType.DMA((planes // 2,)),
            pltpu.SemaphoreType.DMA((2,)),
        ],
    )(*[pltpu.with_memory_space_constraint(x, pltpu.HBM) for x in (cells, mixing, classes)])
    halos = [swapped(face, axis, side) for face, (axis, side) in zip(faces, sides)]

    diffused, sums, heated_sums = call(
        functools.partial(inner_kernel, planes),
        "inside",
        [
            struct(row_count, rows, depth),
            struct(per_device + 1, rows, NB),
            struct(per_device + 1, rows, NB),
        ],
        4,
        [VMEM] * 3,
        scratch=[pltpu.VMEM((8, row_count, depth), F32)],
        flops=10_000_000,
        moved=4_000_000,
    )(rows_in, mixing, thermal, weights)

    window, dz = call(
        functools.partial(edge_kernel, planes, has_b),
        "edges",
        [struct(per_device, rows, 2 * NB), struct(2, rows, row_count)],
        7 + len(halos),
        [VMEM] * 2,
        scratch=[pltpu.VMEM((2 * rows, 2 * rows), F32)],
    )(rows_in, own_z, sums, heated_sums, weights, kinetics_jacobian, positions, *halos)

    deep = lax.axis_size("sec")
    window = window + lax.ppermute(window, "sec", [(i, i ^ 1) for i in range(deep)])
    advanced = call(
        kinetics_kernel,
        "kinetics",
        struct(row_count, rows, depth),
        5,
        VMEM,
        scratch=[
            pltpu.VMEM((row_count, depth), F32),
            pltpu.VMEM((2 * rows, 2 * rows), F32),
        ],
        flops=0,
        moved=0,
    )(rows_in, diffused, thermal, kinetics_jacobian, window)
    terms = summed(window)

    outer_planes = call(
        functools.partial(plane_kernel, planes),
        "planes",
        [struct(width, rows, depth)] * (1 + has_b[0]),
        2,
        [VMEM] * (1 + has_b[0]),
    )(rows_in, advanced)
    wide_halos = [swapped(face, "gx", side) for side, face in enumerate(outer_planes)]
    wide_halos += [halo for halo, (axis, _) in zip(halos, sides) if axis == "gy"]

    total, advanced = call(
        functools.partial(interior_kernel, planes),
        "interior",
        [struct(row_count, rows, depth), struct(species, row_count, depth)],
        2,
        [VMEM, ANY],
        scratch=[pltpu.SemaphoreType.DMA((planes,))],
        flops=1_000_000,
        moved=3_000_000,
    )(advanced, dz)
    ins = [rows_in, total, weights, advanced, *wide_halos, *terms]
    specs = [VMEM] * len(ins)
    specs[3] = ANY
    advanced, cond_means = call(
        functools.partial(last_kernel, planes, has_b[:2], len(terms)),
        "last",
        [struct(species, row_count, depth), struct(species, per_device, NB)],
        len(ins),
        [ANY, ANY],
        in_specs=specs,
        scratch=[
            pltpu.VMEM((2 * (width + planes - 2), rows, depth), F32),
            pltpu.VMEM((species, per_device, NB), F32),
            pltpu.SemaphoreType.DMA((3,)),
        ],
        aliases={3: 0},
    )(*ins)
    return advanced.reshape(composition_matrix.shape), cond_means


def solution(mesh):
    in_specs = (
        P(None, "gx", "gy", "sec"),
        P("gx", "gy", "sec"),
        P("gx", "gy", "sec"),
        P(),
        P(),
        P("gx", "gy", "sec"),
        P(),
    )
    out_specs = (P(None, "gx", "gy", "sec"), P(None, "gx", None))
    return jax.shard_map(
        on_device, mesh=mesh, in_specs=in_specs, out_specs=out_specs, check_vma=False
    )
```

```python
import functools

import jax
import jax.numpy as jnp
from jax import lax
from jax.experimental import pallas as pl
from jax.experimental.pallas import tpu as pltpu
from jax.sharding import PartitionSpec as P

NB = 64
SUBLANES = 8
LANES = 128
F32 = jnp.float32
BF16 = jnp.bfloat16
VMEM = pl.BlockSpec(memory_space=pltpu.VMEM)
ANY = pl.BlockSpec(memory_space=pl.ANY)
DT = 0.05
AHEAD = 2


def padded_rows(species):
    return -(-(species + 2) // SUBLANES) * SUBLANES


def lanes_of(shape):
    return lax.broadcasted_iota(jnp.int32, shape, len(shape) - 1)


def rows_of(shape):
    return lax.broadcasted_iota(jnp.int32, shape, len(shape) - 2)


def halves(block):
    high = block.astype(BF16).astype(F32)
    return jnp.concatenate([high, block - high], axis=0).astype(BF16)


def weight_column(weights_ref, rows):
    species = weights_ref.shape[1]
    shape = (rows, species)
    spread = jnp.where(rows_of(shape) == lanes_of(shape), weights_ref[...], 0.0)
    return DT * jnp.sum(spread, axis=1, keepdims=True)


def hits(classes):
    shape = (NB, classes.shape[1])
    bins = jnp.broadcast_to(classes.astype(BF16), shape)
    found = bins == rows_of(shape).astype(F32).astype(BF16)
    return jnp.where(found, jnp.ones((), BF16), jnp.zeros((), BF16))


def binned(values, hit):
    return lax.dot_general(
        values, hit, (((1,), (1,)), ((), ())), preferred_element_type=F32
    )


def folded(product):
    rows = product.shape[0] // 2
    return product[:rows] + product[rows:]


def upper_of(axis, side):
    even = lax.axis_index(axis) % 2 == 0
    return even if side == 0 else jnp.logical_not(even)


def has_neighbour(axis, side):
    if side == 0:
        return True
    edge = jnp.where(upper_of(axis, 1), lax.axis_size(axis) - 1, 0)
    return lax.axis_index(axis) != edge


def face_rows(axis, upper, planes, width):
    if axis == "gx":
        return jnp.where(upper, (planes - 1) * width, 0), 1, width
    return jnp.where(upper, width - 1, 0), width, planes


def pack_kernel(planes, has_b, cells, mixing, classes, *refs):
    outs, (bins, sem, field_sem) = refs[:-3], refs[-3:]
    rows_out, own_z = outs[0], outs[1]
    faces = list(outs[2:])
    species, row_count, depth = cells.shape
    rows = rows_out.shape[1]
    width = row_count // planes
    chunk = row_count // sem.shape[0]
    field_copies = [
        pltpu.make_async_copy(mixing, rows_out.at[:, species, :], field_sem.at[0]),
        pltpu.make_async_copy(classes, bins, field_sem.at[1]),
    ]
    for copy in field_copies:
        copy.start()
    for n in range(sem.shape[0]):
        span = pl.ds(n * chunk, chunk)
        for k in range(species):
            pltpu.make_async_copy(
                cells.at[k, span], rows_out.at[span, k, :], sem.at[n]
            ).start()

    lane = lanes_of((SUBLANES, depth))
    zero = jnp.zeros((SUBLANES, depth), F32)

    def gathered(groups, span, low, high):
        low, high = list(low), list(high)
        for r in span:
            at, before = lane == r, lane == (r - 1) % depth
            for i, g in enumerate(groups):
                block = rows_out[r, pl.ds(g, SUBLANES), :]
                turned = pltpu.roll(block, r, axis=1) if r else block
                low[i] = jnp.where(at, turned, low[i])
                high[i] = jnp.where(before, turned, high[i])
        return low, high

    whole = species // SUBLANES * SUBLANES
    first = range(0, whole, SUBLANES)
    rest = range(whole, rows, SUBLANES)
    low, high = [zero] * len(first), [zero] * len(first)
    for n in range(sem.shape[0]):
        arrived = rows_out.at[pl.ds(n * chunk, chunk), pl.ds(0, species), :]
        pltpu.make_async_copy(arrived, arrived, sem.at[n]).wait()
        low, high = gathered(first, range(n * chunk, (n + 1) * chunk), low, high)
    for copy in field_copies:
        copy.wait()
    for r in range(0, row_count, SUBLANES):
        span = pl.ds(r, SUBLANES)
        rows_out[span, species + 1, :] = bins[span, :].astype(F32)
    lows, highs = gathered(rest, range(row_count), [zero] * len(rest), [zero] * len(rest))
    for i, g in enumerate([*first, *rest]):
        own_z[0, pl.ds(g, SUBLANES), :] = (low + lows)[i]
        own_z[1, pl.ds(g, SUBLANES), :] = pltpu.roll((high + highs)[i], 1, axis=1)
    for axis, both in zip(("gx", "gy", "sec"), has_b):
        for side in range(1 + both):
            out = faces.pop(0)
            upper = upper_of(axis, side)
            if axis == "sec":
                out[pl.ds(0, rows), :] = own_z[jnp.where(upper, 1, 0)]
                continue
            start, step, count = face_rows(axis, upper, planes, width)
            for i in range(count):
                r = start + i * step
                if axis == "gy":
                    out[i] = rows_out[r]
                else:
                    out[pl.ds(i, 1), :] = rows_out[r, pl.ds(species, 1), :]
                    out[pl.ds(count + i, 1), :] = rows_out[r, pl.ds(species + 1, 1), :]


def join_kernel(window, received, after, out):
    out[...] = window[...] + received[...]


def plane_kernel(planes, cells, held, *faces):
    width = cells.shape[0] // planes
    for side, out in enumerate(faces):
        start, step, count = face_rows("gx", upper_of("gx", side), planes, width)
        for i in range(count):
            out[i] = cells[start + i * step]


def inner_kernel(planes, cells, mixing, thermal, weights, diffused, sums, heated_sums, coefs):
    row_count, rows, depth = cells.shape
    species = weights.shape[1]
    width = row_count // planes
    shape = (row_count, depth)
    lane, row = lanes_of(shape), rows_of(shape)
    mix = mixing[...]
    up = 0.5 * (mix + pltpu.roll(mix, depth - 1, axis=1))
    up = jnp.where(lane == depth - 1, 0.0, up)
    coefs[0] = up
    down = pltpu.roll(up, 1, axis=1)
    coefs[1] = down
    total = up + down
    up = 0.5 * (mix + pltpu.roll(mix, row_count - 1, axis=0))
    up = jnp.where(row % width == width - 1, 0.0, up)
    coefs[2] = up
    down = pltpu.roll(up, 1, axis=0)
    coefs[3] = down
    total = total + (up + down)
    edge = jnp.zeros((width, depth), F32)
    up = jnp.concatenate([0.5 * (mix[: row_count - width] + mix[width:]), edge], axis=0)
    coefs[4] = up
    down = jnp.concatenate([edge, up[: row_count - width]], axis=0)
    coefs[5] = down
    coefs[6] = total + (up + down)
    coefs[7] = rate(thermal)

    weight = jnp.broadcast_to(weight_column(weights, rows), (rows, depth))
    whole = species // SUBLANES * SUBLANES
    ones = rows_of((rows - whole, depth)) >= species - whole
    sums[...] = jnp.zeros_like(sums)
    heated_sums[...] = jnp.zeros_like(heated_sums)

    def advance(pair):
        values, found = [], []
        for r in pair:
            x, y = divmod(r, width)
            c = cells[r]
            at = lambda n: coefs[n, pl.ds(r, 1), :]
            flux = at(0) * pltpu.roll(c, depth - 1, axis=1)
            flux += at(1) * pltpu.roll(c, 1, axis=1)
            if y < width - 1:
                flux += at(2) * cells[r + 1]
            if y > 0:
                flux += at(3) * cells[r - 1]
            if x < planes - 1:
                flux += at(4) * cells[r + width]
            if x > 0:
                flux += at(5) * cells[r - width]
            flux -= at(6) * c
            new = c + weight * flux
            new = jnp.concatenate([new[:whole], jnp.where(ones, 1.0, new[whole:])], axis=0)
            diffused[r] = new
            values.append(jnp.concatenate([halves(new), halves(at(7) * c)], axis=0))
            found.append(hits(cells[r, species + 1 : species + 2, :]))
        return jnp.concatenate(values, axis=1), jnp.concatenate(found, axis=1)

    pairs = [(r, r + 1) for r in range(0, row_count, 2)]
    values, made = {}, 0.0
    for t in range(len(pairs) + AHEAD):
        if t < len(pairs):
            values[t] = advance(pairs[t])
        last = t - AHEAD
        if last >= 0:
            made += binned(*values.pop(last))
            x, y = divmod(pairs[last][1], width)
            if y == width - 1:
                sums[(x + 1) // 2] += folded(made[: 2 * rows])
                heated_sums[(x + 1) // 2] += folded(made[2 * rows :])
                made = 0.0


def rate(thermal):
    return (4.0 * DT) * jnp.exp(-2.0 / thermal[...])


def stacked_square(jacobian, square):
    species, rows = jacobian.shape[0], square.shape[0] // 2
    square[...] = jnp.zeros_like(square)
    matrix = jacobian[...]
    matrix_high = matrix.astype(BF16).astype(F32)
    square[:species, :species] = matrix_high
    square[:species, rows : rows + species] = matrix_high
    square[rows : rows + species, :species] = matrix - matrix_high
    return square[...].astype(BF16)


def kinetics_kernel(cells, diffused, thermal, jacobian, held, advanced, rates, square):
    row_count, rows, depth = cells.shape
    left = stacked_square(jacobian, square)
    rates[...] = rate(thermal)
    pairs = [(r, r + 1) for r in range(0, row_count, 2)]
    mixed = {}
    for t in range(len(pairs) + AHEAD):
        if t < len(pairs):
            wide = jnp.concatenate([halves(cells[r]) for r in pairs[t]], axis=1)
            mixed[t] = folded(jnp.dot(left, wide, preferred_element_type=F32))
        now = t - AHEAD
        if now >= 0:
            product = mixed.pop(now)
            for i, r in enumerate(pairs[now]):
                advanced[r] = (
                    diffused[r]
                    + rates[pl.ds(r, 1), :] * product[:, i * depth : (i + 1) * depth]
                )


def edge_kernel(
    planes, has_b, cells, own_z, sums, heated_sums, weights, jacobian, positions, *refs
):
    halos = list(refs[: 3 + sum(has_b)])
    window, dz, square = refs[3 + sum(has_b) :]
    row_count, rows, depth = cells.shape
    species = weights.shape[1]
    width = row_count // planes
    stations = planes // 2 + 1
    weight = jnp.broadcast_to(weight_column(weights, rows), (rows, depth))
    received = {}
    for axis, both in zip(("gx", "gy", "sec"), has_b):
        received[axis] = [halos.pop(0), halos.pop(0) if both else None]

    def beyond(axis, upper, part, outside):
        first, second = (halo if halo is None else halo[part] for halo in received[axis])
        second = jnp.full_like(first, outside) if second is None else second
        is_first = upper_of(axis, 0) if upper else upper_of(axis, 1)
        edge = lax.axis_size(axis) - 1 if upper else 0
        block = jnp.where(jnp.broadcast_to(is_first, first.shape), first, second)
        inside = jnp.broadcast_to(lax.axis_index(axis) != edge, first.shape)
        return jnp.where(inside, block, outside)

    values = [[] for _ in range(stations)]
    found = [[] for _ in range(stations)]

    def moves(x, y, d, bins):
        c = cells[x * width + y]
        d = 0.5 * (c[species : species + 1] + d)
        values[(x + 1) // 2].append(halves(weight * d * c))
        found[(x + 1) // 2].append(hits(bins) - hits(c[species + 1 : species + 2]))

    for upper in (False, True):
        d_beyond = beyond("gx", upper, pl.ds(0, width), 0.0)
        bins_beyond = beyond("gx", upper, pl.ds(width, width), -1.0)
        for y in range(width):
            moves((planes - 1) * upper, y, d_beyond[y : y + 1], bins_beyond[y : y + 1])
    for upper in (False, True):
        for x in range(planes):
            d = beyond("gy", upper, (x, pl.ds(species, 1)), 0.0)
            bins = beyond("gy", upper, (x, pl.ds(species + 1, 1)), -1.0)
            moves(x, (width - 1) * upper, d, bins)
    station = ((lanes_of((1, row_count)) // width + 1) // 2).astype(F32)
    for upper in (False, True):
        c = own_z[int(upper)]
        halo = beyond("sec", upper, pl.ds(0, rows), 0.0)
        d = 0.5 * (c[species : species + 1] + halo[species : species + 1])
        delta = weight * d * (halo - c)
        dz[int(upper)] = delta
        value = halves(delta)
        for j in range(stations):
            values[j].append(value)
            found[j].append(hits(jnp.where(station == j, c[species + 1 : species + 2], -1.0)))

    left = stacked_square(jacobian, square)
    station_sums = [
        sums[j]
        + folded(jnp.dot(left, halves(heated_sums[j]), preferred_element_type=F32))
        + folded(binned(jnp.concatenate(values[j], axis=1), jnp.concatenate(found[j], axis=1)))
        for j in range(stations)
    ]
    shift = jnp.broadcast_to(positions[0:1, 0:1], (rows, NB))
    per_device = planes // 2
    for s in range(0, 2 * per_device, 2):
        parts = []
        for slot in (s, s + 1):
            part = jnp.zeros((rows, NB), F32)
            for j in range(stations):
                if 0 <= slot - j < per_device:
                    part += jnp.where(shift == slot - j, station_sums[j], 0.0)
            parts.append(part)
        window[s // 2] = jnp.concatenate(parts, axis=1)


def interior_kernel(planes, advanced, dz, total, out, sem):
    row_count, rows, depth = advanced.shape
    species = out.shape[0]
    width = row_count // planes
    shape = (rows, depth)
    lane = lanes_of(shape)
    low = dz[0]
    high = pltpu.roll(dz[1], depth - 1, axis=1)
    for plane in range(planes):
        for r in range(plane * width, (plane + 1) * width):
            turned = depth - r if r else 0
            a = pltpu.roll(low, turned, axis=1) if r else low
            b = pltpu.roll(high, turned, axis=1) if r else high
            total[r] = advanced[r] + jnp.where(
                lane == 0, a, jnp.where(lane == depth - 1, b, 0.0)
            )
        span = pl.ds(plane * width, width)
        for k in range(species):
            pltpu.make_async_copy(
                total.at[span, k, :], out.at[k, span], sem.at[plane]
            ).start()
    for plane in range(planes):
        span = pl.ds(plane * width, width)
        pltpu.make_async_copy(
            total.at[pl.ds(0, species), pl.ds(0, width), :], out.at[:, span], sem.at[plane]
        ).wait()


def face_kernel(planes, has_b, cells, total, weights, *refs):
    halos, changed = list(refs[:-1]), refs[-1]
    row_count, rows, depth = total.shape
    species = weights.shape[1]
    width = row_count // planes
    weight = jnp.broadcast_to(weight_column(weights, rows), (rows, depth))
    received = {}
    for axis, both in zip(("gx", "gy"), has_b):
        received[axis] = [halos.pop(0), halos.pop(0) if both else None]

    def share(axis, upper, c, i):
        first, second = received[axis]
        is_first = jnp.broadcast_to(upper_of(axis, 0) if upper else upper_of(axis, 1), c.shape)
        inside = jnp.broadcast_to(has_neighbour(axis, 1), c.shape)
        other = jnp.zeros_like(c) if second is None else jnp.where(inside, second[i], 0.0)
        there = jnp.where(is_first, first[i], other)
        d = 0.5 * (c[species : species + 1] + there[species : species + 1])
        return weight * d * (there - c)

    n = 0
    for x in (0, planes - 1):
        for y in range(width):
            r = x * width + y
            c = cells[r]
            new = total[r] + share("gx", x > 0, c, y)
            if y in (0, width - 1):
                new += share("gy", y > 0, c, x)
            changed[n] = new
            n += 1
    for y in (0, width - 1):
        for x in range(1, planes - 1):
            r = x * width + y
            changed[n] = total[r] + share("gy", y > 0, cells[r], x)
            n += 1


def last_kernel(planes, changed, first_out, *refs):
    terms, (out, means_out, means, sem) = refs[:-4], refs[-4:]
    species, row_count, _ = out.shape
    width = row_count // planes
    per_device, bins = means.shape[1:]
    copies = []
    n = 0
    for x in (0, planes - 1):
        for k in range(species):
            copies.append(
                pltpu.make_async_copy(
                    changed.at[pl.ds(n, width), k, :],
                    out.at[k, pl.ds(x * width, width)],
                    sem.at[1],
                )
            )
        n += width
    cells_out = out.reshape(species, planes, width, out.shape[2])
    for y in (0, width - 1):
        for k in range(species):
            copies.append(
                pltpu.make_async_copy(
                    changed.at[pl.ds(n, planes - 2), k, :],
                    cells_out.at[k, pl.ds(1, planes - 2), y, :],
                    sem.at[1],
                )
            )
        n += planes - 2
    for s in range(0, per_device, 2):
        block = sum((term[s // 2] for term in terms[1:]), terms[0][s // 2])
        block = block / jnp.maximum(block[species + 1 : species + 2], 1.0)
        means[:, s, :] = block[:species, :bins]
        means[:, s + 1, :] = block[:species, bins:]
    means_copy = pltpu.make_async_copy(means, means_out, sem.at[0])
    means_copy.start()
    for copy in copies:
        copy.start()
    means_copy.wait()
    all_changed = changed.at[pl.ds(0, n), pl.ds(0, species), :]
    pltpu.make_async_copy(all_changed, all_changed, sem.at[1]).wait()


def struct(*shape):
    return jax.ShapeDtypeStruct(shape, F32)


def call(
    kernel, name, out_shape, n_in, out_specs, in_specs=None, scratch=(), flops=0, moved=0, aliases=None
):
    return pl.pallas_call(
        kernel,
        out_shape=out_shape,
        in_specs=in_specs or [VMEM] * n_in,
        out_specs=out_specs,
        scratch_shapes=list(scratch),
        input_output_aliases=aliases or {},
        name=name,
        compiler_params=pltpu.CompilerParams(vmem_limit_bytes=32 * 1024 * 1024),
        cost_estimate=pl.CostEstimate(flops=flops, bytes_accessed=moved, transcendentals=0),
    )


def joint(block, axis, source):
    deep, count = lax.axis_size("sec"), lax.axis_size(axis)
    pairs = []
    for s in range(deep):
        for i in range(count):
            t, j = source(s, i)
            pairs.append((t * count + j, s * count + i))
    return lax.ppermute(block, ("sec", axis), pairs)


def swapped(block, axis, side):
    count = lax.axis_size(axis)
    if side == 0:
        return lax.ppermute(block, axis, [(i, i ^ 1) for i in range(count)])
    if axis == "sec":
        pairs = [(i, ((i + 1) ^ 1) - 1) for i in range(1, count - 1)]
        return lax.ppermute(block, axis, [*pairs, (0, count - 1), (count - 1, 0)])
    return joint(
        block,
        axis,
        lambda s, i: (s, ((i + 1) ^ 1) - 1) if 0 < i < count - 1 else (s ^ 1, i),
    )


def summed(block):
    deep, gx, gy = (lax.axis_size(axis) for axis in ("sec", "gx", "gy"))
    half = block.shape[0] // 2
    block = block[:half] + joint(block[half:], "gx", lambda s, i: (s ^ 1, (i - 1) % gx))
    steps = [(1 << n, 0) for n in range(1, deep.bit_length() - 1)]
    steps += [(0, 1 << n) for n in range(gy.bit_length() - 1)]
    terms = [block]
    while steps:
        (a, b), (c, d) = steps.pop(0), steps.pop(0) if steps else (0, 0)
        block = sum(terms[1:], terms[0])
        terms = [block]
        for e, f in dict.fromkeys([(a, b), (a ^ c, b ^ d), (c, d)]):
            if e or f:
                terms.append(joint(block, "gy", lambda s, i: (s ^ 1 ^ e, i ^ f)))
    return terms


def on_device(
    composition_matrix,
    local_mixing_coefficient,
    thermal_field,
    component_mixing_weight,
    kinetics_jacobian,
    mixture_classes,
    streamwise_positions,
):
    species, planes, width, depth = composition_matrix.shape
    row_count = planes * width
    rows = padded_rows(species)
    cells = composition_matrix.reshape(species, row_count, depth)
    mixing = local_mixing_coefficient.reshape(row_count, depth)
    thermal = thermal_field.reshape(row_count, depth)
    classes = mixture_classes.reshape(row_count, depth)
    weights = component_mixing_weight.reshape(1, species)
    positions = streamwise_positions.reshape(1, -1)
    per_device = planes // 2
    has_b = tuple(lax.axis_size(axis) > 2 for axis in ("gx", "gy", "sec"))
    sides = [
        (axis, side)
        for axis, both in zip(("gx", "gy", "sec"), has_b)
        for side in range(1 + both)
    ]
    shapes = {
        ("gx", 0): struct(2 * width, depth),
        ("gx", 1): struct(2 * width, depth),
        ("gy", 0): struct(planes, rows, depth),
        ("gy", 1): struct(planes, rows, depth),
        ("sec", 0): struct(rows, row_count),
        ("sec", 1): struct(max(rows, 2 * width + SUBLANES), row_count),
    }

    rows_in, own_z, *faces = call(
        functools.partial(pack_kernel, planes, has_b),
        "faces",
        [
            struct(row_count, rows, depth),
            struct(2, rows, row_count),
            *[shapes[side] for side in sides],
        ],
        3,
        [VMEM] * (2 + len(sides)),
        in_specs=[ANY] * 3,
        scratch=[
            pltpu.VMEM((row_count, depth), jnp.int32),
            pltpu.SemaphoreType.DMA((planes // 2,)),
            pltpu.SemaphoreType.DMA((2,)),
        ],
    )(*[pltpu.with_memory_space_constraint(x, pltpu.HBM) for x in (cells, mixing, classes)])
    halos = [swapped(face, axis, side) for face, (axis, side) in zip(faces, sides)]

    diffused, sums, heated_sums = call(
        functools.partial(inner_kernel, planes),
        "inside",
        [
            struct(row_count, rows, depth),
            struct(per_device + 1, rows, NB),
            struct(per_device + 1, rows, NB),
        ],
        4,
        [VMEM] * 3,
        scratch=[pltpu.VMEM((8, row_count, depth), F32)],
        flops=10_000_000,
        moved=4_000_000,
    )(rows_in, mixing, thermal, weights)

    window, dz = call(
        functools.partial(edge_kernel, planes, has_b),
        "edges",
        [struct(per_device, rows, 2 * NB), struct(2, rows, row_count)],
        7 + len(halos),
        [VMEM] * 2,
        scratch=[pltpu.VMEM((2 * rows, 2 * rows), F32)],
    )(rows_in, own_z, sums, heated_sums, weights, kinetics_jacobian, positions, *halos)

    advanced = call(
        kinetics_kernel,
        "kinetics",
        struct(row_count, rows, depth),
        5,
        VMEM,
        scratch=[
            pltpu.VMEM((row_count, depth), F32),
            pltpu.VMEM((2 * rows, 2 * rows), F32),
        ],
        flops=0,
        moved=0,
    )(rows_in, diffused, thermal, kinetics_jacobian, window)
    deep = lax.axis_size("sec")
    received = lax.ppermute(window, "sec", [(i, i ^ 1) for i in range(deep)])
    window = call(join_kernel, "join", struct(*window.shape), 3, VMEM)(window, received, advanced)
    terms = summed(window)

    outer_planes = call(
        functools.partial(plane_kernel, planes),
        "planes",
        [struct(width, rows, depth)] * (1 + has_b[0]),
        2,
        [VMEM] * (1 + has_b[0]),
    )(rows_in, window)
    wide_halos = [swapped(face, "gx", side) for side, face in enumerate(outer_planes)]
    wide_halos += [halo for halo, (axis, _) in zip(halos, sides) if axis == "gy"]

    total, advanced = call(
        functools.partial(interior_kernel, planes),
        "interior",
        [struct(row_count, rows, depth), struct(species, row_count, depth)],
        2,
        [VMEM, ANY],
        scratch=[pltpu.SemaphoreType.DMA((planes,))],
        flops=1_000_000,
        moved=3_000_000,
    )(advanced, dz)
    changed = call(
        functools.partial(face_kernel, planes, has_b[:2]),
        "rows_of_faces",
        struct(2 * (width + planes - 2), rows, depth),
        3 + len(wide_halos),
        VMEM,
    )(rows_in, total, weights, *wide_halos)
    advanced, cond_means = call(
        functools.partial(last_kernel, planes),
        "last",
        [struct(species, row_count, depth), struct(species, per_device, NB)],
        2 + len(terms),
        [ANY, ANY],
        in_specs=[VMEM, ANY] + [VMEM] * len(terms),
        scratch=[
            pltpu.VMEM((species, per_device, NB), F32),
            pltpu.SemaphoreType.DMA((2,)),
        ],
        aliases={1: 0},
    )(changed, advanced, *terms)
    return advanced.reshape(composition_matrix.shape), cond_means


def solution(mesh):
    in_specs = (
        P(None, "gx", "gy", "sec"),
        P("gx", "gy", "sec"),
        P("gx", "gy", "sec"),
        P(),
        P(),
        P("gx", "gy", "sec"),
        P(),
    )
    out_specs = (P(None, "gx", "gy", "sec"), P(None, "gx", None))
    return jax.shard_map(
        on_device, mesh=mesh, in_specs=in_specs, out_specs=out_specs, check_vma=False
    )
```

```python
import functools

import jax
import jax.numpy as jnp
from jax import lax
from jax.experimental import pallas as pl
from jax.experimental.pallas import tpu as pltpu
from jax.sharding import PartitionSpec as P

NB = 64
SUBLANES = 8
LANES = 128
F32 = jnp.float32
BF16 = jnp.bfloat16
VMEM = pl.BlockSpec(memory_space=pltpu.VMEM)
ANY = pl.BlockSpec(memory_space=pl.ANY)
DT = 0.05
AHEAD = 2


def padded_rows(species):
    return -(-(species + 2) // SUBLANES) * SUBLANES


def lanes_of(shape):
    return lax.broadcasted_iota(jnp.int32, shape, len(shape) - 1)


def rows_of(shape):
    return lax.broadcasted_iota(jnp.int32, shape, len(shape) - 2)


def halves(block):
    high = block.astype(BF16).astype(F32)
    return jnp.concatenate([high, block - high], axis=0).astype(BF16)


def weight_column(weights_ref, rows):
    species = weights_ref.shape[1]
    shape = (rows, species)
    spread = jnp.where(rows_of(shape) == lanes_of(shape), weights_ref[...], 0.0)
    return DT * jnp.sum(spread, axis=1, keepdims=True)


def hits(classes):
    shape = (NB, classes.shape[1])
    bins = jnp.broadcast_to(classes.astype(BF16), shape)
    found = bins == rows_of(shape).astype(F32).astype(BF16)
    return jnp.where(found, jnp.ones((), BF16), jnp.zeros((), BF16))


def binned(values, hit):
    return lax.dot_general(
        values, hit, (((1,), (1,)), ((), ())), preferred_element_type=F32
    )


def folded(product):
    rows = product.shape[0] // 2
    return product[:rows] + product[rows:]


def upper_of(axis, side):
    even = lax.axis_index(axis) % 2 == 0
    return even if side == 0 else jnp.logical_not(even)


def has_neighbour(axis, side):
    if side == 0:
        return True
    edge = jnp.where(upper_of(axis, 1), lax.axis_size(axis) - 1, 0)
    return lax.axis_index(axis) != edge


def face_rows(axis, upper, planes, width):
    if axis == "gx":
        return jnp.where(upper, (planes - 1) * width, 0), 1, width
    return jnp.where(upper, width - 1, 0), width, planes


def pack_kernel(planes, has_b, cells, mixing, classes, *refs):
    outs, (bins, sem, field_sem) = refs[:-3], refs[-3:]
    rows_out, own_z = outs[0], outs[1]
    faces = list(outs[2:])
    species, row_count, depth = cells.shape
    rows = rows_out.shape[1]
    width = row_count // planes
    chunk = row_count // sem.shape[0]
    field_copies = [
        pltpu.make_async_copy(mixing, rows_out.at[:, species, :], field_sem.at[0]),
        pltpu.make_async_copy(classes, bins, field_sem.at[1]),
    ]
    for copy in field_copies:
        copy.start()
    for n in range(sem.shape[0]):
        span = pl.ds(n * chunk, chunk)
        for k in range(species):
            pltpu.make_async_copy(
                cells.at[k, span], rows_out.at[span, k, :], sem.at[n]
            ).start()

    lane = lanes_of((SUBLANES, depth))
    zero = jnp.zeros((SUBLANES, depth), F32)

    def gathered(groups, span, low, high):
        low, high = list(low), list(high)
        for r in span:
            at, before = lane == r, lane == (r - 1) % depth
            for i, g in enumerate(groups):
                block = rows_out[r, pl.ds(g, SUBLANES), :]
                turned = pltpu.roll(block, r, axis=1) if r else block
                low[i] = jnp.where(at, turned, low[i])
                high[i] = jnp.where(before, turned, high[i])
        return low, high

    whole = species // SUBLANES * SUBLANES
    first = range(0, whole, SUBLANES)
    rest = range(whole, rows, SUBLANES)
    low, high = [zero] * len(first), [zero] * len(first)
    for n in range(sem.shape[0]):
        arrived = rows_out.at[pl.ds(n * chunk, chunk), pl.ds(0, species), :]
        pltpu.make_async_copy(arrived, arrived, sem.at[n]).wait()
        low, high = gathered(first, range(n * chunk, (n + 1) * chunk), low, high)
    for copy in field_copies:
        copy.wait()
    for r in range(0, row_count, SUBLANES):
        span = pl.ds(r, SUBLANES)
        rows_out[span, species + 1, :] = bins[span, :].astype(F32)
    lows, highs = gathered(rest, range(row_count), [zero] * len(rest), [zero] * len(rest))
    for i, g in enumerate([*first, *rest]):
        own_z[0, pl.ds(g, SUBLANES), :] = (low + lows)[i]
        own_z[1, pl.ds(g, SUBLANES), :] = pltpu.roll((high + highs)[i], 1, axis=1)
    for axis, both in zip(("gx", "gy", "sec"), has_b):
        for side in range(1 + both):
            out = faces.pop(0)
            upper = upper_of(axis, side)
            if axis == "sec":
                out[pl.ds(0, rows), :] = own_z[jnp.where(upper, 1, 0)]
                continue
            start, step, count = face_rows(axis, upper, planes, width)
            for i in range(count):
                r = start + i * step
                if axis == "gy":
                    out[i] = rows_out[r]
                else:
                    out[pl.ds(i, 1), :] = rows_out[r, pl.ds(species, 1), :]
                    out[pl.ds(count + i, 1), :] = rows_out[r, pl.ds(species + 1, 1), :]


def join_kernel(window, received, after, out):
    out[...] = window[...] + received[...]


def plane_kernel(planes, cells, held, *faces):
    width = cells.shape[0] // planes
    for side, out in enumerate(faces):
        start, step, count = face_rows("gx", upper_of("gx", side), planes, width)
        for i in range(count):
            out[i] = cells[start + i * step]


def inner_kernel(planes, cells, mixing, thermal, weights, diffused, sums, heated_sums, coefs, between):
    row_count, rows, depth = cells.shape
    species = weights.shape[1]
    width = row_count // planes
    shape = (row_count, depth)
    lane, row = lanes_of(shape), rows_of(shape)
    mix = mixing[...]
    up = 0.5 * (mix + pltpu.roll(mix, depth - 1, axis=1))
    up = jnp.where(lane == depth - 1, 0.0, up)
    coefs[0] = up
    up = 0.5 * (mix + pltpu.roll(mix, row_count - 1, axis=0))
    coefs[1] = jnp.where(row % width == width - 1, 0.0, up)
    edge = jnp.zeros((width, depth), F32)
    coefs[2] = jnp.concatenate([0.5 * (mix[: row_count - width] + mix[width:]), edge], axis=0)
    coefs[3] = rate(thermal)

    weight = jnp.broadcast_to(weight_column(weights, rows), (rows, depth))
    whole = species // SUBLANES * SUBLANES
    ones = rows_of((rows - whole, depth)) >= species - whole
    sums[...] = jnp.zeros_like(sums)
    heated_sums[...] = jnp.zeros_like(heated_sums)

    across = []

    def advance(pair):
        values, found = [], []
        for r in pair:
            x, y = divmod(r, width)
            c = cells[r]
            at = lambda n: coefs[n, pl.ds(r, 1), :]
            along = at(0) * (pltpu.roll(c, depth - 1, axis=1) - c)
            flux = along - pltpu.roll(along, 1, axis=1)
            if y > 0:
                flux -= across.pop()
            if y < width - 1:
                across.append(at(1) * (cells[r + 1] - c))
                flux += across[0]
            if x > 0:
                flux -= between[y]
            if x < planes - 1:
                upward = at(2) * (cells[r + width] - c)
                between[y] = upward
                flux += upward
            new = c + weight * flux
            new = jnp.concatenate([new[:whole], jnp.where(ones, 1.0, new[whole:])], axis=0)
            diffused[r] = new
            values.append(jnp.concatenate([halves(new), halves(at(3) * c)], axis=0))
            found.append(hits(cells[r, species + 1 : species + 2, :]))
        return jnp.concatenate(values, axis=1), jnp.concatenate(found, axis=1)

    pairs = [(r, r + 1) for r in range(0, row_count, 2)]
    values, made = {}, 0.0
    for t in range(len(pairs) + AHEAD):
        if t < len(pairs):
            values[t] = advance(pairs[t])
        last = t - AHEAD
        if last >= 0:
            made += binned(*values.pop(last))
            x, y = divmod(pairs[last][1], width)
            if y == width - 1:
                sums[(x + 1) // 2] += folded(made[: 2 * rows])
                heated_sums[(x + 1) // 2] += folded(made[2 * rows :])
                made = 0.0


def rate(thermal):
    return (4.0 * DT) * jnp.exp(-2.0 / thermal[...])


def stacked_square(jacobian, square):
    species, rows = jacobian.shape[0], square.shape[0] // 2
    square[...] = jnp.zeros_like(square)
    matrix = jacobian[...]
    matrix_high = matrix.astype(BF16).astype(F32)
    square[:species, :species] = matrix_high
    square[:species, rows : rows + species] = matrix_high
    square[rows : rows + species, :species] = matrix - matrix_high
    return square[...].astype(BF16)


def kinetics_kernel(cells, diffused, thermal, jacobian, held, advanced, rates, square):
    row_count, rows, depth = cells.shape
    left = stacked_square(jacobian, square)
    rates[...] = rate(thermal)
    pairs = [(r, r + 1) for r in range(0, row_count, 2)]
    mixed = {}
    for t in range(len(pairs) + AHEAD):
        if t < len(pairs):
            wide = jnp.concatenate([halves(cells[r]) for r in pairs[t]], axis=1)
            mixed[t] = folded(jnp.dot(left, wide, preferred_element_type=F32))
        now = t - AHEAD
        if now >= 0:
            product = mixed.pop(now)
            for i, r in enumerate(pairs[now]):
                advanced[r] = (
                    diffused[r]
                    + rates[pl.ds(r, 1), :] * product[:, i * depth : (i + 1) * depth]
                )


def edge_kernel(
    planes, has_b, cells, own_z, sums, heated_sums, weights, jacobian, positions, *refs
):
    halos = list(refs[: 3 + sum(has_b)])
    window, dz, square = refs[3 + sum(has_b) :]
    row_count, rows, depth = cells.shape
    species = weights.shape[1]
    width = row_count // planes
    stations = planes // 2 + 1
    weight = jnp.broadcast_to(weight_column(weights, rows), (rows, depth))
    received = {}
    for axis, both in zip(("gx", "gy", "sec"), has_b):
        received[axis] = [halos.pop(0), halos.pop(0) if both else None]

    def beyond(axis, upper, part, outside):
        first, second = (halo if halo is None else halo[part] for halo in received[axis])
        second = jnp.full_like(first, outside) if second is None else second
        is_first = upper_of(axis, 0) if upper else upper_of(axis, 1)
        edge = lax.axis_size(axis) - 1 if upper else 0
        block = jnp.where(jnp.broadcast_to(is_first, first.shape), first, second)
        inside = jnp.broadcast_to(lax.axis_index(axis) != edge, first.shape)
        return jnp.where(inside, block, outside)

    values = [[] for _ in range(stations)]
    found = [[] for _ in range(stations)]

    def moves(x, y, d, bins):
        c = cells[x * width + y]
        d = 0.5 * (c[species : species + 1] + d)
        values[(x + 1) // 2].append(halves(weight * d * c))
        found[(x + 1) // 2].append(hits(bins) - hits(c[species + 1 : species + 2]))

    for upper in (False, True):
        d_beyond = beyond("gx", upper, pl.ds(0, width), 0.0)
        bins_beyond = beyond("gx", upper, pl.ds(width, width), -1.0)
        for y in range(width):
            moves((planes - 1) * upper, y, d_beyond[y : y + 1], bins_beyond[y : y + 1])
    for upper in (False, True):
        for x in range(planes):
            d = beyond("gy", upper, (x, pl.ds(species, 1)), 0.0)
            bins = beyond("gy", upper, (x, pl.ds(species + 1, 1)), -1.0)
            moves(x, (width - 1) * upper, d, bins)
    station = ((lanes_of((1, row_count)) // width + 1) // 2).astype(F32)
    for upper in (False, True):
        c = own_z[int(upper)]
        halo = beyond("sec", upper, pl.ds(0, rows), 0.0)
        d = 0.5 * (c[species : species + 1] + halo[species : species + 1])
        delta = weight * d * (halo - c)
        dz[int(upper)] = delta
        value = halves(delta)
        for j in range(stations):
            values[j].append(value)
            found[j].append(hits(jnp.where(station == j, c[species + 1 : species + 2], -1.0)))

    left = stacked_square(jacobian, square)
    station_sums = [
        sums[j]
        + folded(jnp.dot(left, halves(heated_sums[j]), preferred_element_type=F32))
        + folded(binned(jnp.concatenate(values[j], axis=1), jnp.concatenate(found[j], axis=1)))
        for j in range(stations)
    ]
    shift = jnp.broadcast_to(positions[0:1, 0:1], (rows, NB))
    per_device = planes // 2
    for s in range(0, 2 * per_device, 2):
        parts = []
        for slot in (s, s + 1):
            part = jnp.zeros((rows, NB), F32)
            for j in range(stations):
                if 0 <= slot - j < per_device:
                    part += jnp.where(shift == slot - j, station_sums[j], 0.0)
            parts.append(part)
        window[s // 2] = jnp.concatenate(parts, axis=1)


def neighbour_share(received, weight, axis, upper, c, i):
    first, second = received
    species_row = slice(weight[1], weight[1] + 1)
    is_first = jnp.broadcast_to(upper_of(axis, 0) if upper else upper_of(axis, 1), c.shape)
    inside = jnp.broadcast_to(has_neighbour(axis, 1), c.shape)
    other = jnp.zeros_like(c) if second is None else jnp.where(inside, second[i], 0.0)
    there = jnp.where(is_first, first[i], other)
    d = 0.5 * (c[species_row] + there[species_row])
    return weight[0] * d * (there - c)


def interior_kernel(planes, cells, advanced, dz, weights, *refs):
    received, (total, out, sem) = [*refs[:-3], None][:2], refs[-3:]
    row_count, rows, depth = advanced.shape
    species = out.shape[0]
    width = row_count // planes
    weight = (jnp.broadcast_to(weight_column(weights, rows), (rows, depth)), species)
    shape = (rows, depth)
    lane = lanes_of(shape)
    low = dz[0]
    high = pltpu.roll(dz[1], depth - 1, axis=1)
    mixed = [jnp.where(lane % 2 == parity, low, high) for parity in range(2)]
    ends = jnp.logical_or(lane == 0, lane == depth - 1)
    chunk = row_count // sem.shape[0]
    spans = [pl.ds(start, chunk) for start in range(0, row_count, chunk)]
    for n, span in enumerate(spans):
        for r in range(n * chunk, (n + 1) * chunk):
            turned = pltpu.roll(mixed[r % 2], depth - r, axis=1) if r else mixed[0]
            new = advanced[r] + jnp.where(ends, turned, 0.0)
            x, y = divmod(r, width)
            if y in (0, width - 1):
                new += neighbour_share(received, weight, "gy", y > 0, cells[r], x)
            total[r] = new
        for k in range(species):
            pltpu.make_async_copy(total.at[span, k, :], out.at[k, span], sem.at[n]).start()
    for n, span in enumerate(spans):
        written = total.at[span, pl.ds(0, species), :]
        pltpu.make_async_copy(written, written, sem.at[n]).wait()


def face_kernel(planes, cells, total, weights, *refs):
    received, changed = [*refs[:-1], None][:2], refs[-1]
    row_count, rows, depth = total.shape
    species = weights.shape[1]
    width = row_count // planes
    weight = (jnp.broadcast_to(weight_column(weights, rows), (rows, depth)), species)
    for n, x in enumerate((0, planes - 1)):
        for y in range(width):
            r = x * width + y
            new = total[r] + neighbour_share(received, weight, "gx", x > 0, cells[r], y)
            changed[n, :, y, :] = new[:species]


def last_kernel(planes, changed, first_out, *refs):
    terms, (out, means_out, means, sem) = refs[:-4], refs[-4:]
    species, row_count, _ = out.shape
    width = row_count // planes
    per_device, bins = means.shape[1:]
    for s in range(0, per_device, 2):
        block = sum((term[s // 2] for term in terms[1:]), terms[0][s // 2])
        block = block / jnp.maximum(block[species + 1 : species + 2], 1.0)
        means[:, s, :] = block[:species, :bins]
        means[:, s + 1, :] = block[:species, bins:]
    copies = [pltpu.make_async_copy(means, means_out, sem.at[0])]
    for n, x in enumerate((0, planes - 1)):
        rows_out = out.at[:, pl.ds(x * width, width)]
        copies.append(pltpu.make_async_copy(changed.at[n], rows_out, sem.at[1 + n]))
    for copy in copies:
        copy.start()
    for copy in copies:
        copy.wait()


def struct(*shape):
    return jax.ShapeDtypeStruct(shape, F32)


def call(
    kernel, name, out_shape, n_in, out_specs, in_specs=None, scratch=(), flops=0, moved=0, aliases=None
):
    return pl.pallas_call(
        kernel,
        out_shape=out_shape,
        in_specs=in_specs or [VMEM] * n_in,
        out_specs=out_specs,
        scratch_shapes=list(scratch),
        input_output_aliases=aliases or {},
        name=name,
        compiler_params=pltpu.CompilerParams(vmem_limit_bytes=32 * 1024 * 1024),
        cost_estimate=pl.CostEstimate(flops=flops, bytes_accessed=moved, transcendentals=0),
    )


def joint(block, axis, source):
    deep, count = lax.axis_size("sec"), lax.axis_size(axis)
    pairs = []
    for s in range(deep):
        for i in range(count):
            t, j = source(s, i)
            pairs.append((t * count + j, s * count + i))
    return lax.ppermute(block, ("sec", axis), pairs)


def swapped(block, axis, side):
    count = lax.axis_size(axis)
    if side == 0:
        return lax.ppermute(block, axis, [(i, i ^ 1) for i in range(count)])
    if axis == "sec":
        pairs = [(i, ((i + 1) ^ 1) - 1) for i in range(1, count - 1)]
        return lax.ppermute(block, axis, [*pairs, (0, count - 1), (count - 1, 0)])
    return joint(
        block,
        axis,
        lambda s, i: (s, ((i + 1) ^ 1) - 1) if 0 < i < count - 1 else (s ^ 1, i),
    )


def summed(block):
    deep, gx, gy = (lax.axis_size(axis) for axis in ("sec", "gx", "gy"))
    half = block.shape[0] // 2
    block = block[:half] + joint(block[half:], "gx", lambda s, i: (s ^ 1, (i - 1) % gx))
    steps = [(1 << n, 0) for n in range(1, deep.bit_length() - 1)]
    steps += [(0, 1 << n) for n in range(gy.bit_length() - 1)]
    terms = [block]
    while steps:
        (a, b), (c, d) = steps.pop(0), steps.pop(0) if steps else (0, 0)
        block = sum(terms[1:], terms[0])
        terms = [block]
        for e, f in dict.fromkeys([(a, b), (a ^ c, b ^ d), (c, d)]):
            if e or f:
                terms.append(joint(block, "gy", lambda s, i: (s ^ 1 ^ e, i ^ f)))
    return terms


def on_device(
    composition_matrix,
    local_mixing_coefficient,
    thermal_field,
    component_mixing_weight,
    kinetics_jacobian,
    mixture_classes,
    streamwise_positions,
):
    species, planes, width, depth = composition_matrix.shape
    row_count = planes * width
    rows = padded_rows(species)
    cells = composition_matrix.reshape(species, row_count, depth)
    mixing = local_mixing_coefficient.reshape(row_count, depth)
    thermal = thermal_field.reshape(row_count, depth)
    classes = mixture_classes.reshape(row_count, depth)
    weights = component_mixing_weight.reshape(1, species)
    positions = streamwise_positions.reshape(1, -1)
    per_device = planes // 2
    has_b = tuple(lax.axis_size(axis) > 2 for axis in ("gx", "gy", "sec"))
    sides = [
        (axis, side)
        for axis, both in zip(("gx", "gy", "sec"), has_b)
        for side in range(1 + both)
    ]
    shapes = {
        ("gx", 0): struct(2 * width, depth),
        ("gx", 1): struct(2 * width, depth),
        ("gy", 0): struct(planes, rows, depth),
        ("gy", 1): struct(planes, rows, depth),
        ("sec", 0): struct(rows, row_count),
        ("sec", 1): struct(max(rows, 2 * width + SUBLANES), row_count),
    }

    rows_in, own_z, *faces = call(
        functools.partial(pack_kernel, planes, has_b),
        "faces",
        [
            struct(row_count, rows, depth),
            struct(2, rows, row_count),
            *[shapes[side] for side in sides],
        ],
        3,
        [VMEM] * (2 + len(sides)),
        in_specs=[ANY] * 3,
        scratch=[
            pltpu.VMEM((row_count, depth), jnp.int32),
            pltpu.SemaphoreType.DMA((planes // 2,)),
            pltpu.SemaphoreType.DMA((2,)),
        ],
    )(*[pltpu.with_memory_space_constraint(x, pltpu.HBM) for x in (cells, mixing, classes)])
    halos = [swapped(face, axis, side) for face, (axis, side) in zip(faces, sides)]

    diffused, sums, heated_sums = call(
        functools.partial(inner_kernel, planes),
        "inside",
        [
            struct(row_count, rows, depth),
            struct(per_device + 1, rows, NB),
            struct(per_device + 1, rows, NB),
        ],
        4,
        [VMEM] * 3,
        scratch=[
            pltpu.VMEM((4, row_count, depth), F32),
            pltpu.VMEM((width, rows, depth), F32),
        ],
        flops=10_000_000,
        moved=4_000_000,
    )(rows_in, mixing, thermal, weights)

    window, dz = call(
        functools.partial(edge_kernel, planes, has_b),
        "edges",
        [struct(per_device, rows, 2 * NB), struct(2, rows, row_count)],
        7 + len(halos),
        [VMEM] * 2,
        scratch=[pltpu.VMEM((2 * rows, 2 * rows), F32)],
    )(rows_in, own_z, sums, heated_sums, weights, kinetics_jacobian, positions, *halos)

    advanced = call(
        kinetics_kernel,
        "kinetics",
        struct(row_count, rows, depth),
        5,
        VMEM,
        scratch=[
            pltpu.VMEM((row_count, depth), F32),
            pltpu.VMEM((2 * rows, 2 * rows), F32),
        ],
        flops=0,
        moved=0,
    )(rows_in, diffused, thermal, kinetics_jacobian, window)
    deep = lax.axis_size("sec")
    received = lax.ppermute(window, "sec", [(i, i ^ 1) for i in range(deep)])
    window = call(join_kernel, "join", struct(*window.shape), 3, VMEM)(window, received, advanced)
    terms = summed(window)

    outer_planes = call(
        functools.partial(plane_kernel, planes),
        "planes",
        [struct(width, rows, depth)] * (1 + has_b[0]),
        2,
        [VMEM] * (1 + has_b[0]),
    )(rows_in, window)
    wide_halos = [swapped(face, "gx", side) for side, face in enumerate(outer_planes)]
    gy_halos = [halo for halo, (axis, _) in zip(halos, sides) if axis == "gy"]

    total, advanced = call(
        functools.partial(interior_kernel, planes),
        "interior",
        [struct(row_count, rows, depth), struct(species, row_count, depth)],
        4 + len(gy_halos),
        [VMEM, ANY],
        scratch=[pltpu.SemaphoreType.DMA((planes // 2,))],
        flops=1_000_000,
        moved=3_000_000,
    )(rows_in, advanced, dz, weights, *gy_halos)
    changed = call(
        functools.partial(face_kernel, planes),
        "outer_rows",
        struct(2, species, width, depth),
        3 + len(wide_halos),
        VMEM,
    )(rows_in, total, weights, *wide_halos)
    advanced, cond_means = call(
        functools.partial(last_kernel, planes),
        "last",
        [struct(species, row_count, depth), struct(species, per_device, NB)],
        2 + len(terms),
        [ANY, ANY],
        in_specs=[VMEM, ANY] + [VMEM] * len(terms),
        scratch=[
            pltpu.VMEM((species, per_device, NB), F32),
            pltpu.SemaphoreType.DMA((3,)),
        ],
        aliases={1: 0},
    )(changed, advanced, *terms)
    return advanced.reshape(composition_matrix.shape), cond_means


def solution(mesh):
    in_specs = (
        P(None, "gx", "gy", "sec"),
        P("gx", "gy", "sec"),
        P("gx", "gy", "sec"),
        P(),
        P(),
        P("gx", "gy", "sec"),
        P(),
    )
    out_specs = (P(None, "gx", "gy", "sec"), P(None, "gx", None))
    return jax.shard_map(
        on_device, mesh=mesh, in_specs=in_specs, out_specs=out_specs, check_vma=False
    )
```

```python
import functools

import jax
import jax.numpy as jnp
from jax import lax
from jax.experimental import pallas as pl
from jax.experimental.pallas import tpu as pltpu
from jax.sharding import PartitionSpec as P

NB = 64
SUBLANES = 8
LANES = 128
F32 = jnp.float32
BF16 = jnp.bfloat16
VMEM = pl.BlockSpec(memory_space=pltpu.VMEM)
ANY = pl.BlockSpec(memory_space=pl.ANY)
DT = 0.05
AHEAD = 2


def padded_rows(species):
    return -(-(species + 2) // SUBLANES) * SUBLANES


def lanes_of(shape):
    return lax.broadcasted_iota(jnp.int32, shape, len(shape) - 1)


def rows_of(shape):
    return lax.broadcasted_iota(jnp.int32, shape, len(shape) - 2)


def halves(block):
    high = block.astype(BF16).astype(F32)
    return jnp.concatenate([high, block - high], axis=0).astype(BF16)


def weight_column(weights_ref, rows):
    species = weights_ref.shape[1]
    shape = (rows, species)
    spread = jnp.where(rows_of(shape) == lanes_of(shape), weights_ref[...], 0.0)
    return DT * jnp.sum(spread, axis=1, keepdims=True)


def hits(classes):
    shape = (NB, classes.shape[1])
    bins = jnp.broadcast_to(classes.astype(BF16), shape)
    found = bins == rows_of(shape).astype(F32).astype(BF16)
    return jnp.where(found, jnp.ones((), BF16), jnp.zeros((), BF16))


def binned(values, hit):
    return lax.dot_general(
        values, hit, (((1,), (1,)), ((), ())), preferred_element_type=F32
    )


def folded(product):
    rows = product.shape[0] // 2
    return product[:rows] + product[rows:]


def upper_of(axis, side):
    even = lax.axis_index(axis) % 2 == 0
    return even if side == 0 else jnp.logical_not(even)


def has_neighbour(axis, side):
    if side == 0:
        return True
    edge = jnp.where(upper_of(axis, 1), lax.axis_size(axis) - 1, 0)
    return lax.axis_index(axis) != edge


def face_rows(axis, upper, planes, width):
    if axis == "gx":
        return jnp.where(upper, (planes - 1) * width, 0), 1, width
    return jnp.where(upper, width - 1, 0), width, planes


def pack_kernel(planes, has_b, cells, mixing, classes, *refs):
    outs, (bins, sem, field_sem) = refs[:-3], refs[-3:]
    rows_out, own_z = outs[0], outs[1]
    faces = list(outs[2:])
    species, row_count, depth = cells.shape
    rows = rows_out.shape[1]
    width = row_count // planes
    chunk = row_count // sem.shape[0]
    field_copies = [
        pltpu.make_async_copy(mixing, rows_out.at[:, species, :], field_sem.at[0]),
        pltpu.make_async_copy(classes, bins, field_sem.at[1]),
    ]
    for copy in field_copies:
        copy.start()
    for n in range(sem.shape[0]):
        span = pl.ds(n * chunk, chunk)
        for k in range(species):
            pltpu.make_async_copy(
                cells.at[k, span], rows_out.at[span, k, :], sem.at[n]
            ).start()

    lane = lanes_of((SUBLANES, depth))
    zero = jnp.zeros((SUBLANES, depth), F32)

    def gathered(groups, span, low, high):
        low, high = list(low), list(high)
        for r in span:
            at, before = lane == r, lane == (r - 1) % depth
            for i, g in enumerate(groups):
                block = rows_out[r, pl.ds(g, SUBLANES), :]
                turned = pltpu.roll(block, r, axis=1) if r else block
                low[i] = jnp.where(at, turned, low[i])
                high[i] = jnp.where(before, turned, high[i])
        return low, high

    whole = species // SUBLANES * SUBLANES
    first = range(0, whole, SUBLANES)
    rest = range(whole, rows, SUBLANES)
    low, high = [zero] * len(first), [zero] * len(first)
    for n in range(sem.shape[0]):
        arrived = rows_out.at[pl.ds(n * chunk, chunk), pl.ds(0, species), :]
        pltpu.make_async_copy(arrived, arrived, sem.at[n]).wait()
        low, high = gathered(first, range(n * chunk, (n + 1) * chunk), low, high)
    for copy in field_copies:
        copy.wait()
    for r in range(0, row_count, SUBLANES):
        span = pl.ds(r, SUBLANES)
        rows_out[span, species + 1, :] = bins[span, :].astype(F32)
    lows, highs = gathered(rest, range(row_count), [zero] * len(rest), [zero] * len(rest))
    for i, g in enumerate([*first, *rest]):
        own_z[0, pl.ds(g, SUBLANES), :] = (low + lows)[i]
        own_z[1, pl.ds(g, SUBLANES), :] = pltpu.roll((high + highs)[i], 1, axis=1)
    for axis, both in zip(("gx", "gy", "sec"), has_b):
        for side in range(1 + both):
            out = faces.pop(0)
            upper = upper_of(axis, side)
            if axis == "sec":
                out[pl.ds(0, rows), :] = own_z[jnp.where(upper, 1, 0)]
                continue
            start, step, count = face_rows(axis, upper, planes, width)
            for i in range(count):
                r = start + i * step
                if axis == "gy":
                    out[i] = rows_out[r]
                else:
                    out[pl.ds(i, 1), :] = rows_out[r, pl.ds(species, 1), :]
                    out[pl.ds(count + i, 1), :] = rows_out[r, pl.ds(species + 1, 1), :]


def plane_kernel(planes, cells, held, *faces):
    width = cells.shape[0] // planes
    for side, out in enumerate(faces):
        start, step, count = face_rows("gx", upper_of("gx", side), planes, width)
        for i in range(count):
            out[i] = cells[start + i * step]


def inner_kernel(planes, cells, mixing, thermal, weights, diffused, sums, heated_sums, coefs, between):
    row_count, rows, depth = cells.shape
    species = weights.shape[1]
    width = row_count // planes
    shape = (row_count, depth)
    lane, row = lanes_of(shape), rows_of(shape)
    mix = mixing[...]
    up = 0.5 * (mix + pltpu.roll(mix, depth - 1, axis=1))
    up = jnp.where(lane == depth - 1, 0.0, up)
    coefs[0] = up
    up = 0.5 * (mix + pltpu.roll(mix, row_count - 1, axis=0))
    coefs[1] = jnp.where(row % width == width - 1, 0.0, up)
    edge = jnp.zeros((width, depth), F32)
    coefs[2] = jnp.concatenate([0.5 * (mix[: row_count - width] + mix[width:]), edge], axis=0)
    coefs[3] = rate(thermal)

    weight = jnp.broadcast_to(weight_column(weights, rows), (rows, depth))
    whole = species // SUBLANES * SUBLANES
    ones = rows_of((rows - whole, depth)) >= species - whole
    sums[...] = jnp.zeros_like(sums)
    heated_sums[...] = jnp.zeros_like(heated_sums)

    across = []

    def advance(pair):
        values, found = [], []
        for r in pair:
            x, y = divmod(r, width)
            c = cells[r]
            at = lambda n: coefs[n, pl.ds(r, 1), :]
            along = at(0) * (pltpu.roll(c, depth - 1, axis=1) - c)
            flux = along - pltpu.roll(along, 1, axis=1)
            if y > 0:
                flux -= across.pop()
            if y < width - 1:
                across.append(at(1) * (cells[r + 1] - c))
                flux += across[0]
            if x > 0:
                flux -= between[y]
            if x < planes - 1:
                upward = at(2) * (cells[r + width] - c)
                between[y] = upward
                flux += upward
            new = c + weight * flux
            new = jnp.concatenate([new[:whole], jnp.where(ones, 1.0, new[whole:])], axis=0)
            diffused[r] = new
            values.append(jnp.concatenate([halves(new), halves(at(3) * c)], axis=0))
            found.append(hits(cells[r, species + 1 : species + 2, :]))
        return jnp.concatenate(values, axis=1), jnp.concatenate(found, axis=1)

    pairs = [(r, r + 1) for r in range(0, row_count, 2)]
    values, made = {}, 0.0
    for t in range(len(pairs) + AHEAD):
        if t < len(pairs):
            values[t] = advance(pairs[t])
        last = t - AHEAD
        if last >= 0:
            made += binned(*values.pop(last))
            x, y = divmod(pairs[last][1], width)
            if y == width - 1:
                sums[(x + 1) // 2] += folded(made[: 2 * rows])
                heated_sums[(x + 1) // 2] += folded(made[2 * rows :])
                made = 0.0


def rate(thermal):
    return (4.0 * DT) * jnp.exp(-2.0 / thermal[...])


def stacked_square(jacobian, square):
    species, rows = jacobian.shape[0], square.shape[0] // 2
    square[...] = jnp.zeros_like(square)
    matrix = jacobian[...]
    matrix_high = matrix.astype(BF16).astype(F32)
    square[:species, :species] = matrix_high
    square[:species, rows : rows + species] = matrix_high
    square[rows : rows + species, :species] = matrix - matrix_high
    return square[...].astype(BF16)


def kinetics_kernel(cells, diffused, thermal, jacobian, held, advanced, rates, square):
    row_count, rows, depth = cells.shape
    left = stacked_square(jacobian, square)
    rates[...] = rate(thermal)
    pairs = [(r, r + 1) for r in range(0, row_count, 2)]
    mixed = {}
    for t in range(len(pairs) + AHEAD):
        if t < len(pairs):
            wide = jnp.concatenate([halves(cells[r]) for r in pairs[t]], axis=1)
            mixed[t] = folded(jnp.dot(left, wide, preferred_element_type=F32))
        now = t - AHEAD
        if now >= 0:
            product = mixed.pop(now)
            for i, r in enumerate(pairs[now]):
                advanced[r] = (
                    diffused[r]
                    + rates[pl.ds(r, 1), :] * product[:, i * depth : (i + 1) * depth]
                )


def edge_kernel(
    planes, has_b, cells, own_z, sums, heated_sums, weights, jacobian, positions, *refs
):
    halos = list(refs[: 3 + sum(has_b)])
    window, dz, square = refs[3 + sum(has_b) :]
    row_count, rows, depth = cells.shape
    species = weights.shape[1]
    width = row_count // planes
    stations = planes // 2 + 1
    weight = jnp.broadcast_to(weight_column(weights, rows), (rows, depth))
    received = {}
    for axis, both in zip(("gx", "gy", "sec"), has_b):
        received[axis] = [halos.pop(0), halos.pop(0) if both else None]

    def beyond(axis, upper, part, outside):
        first, second = (halo if halo is None else halo[part] for halo in received[axis])
        second = jnp.full_like(first, outside) if second is None else second
        is_first = upper_of(axis, 0) if upper else upper_of(axis, 1)
        edge = lax.axis_size(axis) - 1 if upper else 0
        block = jnp.where(jnp.broadcast_to(is_first, first.shape), first, second)
        inside = jnp.broadcast_to(lax.axis_index(axis) != edge, first.shape)
        return jnp.where(inside, block, outside)

    values = [[] for _ in range(stations)]
    found = [[] for _ in range(stations)]

    def moves(x, y, d, bins):
        c = cells[x * width + y]
        d = 0.5 * (c[species : species + 1] + d)
        values[(x + 1) // 2].append(halves(weight * d * c))
        found[(x + 1) // 2].append(hits(bins) - hits(c[species + 1 : species + 2]))

    for upper in (False, True):
        d_beyond = beyond("gx", upper, pl.ds(0, width), 0.0)
        bins_beyond = beyond("gx", upper, pl.ds(width, width), -1.0)
        for y in range(width):
            moves((planes - 1) * upper, y, d_beyond[y : y + 1], bins_beyond[y : y + 1])
    for upper in (False, True):
        for x in range(planes):
            d = beyond("gy", upper, (x, pl.ds(species, 1)), 0.0)
            bins = beyond("gy", upper, (x, pl.ds(species + 1, 1)), -1.0)
            moves(x, (width - 1) * upper, d, bins)
    station = ((lanes_of((1, row_count)) // width + 1) // 2).astype(F32)
    for upper in (False, True):
        c = own_z[int(upper)]
        halo = beyond("sec", upper, pl.ds(0, rows), 0.0)
        d = 0.5 * (c[species : species + 1] + halo[species : species + 1])
        delta = weight * d * (halo - c)
        dz[int(upper)] = delta
        value = halves(delta)
        for j in range(stations):
            values[j].append(value)
            found[j].append(hits(jnp.where(station == j, c[species + 1 : species + 2], -1.0)))

    left = stacked_square(jacobian, square)
    station_sums = [
        sums[j]
        + folded(jnp.dot(left, halves(heated_sums[j]), preferred_element_type=F32))
        + folded(binned(jnp.concatenate(values[j], axis=1), jnp.concatenate(found[j], axis=1)))
        for j in range(stations)
    ]
    shift = jnp.broadcast_to(positions[0:1, 0:1], (rows, NB))
    per_device = planes // 2
    for s in range(0, 2 * per_device, 2):
        parts = []
        for slot in (s, s + 1):
            part = jnp.zeros((rows, NB), F32)
            for j in range(stations):
                if 0 <= slot - j < per_device:
                    part += jnp.where(shift == slot - j, station_sums[j], 0.0)
            parts.append(part)
        window[s // 2] = jnp.concatenate(parts, axis=1)


def neighbour_share(received, weight, axis, upper, c, i):
    first, second = received
    species_row = slice(weight[1], weight[1] + 1)
    is_first = jnp.broadcast_to(upper_of(axis, 0) if upper else upper_of(axis, 1), c.shape)
    inside = jnp.broadcast_to(has_neighbour(axis, 1), c.shape)
    other = jnp.zeros_like(c) if second is None else jnp.where(inside, second[i], 0.0)
    there = jnp.where(is_first, first[i], other)
    d = 0.5 * (c[species_row] + there[species_row])
    return weight[0] * d * (there - c)


def interior_kernel(planes, cells, advanced, dz, weights, *refs):
    received, (total, out, sem) = [*refs[:-3], None][:2], refs[-3:]
    row_count, rows, depth = advanced.shape
    species = out.shape[0]
    width = row_count // planes
    weight = (jnp.broadcast_to(weight_column(weights, rows), (rows, depth)), species)
    shape = (rows, depth)
    lane = lanes_of(shape)
    low = dz[0]
    high = pltpu.roll(dz[1], depth - 1, axis=1)
    mixed = [jnp.where(lane % 2 == parity, low, high) for parity in range(2)]
    ends = jnp.logical_or(lane == 0, lane == depth - 1)
    chunk = row_count // sem.shape[0]
    spans = [pl.ds(start, chunk) for start in range(0, row_count, chunk)]
    for n, span in enumerate(spans):
        for r in range(n * chunk, (n + 1) * chunk):
            turned = pltpu.roll(mixed[r % 2], depth - r, axis=1) if r else mixed[0]
            new = advanced[r] + jnp.where(ends, turned, 0.0)
            x, y = divmod(r, width)
            if y in (0, width - 1):
                new += neighbour_share(received, weight, "gy", y > 0, cells[r], x)
            total[r] = new
        for k in range(species):
            pltpu.make_async_copy(total.at[span, k, :], out.at[k, span], sem.at[n]).start()
    for n, span in enumerate(spans):
        written = total.at[span, pl.ds(0, species), :]
        pltpu.make_async_copy(written, written, sem.at[n]).wait()


def face_kernel(planes, cells, total, weights, *refs):
    received, changed = [*refs[:-1], None][:2], refs[-1]
    row_count, rows, depth = total.shape
    species = weights.shape[1]
    width = row_count // planes
    weight = (jnp.broadcast_to(weight_column(weights, rows), (rows, depth)), species)
    for n, x in enumerate((0, planes - 1)):
        for y in range(width):
            r = x * width + y
            new = total[r] + neighbour_share(received, weight, "gx", x > 0, cells[r], y)
            changed[n, :, y, :] = new[:species]


def last_kernel(planes, changed, first_out, *refs):
    terms, (out, means_out, means, sem) = refs[:-4], refs[-4:]
    species, row_count, _ = out.shape
    width = row_count // planes
    per_device, bins = means.shape[1:]
    for s in range(0, per_device, 2):
        block = sum((term[s // 2] for term in terms[1:]), terms[0][s // 2])
        block = block / jnp.maximum(block[species + 1 : species + 2], 1.0)
        means[:, s, :] = block[:species, :bins]
        means[:, s + 1, :] = block[:species, bins:]
    copies = [pltpu.make_async_copy(means, means_out, sem.at[0])]
    for n, x in enumerate((0, planes - 1)):
        rows_out = out.at[:, pl.ds(x * width, width)]
        copies.append(pltpu.make_async_copy(changed.at[n], rows_out, sem.at[1 + n]))
    for copy in copies:
        copy.start()
    for copy in copies:
        copy.wait()


def struct(*shape):
    return jax.ShapeDtypeStruct(shape, F32)


def call(
    kernel, name, out_shape, n_in, out_specs, in_specs=None, scratch=(), flops=0, moved=0, aliases=None
):
    return pl.pallas_call(
        kernel,
        out_shape=out_shape,
        in_specs=in_specs or [VMEM] * n_in,
        out_specs=out_specs,
        scratch_shapes=list(scratch),
        input_output_aliases=aliases or {},
        name=name,
        compiler_params=pltpu.CompilerParams(vmem_limit_bytes=32 * 1024 * 1024),
        cost_estimate=pl.CostEstimate(flops=flops, bytes_accessed=moved, transcendentals=0),
    )


def joint(block, axis, source):
    deep, count = lax.axis_size("sec"), lax.axis_size(axis)
    pairs = []
    for s in range(deep):
        for i in range(count):
            t, j = source(s, i)
            pairs.append((t * count + j, s * count + i))
    return lax.ppermute(block, ("sec", axis), pairs)


def swapped(block, axis, side):
    count = lax.axis_size(axis)
    if side == 0:
        return lax.ppermute(block, axis, [(i, i ^ 1) for i in range(count)])
    if axis == "sec":
        pairs = [(i, ((i + 1) ^ 1) - 1) for i in range(1, count - 1)]
        return lax.ppermute(block, axis, [*pairs, (0, count - 1), (count - 1, 0)])
    return joint(
        block,
        axis,
        lambda s, i: (s, ((i + 1) ^ 1) - 1) if 0 < i < count - 1 else (s ^ 1, i),
    )


def summed(block):
    deep, gx, gy = (lax.axis_size(axis) for axis in ("sec", "gx", "gy"))
    half = block.shape[0] // 2
    block = block[:half] + joint(block[half:], "gx", lambda s, i: (s ^ 1, (i - 1) % gx))
    block = block + lax.ppermute(block, "sec", [(i, i ^ 1) for i in range(deep)])
    steps = [(1 << n, 0) for n in range(1, deep.bit_length() - 1)]
    steps += [(0, 1 << n) for n in range(gy.bit_length() - 1)]
    terms = [block]
    while steps:
        (a, b), (c, d) = steps.pop(0), steps.pop(0) if steps else (0, 0)
        block = sum(terms[1:], terms[0])
        terms = [block]
        for e, f in dict.fromkeys([(a, b), (a ^ c, b ^ d), (c, d)]):
            if e or f:
                terms.append(joint(block, "gy", lambda s, i: (s ^ 1 ^ e, i ^ f)))
    return terms


def on_device(
    composition_matrix,
    local_mixing_coefficient,
    thermal_field,
    component_mixing_weight,
    kinetics_jacobian,
    mixture_classes,
    streamwise_positions,
):
    species, planes, width, depth = composition_matrix.shape
    row_count = planes * width
    rows = padded_rows(species)
    cells = composition_matrix.reshape(species, row_count, depth)
    mixing = local_mixing_coefficient.reshape(row_count, depth)
    thermal = thermal_field.reshape(row_count, depth)
    classes = mixture_classes.reshape(row_count, depth)
    weights = component_mixing_weight.reshape(1, species)
    positions = streamwise_positions.reshape(1, -1)
    per_device = planes // 2
    has_b = tuple(lax.axis_size(axis) > 2 for axis in ("gx", "gy", "sec"))
    sides = [
        (axis, side)
        for axis, both in zip(("gx", "gy", "sec"), has_b)
        for side in range(1 + both)
    ]
    shapes = {
        ("gx", 0): struct(2 * width, depth),
        ("gx", 1): struct(2 * width, depth),
        ("gy", 0): struct(planes, rows, depth),
        ("gy", 1): struct(planes, rows, depth),
        ("sec", 0): struct(rows, row_count),
        ("sec", 1): struct(max(rows, 2 * width + SUBLANES), row_count),
    }

    rows_in, own_z, *faces = call(
        functools.partial(pack_kernel, planes, has_b),
        "faces",
        [
            struct(row_count, rows, depth),
            struct(2, rows, row_count),
            *[shapes[side] for side in sides],
        ],
        3,
        [VMEM] * (2 + len(sides)),
        in_specs=[ANY] * 3,
        scratch=[
            pltpu.VMEM((row_count, depth), jnp.int32),
            pltpu.SemaphoreType.DMA((planes // 2,)),
            pltpu.SemaphoreType.DMA((2,)),
        ],
    )(*[pltpu.with_memory_space_constraint(x, pltpu.HBM) for x in (cells, mixing, classes)])
    halos = [swapped(face, axis, side) for face, (axis, side) in zip(faces, sides)]

    diffused, sums, heated_sums = call(
        functools.partial(inner_kernel, planes),
        "inside",
        [
            struct(row_count, rows, depth),
            struct(per_device + 1, rows, NB),
            struct(per_device + 1, rows, NB),
        ],
        4,
        [VMEM] * 3,
        scratch=[
            pltpu.VMEM((4, row_count, depth), F32),
            pltpu.VMEM((width, rows, depth), F32),
        ],
        flops=10_000_000,
        moved=4_000_000,
    )(rows_in, mixing, thermal, weights)

    window, dz = call(
        functools.partial(edge_kernel, planes, has_b),
        "edges",
        [struct(per_device, rows, 2 * NB), struct(2, rows, row_count)],
        7 + len(halos),
        [VMEM] * 2,
        scratch=[pltpu.VMEM((2 * rows, 2 * rows), F32)],
    )(rows_in, own_z, sums, heated_sums, weights, kinetics_jacobian, positions, *halos)

    advanced = call(
        kinetics_kernel,
        "kinetics",
        struct(row_count, rows, depth),
        5,
        VMEM,
        scratch=[
            pltpu.VMEM((row_count, depth), F32),
            pltpu.VMEM((2 * rows, 2 * rows), F32),
        ],
        flops=0,
        moved=0,
    )(rows_in, diffused, thermal, kinetics_jacobian, window)
    terms = summed(window)

    outer_planes = call(
        functools.partial(plane_kernel, planes),
        "planes",
        [struct(width, rows, depth)] * (1 + has_b[0]),
        2,
        [VMEM] * (1 + has_b[0]),
    )(rows_in, advanced)
    wide_halos = [swapped(face, "gx", side) for side, face in enumerate(outer_planes)]
    gy_halos = [halo for halo, (axis, _) in zip(halos, sides) if axis == "gy"]

    total, advanced = call(
        functools.partial(interior_kernel, planes),
        "interior",
        [struct(row_count, rows, depth), struct(species, row_count, depth)],
        4 + len(gy_halos),
        [VMEM, ANY],
        scratch=[pltpu.SemaphoreType.DMA((planes // 2,))],
        flops=1_000_000,
        moved=3_000_000,
    )(rows_in, advanced, dz, weights, *gy_halos)
    changed = call(
        functools.partial(face_kernel, planes),
        "outer_rows",
        struct(2, species, width, depth),
        3 + len(wide_halos),
        VMEM,
    )(rows_in, total, weights, *wide_halos)
    advanced, cond_means = call(
        functools.partial(last_kernel, planes),
        "last",
        [struct(species, row_count, depth), struct(species, per_device, NB)],
        2 + len(terms),
        [ANY, ANY],
        in_specs=[VMEM, ANY] + [VMEM] * len(terms),
        scratch=[
            pltpu.VMEM((species, per_device, NB), F32),
            pltpu.SemaphoreType.DMA((3,)),
        ],
        aliases={1: 0},
    )(changed, advanced, *terms)
    return advanced.reshape(composition_matrix.shape), cond_means


def solution(mesh):
    in_specs = (
        P(None, "gx", "gy", "sec"),
        P("gx", "gy", "sec"),
        P("gx", "gy", "sec"),
        P(),
        P(),
        P("gx", "gy", "sec"),
        P(),
    )
    out_specs = (P(None, "gx", "gy", "sec"), P(None, "gx", None))
    return jax.shard_map(
        on_device, mesh=mesh, in_specs=in_specs, out_specs=out_specs, check_vma=False
    )
```

```python
import functools

import jax
import jax.numpy as jnp
from jax import lax
from jax.experimental import pallas as pl
from jax.experimental.pallas import tpu as pltpu
from jax.sharding import PartitionSpec as P

NB = 64
SUBLANES = 8
LANES = 128
F32 = jnp.float32
BF16 = jnp.bfloat16
VMEM = pl.BlockSpec(memory_space=pltpu.VMEM)
ANY = pl.BlockSpec(memory_space=pl.ANY)
DT = 0.05
AHEAD = 2


def padded_rows(species):
    return -(-(species + 2) // SUBLANES) * SUBLANES


def lanes_of(shape):
    return lax.broadcasted_iota(jnp.int32, shape, len(shape) - 1)


def rows_of(shape):
    return lax.broadcasted_iota(jnp.int32, shape, len(shape) - 2)


def halves(block):
    high = block.astype(BF16).astype(F32)
    return jnp.concatenate([high, block - high], axis=0).astype(BF16)


def weight_column(weights_ref, rows):
    species = weights_ref.shape[1]
    shape = (rows, species)
    spread = jnp.where(rows_of(shape) == lanes_of(shape), weights_ref[...], 0.0)
    return DT * jnp.sum(spread, axis=1, keepdims=True)


def hits(classes):
    shape = (NB, classes.shape[1])
    bins = jnp.broadcast_to(classes.astype(BF16), shape)
    found = bins == rows_of(shape).astype(F32).astype(BF16)
    return jnp.where(found, jnp.ones((), BF16), jnp.zeros((), BF16))


def binned(values, hit):
    return lax.dot_general(
        values, hit, (((1,), (1,)), ((), ())), preferred_element_type=F32
    )


def folded(product):
    rows = product.shape[0] // 2
    return product[:rows] + product[rows:]


def upper_of(axis, side):
    even = lax.axis_index(axis) % 2 == 0
    return even if side == 0 else jnp.logical_not(even)


def has_neighbour(axis, side):
    if side == 0:
        return True
    edge = jnp.where(upper_of(axis, 1), lax.axis_size(axis) - 1, 0)
    return lax.axis_index(axis) != edge


def face_rows(axis, upper, planes, width):
    if axis == "gx":
        return jnp.where(upper, (planes - 1) * width, 0), 1, width
    return jnp.where(upper, width - 1, 0), width, planes


def pack_kernel(planes, has_b, cells, mixing, classes, *refs):
    outs, (bins, sem, field_sem) = refs[:-3], refs[-3:]
    rows_out, own_z = outs[0], outs[1]
    faces = list(outs[2:])
    species, row_count, depth = cells.shape
    rows = rows_out.shape[1]
    width = row_count // planes
    chunk = row_count // sem.shape[0]
    field_copies = [
        pltpu.make_async_copy(mixing, rows_out.at[:, species, :], field_sem.at[0]),
        pltpu.make_async_copy(classes, bins, field_sem.at[1]),
    ]
    for copy in field_copies:
        copy.start()
    for n in range(sem.shape[0]):
        span = pl.ds(n * chunk, chunk)
        for k in range(species):
            pltpu.make_async_copy(
                cells.at[k, span], rows_out.at[span, k, :], sem.at[n]
            ).start()

    lane = lanes_of((SUBLANES, depth))
    zero = jnp.zeros((SUBLANES, depth), F32)

    def gathered(groups, span, low, high):
        low, high = list(low), list(high)
        for r in span:
            at, before = lane == r, lane == (r - 1) % depth
            for i, g in enumerate(groups):
                block = rows_out[r, pl.ds(g, SUBLANES), :]
                turned = pltpu.roll(block, r, axis=1) if r else block
                low[i] = jnp.where(at, turned, low[i])
                high[i] = jnp.where(before, turned, high[i])
        return low, high

    whole = species // SUBLANES * SUBLANES
    first = range(0, whole, SUBLANES)
    rest = range(whole, rows, SUBLANES)
    low, high = [zero] * len(first), [zero] * len(first)
    for n in range(sem.shape[0]):
        arrived = rows_out.at[pl.ds(n * chunk, chunk), pl.ds(0, species), :]
        pltpu.make_async_copy(arrived, arrived, sem.at[n]).wait()
        low, high = gathered(first, range(n * chunk, (n + 1) * chunk), low, high)
    for copy in field_copies:
        copy.wait()
    for r in range(0, row_count, SUBLANES):
        span = pl.ds(r, SUBLANES)
        rows_out[span, species + 1, :] = bins[span, :].astype(F32)
    lows, highs = gathered(rest, range(row_count), [zero] * len(rest), [zero] * len(rest))
    for i, g in enumerate([*first, *rest]):
        own_z[0, pl.ds(g, SUBLANES), :] = (low + lows)[i]
        own_z[1, pl.ds(g, SUBLANES), :] = pltpu.roll((high + highs)[i], 1, axis=1)
    for axis, both in zip(("gx", "gy", "sec"), has_b):
        for side in range(1 + both):
            out = faces.pop(0)
            upper = upper_of(axis, side)
            if axis == "sec":
                out[pl.ds(0, rows), :] = own_z[jnp.where(upper, 1, 0)]
                continue
            start, step, count = face_rows(axis, upper, planes, width)
            for i in range(count):
                r = start + i * step
                if axis == "gy":
                    out[i] = rows_out[r]
                else:
                    out[pl.ds(i, 1), :] = rows_out[r, pl.ds(species, 1), :]
                    out[pl.ds(count + i, 1), :] = rows_out[r, pl.ds(species + 1, 1), :]


def plane_kernel(planes, cells, held, *faces):
    width = cells.shape[0] // planes
    for side, out in enumerate(faces):
        start, step, count = face_rows("gx", upper_of("gx", side), planes, width)
        for i in range(count):
            out[i] = cells[start + i * step]


def inner_kernel(planes, cells, mixing, thermal, weights, diffused, sums, heated_sums, coefs, between):
    row_count, rows, depth = cells.shape
    species = weights.shape[1]
    width = row_count // planes
    shape = (row_count, depth)
    lane, row = lanes_of(shape), rows_of(shape)
    mix = mixing[...]
    up = 0.5 * (mix + pltpu.roll(mix, depth - 1, axis=1))
    up = jnp.where(lane == depth - 1, 0.0, up)
    coefs[0] = up
    up = 0.5 * (mix + pltpu.roll(mix, row_count - 1, axis=0))
    coefs[1] = jnp.where(row % width == width - 1, 0.0, up)
    edge = jnp.zeros((width, depth), F32)
    coefs[2] = jnp.concatenate([0.5 * (mix[: row_count - width] + mix[width:]), edge], axis=0)
    coefs[3] = rate(thermal)

    weight = jnp.broadcast_to(weight_column(weights, rows), (rows, depth))
    whole = species // SUBLANES * SUBLANES
    ones = rows_of((rows - whole, depth)) >= species - whole
    sums[...] = jnp.zeros_like(sums)
    heated_sums[...] = jnp.zeros_like(heated_sums)

    across = []

    def advance(pair):
        values, found = [], []
        for r in pair:
            x, y = divmod(r, width)
            c = cells[r]
            at = lambda n: coefs[n, pl.ds(r, 1), :]
            along = at(0) * (pltpu.roll(c, depth - 1, axis=1) - c)
            flux = along - pltpu.roll(along, 1, axis=1)
            if y > 0:
                flux -= across.pop()
            if y < width - 1:
                across.append(at(1) * (cells[r + 1] - c))
                flux += across[0]
            if x > 0:
                flux -= between[y]
            if x < planes - 1:
                upward = at(2) * (cells[r + width] - c)
                between[y] = upward
                flux += upward
            new = c + weight * flux
            new = jnp.concatenate([new[:whole], jnp.where(ones, 1.0, new[whole:])], axis=0)
            diffused[r] = new
            values.append(jnp.concatenate([halves(new), halves(at(3) * c)], axis=0))
            found.append(hits(cells[r, species + 1 : species + 2, :]))
        return jnp.concatenate(values, axis=1), jnp.concatenate(found, axis=1)

    pairs = [(r, r + 1) for r in range(0, row_count, 2)]
    values, made = {}, 0.0
    for t in range(len(pairs) + AHEAD):
        if t < len(pairs):
            values[t] = advance(pairs[t])
        last = t - AHEAD
        if last >= 0:
            made += binned(*values.pop(last))
            x, y = divmod(pairs[last][1], width)
            if y == width - 1:
                sums[(x + 1) // 2] += folded(made[: 2 * rows])
                heated_sums[(x + 1) // 2] += folded(made[2 * rows :])
                made = 0.0


def rate(thermal):
    return (4.0 * DT) * jnp.exp(-2.0 / thermal[...])


def stacked_square(jacobian, square):
    species, rows = jacobian.shape[0], square.shape[0] // 2
    square[...] = jnp.zeros_like(square)
    matrix = jacobian[...]
    matrix_high = matrix.astype(BF16).astype(F32)
    square[:species, :species] = matrix_high
    square[:species, rows : rows + species] = matrix_high
    square[rows : rows + species, :species] = matrix - matrix_high
    return square[...].astype(BF16)


def kinetics_kernel(cells, diffused, thermal, jacobian, held, advanced, rates, square):
    row_count, rows, depth = cells.shape
    left = stacked_square(jacobian, square)
    rates[...] = rate(thermal)
    pairs = [(r, r + 1) for r in range(0, row_count, 2)]
    mixed = {}
    for t in range(len(pairs) + AHEAD):
        if t < len(pairs):
            wide = jnp.concatenate([halves(cells[r]) for r in pairs[t]], axis=1)
            mixed[t] = folded(jnp.dot(left, wide, preferred_element_type=F32))
        now = t - AHEAD
        if now >= 0:
            product = mixed.pop(now)
            for i, r in enumerate(pairs[now]):
                advanced[r] = (
                    diffused[r]
                    + rates[pl.ds(r, 1), :] * product[:, i * depth : (i + 1) * depth]
                )


def edge_kernel(
    planes, has_b, cells, own_z, sums, heated_sums, weights, jacobian, positions, *refs
):
    halos = list(refs[: 3 + sum(has_b)])
    window, dz, square = refs[3 + sum(has_b) :]
    row_count, rows, depth = cells.shape
    species = weights.shape[1]
    width = row_count // planes
    stations = planes // 2 + 1
    weight = jnp.broadcast_to(weight_column(weights, rows), (rows, depth))
    received = {}
    for axis, both in zip(("gx", "gy", "sec"), has_b):
        received[axis] = [halos.pop(0), halos.pop(0) if both else None]

    def beyond(axis, upper, part, outside):
        first, second = (halo if halo is None else halo[part] for halo in received[axis])
        second = jnp.full_like(first, outside) if second is None else second
        is_first = upper_of(axis, 0) if upper else upper_of(axis, 1)
        edge = lax.axis_size(axis) - 1 if upper else 0
        block = jnp.where(jnp.broadcast_to(is_first, first.shape), first, second)
        inside = jnp.broadcast_to(lax.axis_index(axis) != edge, first.shape)
        return jnp.where(inside, block, outside)

    values = [[] for _ in range(stations)]
    found = [[] for _ in range(stations)]

    def moves(x, y, d, bins):
        c = cells[x * width + y]
        d = 0.5 * (c[species : species + 1] + d)
        values[(x + 1) // 2].append(halves(weight * d * c))
        found[(x + 1) // 2].append(hits(bins) - hits(c[species + 1 : species + 2]))

    for upper in (False, True):
        d_beyond = beyond("gx", upper, pl.ds(0, width), 0.0)
        bins_beyond = beyond("gx", upper, pl.ds(width, width), -1.0)
        for y in range(width):
            moves((planes - 1) * upper, y, d_beyond[y : y + 1], bins_beyond[y : y + 1])
    for upper in (False, True):
        for x in range(planes):
            d = beyond("gy", upper, (x, pl.ds(species, 1)), 0.0)
            bins = beyond("gy", upper, (x, pl.ds(species + 1, 1)), -1.0)
            moves(x, (width - 1) * upper, d, bins)
    station = ((lanes_of((1, row_count)) // width + 1) // 2).astype(F32)
    for upper in (False, True):
        c = own_z[int(upper)]
        halo = beyond("sec", upper, pl.ds(0, rows), 0.0)
        d = 0.5 * (c[species : species + 1] + halo[species : species + 1])
        delta = weight * d * (halo - c)
        dz[int(upper)] = delta
        value = halves(delta)
        for j in range(stations):
            values[j].append(value)
            found[j].append(hits(jnp.where(station == j, c[species + 1 : species + 2], -1.0)))

    left = stacked_square(jacobian, square)
    station_sums = [
        sums[j]
        + folded(jnp.dot(left, halves(heated_sums[j]), preferred_element_type=F32))
        + folded(binned(jnp.concatenate(values[j], axis=1), jnp.concatenate(found[j], axis=1)))
        for j in range(stations)
    ]
    shift = jnp.broadcast_to(positions[0:1, 0:1], (rows, NB))
    per_device = planes // 2
    for s in range(0, 2 * per_device, 2):
        parts = []
        for slot in (s, s + 1):
            part = jnp.zeros((rows, NB), F32)
            for j in range(stations):
                if 0 <= slot - j < per_device:
                    part += jnp.where(shift == slot - j, station_sums[j], 0.0)
            parts.append(part)
        window[s // 2] = jnp.concatenate(parts, axis=1)


def neighbour_share(received, weight, axis, upper, c, i):
    first, second = received
    species_row = slice(weight[1], weight[1] + 1)
    is_first = jnp.broadcast_to(upper_of(axis, 0) if upper else upper_of(axis, 1), c.shape)
    inside = jnp.broadcast_to(has_neighbour(axis, 1), c.shape)
    other = jnp.zeros_like(c) if second is None else jnp.where(inside, second[i], 0.0)
    there = jnp.where(is_first, first[i], other)
    d = 0.5 * (c[species_row] + there[species_row])
    return weight[0] * d * (there - c)


def interior_kernel(planes, cells, advanced, dz, weights, *refs):
    received, (total, out, sem) = [*refs[:-3], None][:2], refs[-3:]
    row_count, rows, depth = advanced.shape
    species = out.shape[0]
    width = row_count // planes
    weight = (jnp.broadcast_to(weight_column(weights, rows), (rows, depth)), species)
    shape = (rows, depth)
    lane = lanes_of(shape)
    low = dz[0]
    high = pltpu.roll(dz[1], depth - 1, axis=1)
    mixed = [jnp.where(lane % 2 == parity, low, high) for parity in range(2)]
    ends = jnp.logical_or(lane == 0, lane == depth - 1)
    chunk = row_count // sem.shape[0]
    spans = [pl.ds(start, chunk) for start in range(0, row_count, chunk)]
    for n, span in enumerate(spans):
        for r in range(n * chunk, (n + 1) * chunk):
            turned = pltpu.roll(mixed[r % 2], depth - r, axis=1) if r else mixed[0]
            new = advanced[r] + jnp.where(ends, turned, 0.0)
            x, y = divmod(r, width)
            if y in (0, width - 1):
                new += neighbour_share(received, weight, "gy", y > 0, cells[r], x)
            total[r] = new
        for k in range(species):
            pltpu.make_async_copy(total.at[span, k, :], out.at[k, span], sem.at[n]).start()
    for n, span in enumerate(spans):
        written = total.at[span, pl.ds(0, species), :]
        pltpu.make_async_copy(written, written, sem.at[n]).wait()


def face_kernel(planes, cells, total, weights, *refs):
    received, changed = [*refs[:-1], None][:2], refs[-1]
    row_count, rows, depth = total.shape
    species = weights.shape[1]
    width = row_count // planes
    weight = (jnp.broadcast_to(weight_column(weights, rows), (rows, depth)), species)
    for n, x in enumerate((0, planes - 1)):
        for y in range(width):
            r = x * width + y
            new = total[r] + neighbour_share(received, weight, "gx", x > 0, cells[r], y)
            changed[n, :, y, :] = new[:species]


def last_kernel(planes, changed, first_out, *refs):
    terms, (out, means_out, means, sem) = refs[:-4], refs[-4:]
    species, row_count, _ = out.shape
    width = row_count // planes
    per_device, bins = means.shape[1:]
    copies = []
    for n, x in enumerate((0, planes - 1)):
        rows_out = out.at[:, pl.ds(x * width, width)]
        copies.append(pltpu.make_async_copy(changed.at[n], rows_out, sem.at[1 + n]))
        copies[n].start()
    for s in range(0, per_device, 2):
        block = sum((term[s // 2] for term in terms[1:]), terms[0][s // 2])
        block = block / jnp.maximum(block[species + 1 : species + 2], 1.0)
        means[:, s, :] = block[:species, :bins]
        means[:, s + 1, :] = block[:species, bins:]
    copies.append(pltpu.make_async_copy(means, means_out, sem.at[0]))
    copies[-1].start()
    for copy in copies:
        copy.wait()


def struct(*shape):
    return jax.ShapeDtypeStruct(shape, F32)


def call(
    kernel, name, out_shape, n_in, out_specs, in_specs=None, scratch=(), flops=0, moved=0, aliases=None
):
    return pl.pallas_call(
        kernel,
        out_shape=out_shape,
        in_specs=in_specs or [VMEM] * n_in,
        out_specs=out_specs,
        scratch_shapes=list(scratch),
        input_output_aliases=aliases or {},
        name=name,
        compiler_params=pltpu.CompilerParams(vmem_limit_bytes=32 * 1024 * 1024),
        cost_estimate=pl.CostEstimate(flops=flops, bytes_accessed=moved, transcendentals=0),
    )


def joint(block, axis, source):
    deep, count = lax.axis_size("sec"), lax.axis_size(axis)
    pairs = []
    for s in range(deep):
        for i in range(count):
            t, j = source(s, i)
            pairs.append((t * count + j, s * count + i))
    return lax.ppermute(block, ("sec", axis), pairs)


def swapped(block, axis, side):
    count = lax.axis_size(axis)
    if side == 0:
        return lax.ppermute(block, axis, [(i, i ^ 1) for i in range(count)])
    if axis == "sec":
        pairs = [(i, ((i + 1) ^ 1) - 1) for i in range(1, count - 1)]
        return lax.ppermute(block, axis, [*pairs, (0, count - 1), (count - 1, 0)])
    return joint(
        block,
        axis,
        lambda s, i: (s, ((i + 1) ^ 1) - 1) if 0 < i < count - 1 else (s ^ 1, i),
    )


def summed(block):
    deep, gx, gy = (lax.axis_size(axis) for axis in ("sec", "gx", "gy"))
    half = block.shape[0] // 2
    block = block[:half] + joint(block[half:], "gx", lambda s, i: (s ^ 1, (i - 1) % gx))
    block = block + lax.ppermute(block, "sec", [(i, i ^ 1) for i in range(deep)])
    steps = [(1 << n, 0) for n in range(1, deep.bit_length() - 1)]
    steps += [(0, 1 << n) for n in range(gy.bit_length() - 1)]
    terms = [block]
    while steps:
        (a, b), (c, d) = steps.pop(0), steps.pop(0) if steps else (0, 0)
        block = sum(terms[1:], terms[0])
        terms = [block]
        for e, f in dict.fromkeys([(a, b), (a ^ c, b ^ d), (c, d)]):
            if e or f:
                terms.append(joint(block, "gy", lambda s, i: (s ^ 1 ^ e, i ^ f)))
    return terms


def on_device(
    composition_matrix,
    local_mixing_coefficient,
    thermal_field,
    component_mixing_weight,
    kinetics_jacobian,
    mixture_classes,
    streamwise_positions,
):
    species, planes, width, depth = composition_matrix.shape
    row_count = planes * width
    rows = padded_rows(species)
    cells = composition_matrix.reshape(species, row_count, depth)
    mixing = local_mixing_coefficient.reshape(row_count, depth)
    thermal = thermal_field.reshape(row_count, depth)
    classes = mixture_classes.reshape(row_count, depth)
    weights = component_mixing_weight.reshape(1, species)
    positions = streamwise_positions.reshape(1, -1)
    per_device = planes // 2
    has_b = tuple(lax.axis_size(axis) > 2 for axis in ("gx", "gy", "sec"))
    sides = [
        (axis, side)
        for axis, both in zip(("gx", "gy", "sec"), has_b)
        for side in range(1 + both)
    ]
    shapes = {
        ("gx", 0): struct(2 * width, depth),
        ("gx", 1): struct(2 * width, depth),
        ("gy", 0): struct(planes, rows, depth),
        ("gy", 1): struct(planes, rows, depth),
        ("sec", 0): struct(rows, row_count),
        ("sec", 1): struct(max(rows, 2 * width + SUBLANES), row_count),
    }

    rows_in, own_z, *faces = call(
        functools.partial(pack_kernel, planes, has_b),
        "faces",
        [
            struct(row_count, rows, depth),
            struct(2, rows, row_count),
            *[shapes[side] for side in sides],
        ],
        3,
        [VMEM] * (2 + len(sides)),
        in_specs=[ANY] * 3,
        scratch=[
            pltpu.VMEM((row_count, depth), jnp.int32),
            pltpu.SemaphoreType.DMA((planes // 2,)),
            pltpu.SemaphoreType.DMA((2,)),
        ],
    )(*[pltpu.with_memory_space_constraint(x, pltpu.HBM) for x in (cells, mixing, classes)])
    halos = [swapped(face, axis, side) for face, (axis, side) in zip(faces, sides)]

    diffused, sums, heated_sums = call(
        functools.partial(inner_kernel, planes),
        "inside",
        [
            struct(row_count, rows, depth),
            struct(per_device + 1, rows, NB),
            struct(per_device + 1, rows, NB),
        ],
        4,
        [VMEM] * 3,
        scratch=[
            pltpu.VMEM((4, row_count, depth), F32),
            pltpu.VMEM((width, rows, depth), F32),
        ],
        flops=10_000_000,
        moved=4_000_000,
    )(rows_in, mixing, thermal, weights)

    window, dz = call(
        functools.partial(edge_kernel, planes, has_b),
        "edges",
        [struct(per_device, rows, 2 * NB), struct(2, rows, row_count)],
        7 + len(halos),
        [VMEM] * 2,
        scratch=[pltpu.VMEM((2 * rows, 2 * rows), F32)],
    )(rows_in, own_z, sums, heated_sums, weights, kinetics_jacobian, positions, *halos)

    advanced = call(
        kinetics_kernel,
        "kinetics",
        struct(row_count, rows, depth),
        5,
        VMEM,
        scratch=[
            pltpu.VMEM((row_count, depth), F32),
            pltpu.VMEM((2 * rows, 2 * rows), F32),
        ],
        flops=0,
        moved=0,
    )(rows_in, diffused, thermal, kinetics_jacobian, window)
    terms = summed(window)

    outer_planes = call(
        functools.partial(plane_kernel, planes),
        "planes",
        [struct(width, rows, depth)] * (1 + has_b[0]),
        2,
        [VMEM] * (1 + has_b[0]),
    )(rows_in, advanced)
    wide_halos = [swapped(face, "gx", side) for side, face in enumerate(outer_planes)]
    gy_halos = [halo for halo, (axis, _) in zip(halos, sides) if axis == "gy"]

    total, advanced = call(
        functools.partial(interior_kernel, planes),
        "interior",
        [struct(row_count, rows, depth), struct(species, row_count, depth)],
        4 + len(gy_halos),
        [VMEM, ANY],
        scratch=[pltpu.SemaphoreType.DMA((planes // 2,))],
        flops=1_000_000,
        moved=3_000_000,
    )(rows_in, advanced, dz, weights, *gy_halos)
    changed = call(
        functools.partial(face_kernel, planes),
        "outer_rows",
        struct(2, species, width, depth),
        3 + len(wide_halos),
        VMEM,
    )(rows_in, total, weights, *wide_halos)
    advanced, cond_means = call(
        functools.partial(last_kernel, planes),
        "last",
        [struct(species, row_count, depth), struct(species, per_device, NB)],
        2 + len(terms),
        [ANY, ANY],
        in_specs=[VMEM, ANY] + [VMEM] * len(terms),
        scratch=[
            pltpu.VMEM((species, per_device, NB), F32),
            pltpu.SemaphoreType.DMA((3,)),
        ],
        aliases={1: 0},
    )(changed, advanced, *terms)
    return advanced.reshape(composition_matrix.shape), cond_means


def solution(mesh):
    in_specs = (
        P(None, "gx", "gy", "sec"),
        P("gx", "gy", "sec"),
        P("gx", "gy", "sec"),
        P(),
        P(),
        P("gx", "gy", "sec"),
        P(),
    )
    out_specs = (P(None, "gx", "gy", "sec"), P(None, "gx", None))
    return jax.shard_map(
        on_device, mesh=mesh, in_specs=in_specs, out_specs=out_specs, check_vma=False
    )
```

```python
import functools

import jax
import jax.numpy as jnp
from jax import lax
from jax.experimental import pallas as pl
from jax.experimental.pallas import tpu as pltpu
from jax.sharding import PartitionSpec as P

NB = 64
SUBLANES = 8
LANES = 128
F32 = jnp.float32
BF16 = jnp.bfloat16
VMEM = pl.BlockSpec(memory_space=pltpu.VMEM)
ANY = pl.BlockSpec(memory_space=pl.ANY)
DT = 0.05
AHEAD = 2


def padded_rows(species):
    return -(-(species + 2) // SUBLANES) * SUBLANES


def lanes_of(shape):
    return lax.broadcasted_iota(jnp.int32, shape, len(shape) - 1)


def rows_of(shape):
    return lax.broadcasted_iota(jnp.int32, shape, len(shape) - 2)


def halves(block):
    high = block.astype(BF16).astype(F32)
    return jnp.concatenate([high, block - high], axis=0).astype(BF16)


def weight_column(weights_ref, rows):
    species = weights_ref.shape[1]
    shape = (rows, species)
    spread = jnp.where(rows_of(shape) == lanes_of(shape), weights_ref[...], 0.0)
    return DT * jnp.sum(spread, axis=1, keepdims=True)


def hits(classes):
    shape = (NB, classes.shape[1])
    bins = jnp.broadcast_to(classes.astype(BF16), shape)
    found = bins == rows_of(shape).astype(F32).astype(BF16)
    return jnp.where(found, jnp.ones((), BF16), jnp.zeros((), BF16))


def binned(values, hit):
    return lax.dot_general(
        values, hit, (((1,), (1,)), ((), ())), preferred_element_type=F32
    )


def folded(product):
    rows = product.shape[0] // 2
    return product[:rows] + product[rows:]


def upper_of(axis, side):
    even = lax.axis_index(axis) % 2 == 0
    return even if side == 0 else jnp.logical_not(even)


def has_neighbour(axis, side):
    if side == 0:
        return True
    edge = jnp.where(upper_of(axis, 1), lax.axis_size(axis) - 1, 0)
    return lax.axis_index(axis) != edge


def face_rows(axis, upper, planes, width):
    if axis == "gx":
        return jnp.where(upper, (planes - 1) * width, 0), 1, width
    return jnp.where(upper, width - 1, 0), width, planes


def pack_kernel(planes, has_b, cells, mixing, classes, *refs):
    outs, (bins, sem, field_sem) = refs[:-3], refs[-3:]
    rows_out, own_z = outs[0], outs[1]
    faces = list(outs[2:])
    species, row_count, depth = cells.shape
    rows = rows_out.shape[1]
    width = row_count // planes
    chunk = row_count // sem.shape[0]
    field_copies = [
        pltpu.make_async_copy(mixing, rows_out.at[:, species, :], field_sem.at[0]),
        pltpu.make_async_copy(classes, bins, field_sem.at[1]),
    ]
    for copy in field_copies:
        copy.start()
    for n in range(sem.shape[0]):
        span = pl.ds(n * chunk, chunk)
        for k in range(species):
            pltpu.make_async_copy(
                cells.at[k, span], rows_out.at[span, k, :], sem.at[n]
            ).start()

    lane = lanes_of((SUBLANES, depth))
    zero = jnp.zeros((SUBLANES, depth), F32)

    def gathered(groups, span, low, high):
        low, high = list(low), list(high)
        for r in span:
            at, before = lane == r, lane == (r - 1) % depth
            for i, g in enumerate(groups):
                block = rows_out[r, pl.ds(g, SUBLANES), :]
                turned = pltpu.roll(block, r, axis=1) if r else block
                low[i] = jnp.where(at, turned, low[i])
                high[i] = jnp.where(before, turned, high[i])
        return low, high

    whole = species // SUBLANES * SUBLANES
    first = range(0, whole, SUBLANES)
    rest = range(whole, rows, SUBLANES)
    low, high = [zero] * len(first), [zero] * len(first)
    for n in range(sem.shape[0]):
        arrived = rows_out.at[pl.ds(n * chunk, chunk), pl.ds(0, species), :]
        pltpu.make_async_copy(arrived, arrived, sem.at[n]).wait()
        low, high = gathered(first, range(n * chunk, (n + 1) * chunk), low, high)
    for copy in field_copies:
        copy.wait()
    for r in range(0, row_count, SUBLANES):
        span = pl.ds(r, SUBLANES)
        rows_out[span, species + 1, :] = bins[span, :].astype(F32)
    lows, highs = gathered(rest, range(row_count), [zero] * len(rest), [zero] * len(rest))
    for i, g in enumerate([*first, *rest]):
        own_z[0, pl.ds(g, SUBLANES), :] = (low + lows)[i]
        own_z[1, pl.ds(g, SUBLANES), :] = pltpu.roll((high + highs)[i], 1, axis=1)
    for axis, both in zip(("gx", "gy", "sec"), has_b):
        for side in range(1 + both):
            out = faces.pop(0)
            upper = upper_of(axis, side)
            if axis == "sec":
                out[pl.ds(0, rows), :] = own_z[jnp.where(upper, 1, 0)]
                continue
            start, step, count = face_rows(axis, upper, planes, width)
            for i in range(count):
                r = start + i * step
                if axis == "gy":
                    out[i] = rows_out[r]
                else:
                    out[pl.ds(i, 1), :] = rows_out[r, pl.ds(species, 1), :]
                    out[pl.ds(count + i, 1), :] = rows_out[r, pl.ds(species + 1, 1), :]


def plane_kernel(planes, cells, held, *faces):
    width = cells.shape[0] // planes
    for side, out in enumerate(faces):
        start, step, count = face_rows("gx", upper_of("gx", side), planes, width)
        for i in range(count):
            out[i] = cells[start + i * step]


def inner_kernel(planes, cells, mixing, thermal, weights, diffused, sums, heated_sums, coefs, between):
    row_count, rows, depth = cells.shape
    species = weights.shape[1]
    width = row_count // planes
    shape = (row_count, depth)
    lane, row = lanes_of(shape), rows_of(shape)
    mix = mixing[...]
    up = 0.5 * (mix + pltpu.roll(mix, depth - 1, axis=1))
    up = jnp.where(lane == depth - 1, 0.0, up)
    coefs[0] = up
    up = 0.5 * (mix + pltpu.roll(mix, row_count - 1, axis=0))
    coefs[1] = jnp.where(row % width == width - 1, 0.0, up)
    edge = jnp.zeros((width, depth), F32)
    coefs[2] = jnp.concatenate([0.5 * (mix[: row_count - width] + mix[width:]), edge], axis=0)
    coefs[3] = rate(thermal)

    weight = jnp.broadcast_to(weight_column(weights, rows), (rows, depth))
    whole = species // SUBLANES * SUBLANES
    ones = rows_of((rows - whole, depth)) >= species - whole
    sums[...] = jnp.zeros_like(sums)
    heated_sums[...] = jnp.zeros_like(heated_sums)

    across = []

    def advance(pair):
        values, found = [], []
        for r in pair:
            x, y = divmod(r, width)
            c = cells[r]
            at = lambda n: coefs[n, pl.ds(r, 1), :]
            along = at(0) * (pltpu.roll(c, depth - 1, axis=1) - c)
            flux = along - pltpu.roll(along, 1, axis=1)
            if y > 0:
                flux -= across.pop()
            if y < width - 1:
                across.append(at(1) * (cells[r + 1] - c))
                flux += across[0]
            if x > 0:
                flux -= between[y]
            if x < planes - 1:
                upward = at(2) * (cells[r + width] - c)
                between[y] = upward
                flux += upward
            new = c + weight * flux
            new = jnp.concatenate([new[:whole], jnp.where(ones, 1.0, new[whole:])], axis=0)
            diffused[r] = new
            values.append(jnp.concatenate([halves(new), halves(at(3) * c)], axis=0))
            found.append(hits(cells[r, species + 1 : species + 2, :]))
        return jnp.concatenate(values, axis=1), jnp.concatenate(found, axis=1)

    pairs = [(r, r + 1) for r in range(0, row_count, 2)]
    values, made = {}, 0.0
    for t in range(len(pairs) + AHEAD):
        if t < len(pairs):
            values[t] = advance(pairs[t])
        last = t - AHEAD
        if last >= 0:
            made += binned(*values.pop(last))
            x, y = divmod(pairs[last][1], width)
            if y == width - 1:
                sums[(x + 1) // 2] += folded(made[: 2 * rows])
                heated_sums[(x + 1) // 2] += folded(made[2 * rows :])
                made = 0.0


def rate(thermal):
    return (4.0 * DT) * jnp.exp(-2.0 / thermal[...])


def stacked_square(jacobian, square):
    species, rows = jacobian.shape[0], square.shape[0] // 2
    square[...] = jnp.zeros_like(square)
    matrix = jacobian[...]
    matrix_high = matrix.astype(BF16).astype(F32)
    square[:species, :species] = matrix_high
    square[:species, rows : rows + species] = matrix_high
    square[rows : rows + species, :species] = matrix - matrix_high
    return square[...].astype(BF16)


def kinetics_kernel(cells, diffused, thermal, jacobian, held, advanced, rates, square):
    row_count, rows, depth = cells.shape
    left = stacked_square(jacobian, square)
    rates[...] = rate(thermal)
    pairs = [(r, r + 1) for r in range(0, row_count, 2)]
    mixed = {}
    for t in range(len(pairs) + AHEAD):
        if t < len(pairs):
            wide = jnp.concatenate([halves(cells[r]) for r in pairs[t]], axis=1)
            mixed[t] = folded(jnp.dot(left, wide, preferred_element_type=F32))
        now = t - AHEAD
        if now >= 0:
            product = mixed.pop(now)
            for i, r in enumerate(pairs[now]):
                advanced[r] = (
                    diffused[r]
                    + rates[pl.ds(r, 1), :] * product[:, i * depth : (i + 1) * depth]
                )


def edge_kernel(
    planes, has_b, cells, own_z, sums, heated_sums, weights, jacobian, positions, *refs
):
    halos = list(refs[: 3 + sum(has_b)])
    window, dz, square = refs[3 + sum(has_b) :]
    row_count, rows, depth = cells.shape
    species = weights.shape[1]
    width = row_count // planes
    stations = planes // 2 + 1
    weight = jnp.broadcast_to(weight_column(weights, rows), (rows, depth))
    received = {}
    for axis, both in zip(("gx", "gy", "sec"), has_b):
        received[axis] = [halos.pop(0), halos.pop(0) if both else None]

    def beyond(axis, upper, part, outside):
        first, second = (halo if halo is None else halo[part] for halo in received[axis])
        second = jnp.full_like(first, outside) if second is None else second
        is_first = upper_of(axis, 0) if upper else upper_of(axis, 1)
        edge = lax.axis_size(axis) - 1 if upper else 0
        block = jnp.where(jnp.broadcast_to(is_first, first.shape), first, second)
        inside = jnp.broadcast_to(lax.axis_index(axis) != edge, first.shape)
        return jnp.where(inside, block, outside)

    values = [[] for _ in range(stations)]
    found = [[] for _ in range(stations)]

    def moves(x, y, d, bins):
        c = cells[x * width + y]
        d = 0.5 * (c[species : species + 1] + d)
        values[(x + 1) // 2].append(halves(weight * d * c))
        found[(x + 1) // 2].append(hits(bins) - hits(c[species + 1 : species + 2]))

    for upper in (False, True):
        d_beyond = beyond("gx", upper, pl.ds(0, width), 0.0)
        bins_beyond = beyond("gx", upper, pl.ds(width, width), -1.0)
        for y in range(width):
            moves((planes - 1) * upper, y, d_beyond[y : y + 1], bins_beyond[y : y + 1])
    for upper in (False, True):
        for x in range(planes):
            d = beyond("gy", upper, (x, pl.ds(species, 1)), 0.0)
            bins = beyond("gy", upper, (x, pl.ds(species + 1, 1)), -1.0)
            moves(x, (width - 1) * upper, d, bins)
    station = ((lanes_of((1, row_count)) // width + 1) // 2).astype(F32)
    for upper in (False, True):
        c = own_z[int(upper)]
        halo = beyond("sec", upper, pl.ds(0, rows), 0.0)
        d = 0.5 * (c[species : species + 1] + halo[species : species + 1])
        delta = weight * d * (halo - c)
        dz[int(upper)] = delta
        value = halves(delta)
        hit = hits(c[species + 1 : species + 2])
        for j in range(stations):
            values[j].append(value)
            found[j].append(hit * (station == j).astype(F32).astype(BF16))

    left = stacked_square(jacobian, square)
    station_sums = [
        sums[j]
        + folded(jnp.dot(left, halves(heated_sums[j]), preferred_element_type=F32))
        + folded(binned(jnp.concatenate(values[j], axis=1), jnp.concatenate(found[j], axis=1)))
        for j in range(stations)
    ]
    shift = jnp.broadcast_to(positions[0:1, 0:1], (rows, NB))
    per_device = planes // 2
    for s in range(0, 2 * per_device, 2):
        parts = []
        for slot in (s, s + 1):
            part = jnp.zeros((rows, NB), F32)
            for j in range(stations):
                if 0 <= slot - j < per_device:
                    part += jnp.where(shift == slot - j, station_sums[j], 0.0)
            parts.append(part)
        window[s // 2] = jnp.concatenate(parts, axis=1)


def neighbour_share(received, weight, axis, upper, c, i):
    first, second = received
    species_row = slice(weight[1], weight[1] + 1)
    is_first = jnp.broadcast_to(upper_of(axis, 0) if upper else upper_of(axis, 1), c.shape)
    inside = jnp.broadcast_to(has_neighbour(axis, 1), c.shape)
    other = jnp.zeros_like(c) if second is None else jnp.where(inside, second[i], 0.0)
    there = jnp.where(is_first, first[i], other)
    d = 0.5 * (c[species_row] + there[species_row])
    return weight[0] * d * (there - c)


def interior_kernel(planes, cells, advanced, dz, weights, *refs):
    received, (total, out, sem) = [*refs[:-3], None][:2], refs[-3:]
    row_count, rows, depth = advanced.shape
    species = out.shape[0]
    width = row_count // planes
    weight = (jnp.broadcast_to(weight_column(weights, rows), (rows, depth)), species)
    shape = (rows, depth)
    lane = lanes_of(shape)
    low = dz[0]
    high = pltpu.roll(dz[1], depth - 1, axis=1)
    mixed = [jnp.where(lane % 2 == parity, low, high) for parity in range(2)]
    ends = jnp.logical_or(lane == 0, lane == depth - 1)
    chunk = row_count // sem.shape[0]
    spans = [pl.ds(start, chunk) for start in range(0, row_count, chunk)]
    for n, span in enumerate(spans):
        for r in range(n * chunk, (n + 1) * chunk):
            turned = pltpu.roll(mixed[r % 2], depth - r, axis=1) if r else mixed[0]
            new = advanced[r] + jnp.where(ends, turned, 0.0)
            x, y = divmod(r, width)
            if y in (0, width - 1):
                new += neighbour_share(received, weight, "gy", y > 0, cells[r], x)
            total[r] = new
        for k in range(species):
            pltpu.make_async_copy(total.at[span, k, :], out.at[k, span], sem.at[n]).start()
    for n, span in enumerate(spans):
        written = total.at[span, pl.ds(0, species), :]
        pltpu.make_async_copy(written, written, sem.at[n]).wait()


def face_kernel(planes, cells, total, weights, *refs):
    received, changed = [*refs[:-1], None][:2], refs[-1]
    row_count, rows, depth = total.shape
    species = weights.shape[1]
    width = row_count // planes
    weight = (jnp.broadcast_to(weight_column(weights, rows), (rows, depth)), species)
    for n, x in enumerate((0, planes - 1)):
        for y in range(width):
            r = x * width + y
            new = total[r] + neighbour_share(received, weight, "gx", x > 0, cells[r], y)
            changed[n, :, y, :] = new[:species]


def last_kernel(planes, changed, first_out, *refs):
    terms, (out, means_out, means, sem) = refs[:-4], refs[-4:]
    species, row_count, _ = out.shape
    width = row_count // planes
    per_device, bins = means.shape[1:]
    copies = []
    for n, x in enumerate((0, planes - 1)):
        rows_out = out.at[:, pl.ds(x * width, width)]
        copies.append(pltpu.make_async_copy(changed.at[n], rows_out, sem.at[1 + n]))
        copies[n].start()
    for s in range(0, per_device, 2):
        block = sum((term[s // 2] for term in terms[1:]), terms[0][s // 2])
        block = block / jnp.maximum(block[species + 1 : species + 2], 1.0)
        means[:, s, :] = block[:species, :bins]
        means[:, s + 1, :] = block[:species, bins:]
    copies.append(pltpu.make_async_copy(means, means_out, sem.at[0]))
    copies[-1].start()
    for copy in copies:
        copy.wait()


def struct(*shape):
    return jax.ShapeDtypeStruct(shape, F32)


def call(
    kernel, name, out_shape, n_in, out_specs, in_specs=None, scratch=(), flops=0, moved=0, aliases=None
):
    return pl.pallas_call(
        kernel,
        out_shape=out_shape,
        in_specs=in_specs or [VMEM] * n_in,
        out_specs=out_specs,
        scratch_shapes=list(scratch),
        input_output_aliases=aliases or {},
        name=name,
        compiler_params=pltpu.CompilerParams(vmem_limit_bytes=32 * 1024 * 1024),
        cost_estimate=pl.CostEstimate(flops=flops, bytes_accessed=moved, transcendentals=0),
    )


def joint(block, axis, source):
    deep, count = lax.axis_size("sec"), lax.axis_size(axis)
    pairs = []
    for s in range(deep):
        for i in range(count):
            t, j = source(s, i)
            pairs.append((t * count + j, s * count + i))
    return lax.ppermute(block, ("sec", axis), pairs)


def swapped(block, axis, side):
    count = lax.axis_size(axis)
    if side == 0:
        return lax.ppermute(block, axis, [(i, i ^ 1) for i in range(count)])
    if axis == "sec":
        pairs = [(i, ((i + 1) ^ 1) - 1) for i in range(1, count - 1)]
        return lax.ppermute(block, axis, [*pairs, (0, count - 1), (count - 1, 0)])
    return joint(
        block,
        axis,
        lambda s, i: (s, ((i + 1) ^ 1) - 1) if 0 < i < count - 1 else (s ^ 1, i),
    )


def summed(block):
    deep, gx, gy = (lax.axis_size(axis) for axis in ("sec", "gx", "gy"))
    half = block.shape[0] // 2
    block = block[:half] + joint(block[half:], "gx", lambda s, i: (s ^ 1, (i - 1) % gx))
    block = block + lax.ppermute(block, "sec", [(i, i ^ 1) for i in range(deep)])
    steps = [(1 << n, 0) for n in range(1, deep.bit_length() - 1)]
    steps += [(0, 1 << n) for n in range(gy.bit_length() - 1)]
    terms = [block]
    while steps:
        (a, b), (c, d) = steps.pop(0), steps.pop(0) if steps else (0, 0)
        block = sum(terms[1:], terms[0])
        terms = [block]
        for e, f in dict.fromkeys([(a, b), (a ^ c, b ^ d), (c, d)]):
            if e or f:
                terms.append(joint(block, "gy", lambda s, i: (s ^ 1 ^ e, i ^ f)))
    return terms


def on_device(
    composition_matrix,
    local_mixing_coefficient,
    thermal_field,
    component_mixing_weight,
    kinetics_jacobian,
    mixture_classes,
    streamwise_positions,
):
    species, planes, width, depth = composition_matrix.shape
    row_count = planes * width
    rows = padded_rows(species)
    cells = composition_matrix.reshape(species, row_count, depth)
    mixing = local_mixing_coefficient.reshape(row_count, depth)
    thermal = thermal_field.reshape(row_count, depth)
    classes = mixture_classes.reshape(row_count, depth)
    weights = component_mixing_weight.reshape(1, species)
    positions = streamwise_positions.reshape(1, -1)
    per_device = planes // 2
    has_b = tuple(lax.axis_size(axis) > 2 for axis in ("gx", "gy", "sec"))
    sides = [
        (axis, side)
        for axis, both in zip(("gx", "gy", "sec"), has_b)
        for side in range(1 + both)
    ]
    shapes = {
        ("gx", 0): struct(2 * width, depth),
        ("gx", 1): struct(2 * width, depth),
        ("gy", 0): struct(planes, rows, depth),
        ("gy", 1): struct(planes, rows, depth),
        ("sec", 0): struct(rows, row_count),
        ("sec", 1): struct(max(rows, 2 * width + SUBLANES), row_count),
    }

    rows_in, own_z, *faces = call(
        functools.partial(pack_kernel, planes, has_b),
        "faces",
        [
            struct(row_count, rows, depth),
            struct(2, rows, row_count),
            *[shapes[side] for side in sides],
        ],
        3,
        [VMEM] * (2 + len(sides)),
        in_specs=[ANY] * 3,
        scratch=[
            pltpu.VMEM((row_count, depth), jnp.int32),
            pltpu.SemaphoreType.DMA((planes // 2,)),
            pltpu.SemaphoreType.DMA((2,)),
        ],
    )(*[pltpu.with_memory_space_constraint(x, pltpu.HBM) for x in (cells, mixing, classes)])
    halos = [swapped(face, axis, side) for face, (axis, side) in zip(faces, sides)]

    diffused, sums, heated_sums = call(
        functools.partial(inner_kernel, planes),
        "inside",
        [
            struct(row_count, rows, depth),
            struct(per_device + 1, rows, NB),
            struct(per_device + 1, rows, NB),
        ],
        4,
        [VMEM] * 3,
        scratch=[
            pltpu.VMEM((4, row_count, depth), F32),
            pltpu.VMEM((width, rows, depth), F32),
        ],
        flops=10_000_000,
        moved=4_000_000,
    )(rows_in, mixing, thermal, weights)

    window, dz = call(
        functools.partial(edge_kernel, planes, has_b),
        "edges",
        [struct(per_device, rows, 2 * NB), struct(2, rows, row_count)],
        7 + len(halos),
        [VMEM] * 2,
        scratch=[pltpu.VMEM((2 * rows, 2 * rows), F32)],
    )(rows_in, own_z, sums, heated_sums, weights, kinetics_jacobian, positions, *halos)

    advanced = call(
        kinetics_kernel,
        "kinetics",
        struct(row_count, rows, depth),
        5,
        VMEM,
        scratch=[
            pltpu.VMEM((row_count, depth), F32),
            pltpu.VMEM((2 * rows, 2 * rows), F32),
        ],
        flops=0,
        moved=0,
    )(rows_in, diffused, thermal, kinetics_jacobian, window)
    terms = summed(window)

    outer_planes = call(
        functools.partial(plane_kernel, planes),
        "planes",
        [struct(width, rows, depth)] * (1 + has_b[0]),
        2,
        [VMEM] * (1 + has_b[0]),
    )(rows_in, advanced)
    wide_halos = [swapped(face, "gx", side) for side, face in enumerate(outer_planes)]
    gy_halos = [halo for halo, (axis, _) in zip(halos, sides) if axis == "gy"]

    total, advanced = call(
        functools.partial(interior_kernel, planes),
        "interior",
        [struct(row_count, rows, depth), struct(species, row_count, depth)],
        4 + len(gy_halos),
        [VMEM, ANY],
        scratch=[pltpu.SemaphoreType.DMA((planes // 2,))],
        flops=1_000_000,
        moved=3_000_000,
    )(rows_in, advanced, dz, weights, *gy_halos)
    changed = call(
        functools.partial(face_kernel, planes),
        "outer_rows",
        struct(2, species, width, depth),
        3 + len(wide_halos),
        VMEM,
    )(rows_in, total, weights, *wide_halos)
    advanced, cond_means = call(
        functools.partial(last_kernel, planes),
        "last",
        [struct(species, row_count, depth), struct(species, per_device, NB)],
        2 + len(terms),
        [ANY, ANY],
        in_specs=[VMEM, ANY] + [VMEM] * len(terms),
        scratch=[
            pltpu.VMEM((species, per_device, NB), F32),
            pltpu.SemaphoreType.DMA((3,)),
        ],
        aliases={1: 0},
    )(changed, advanced, *terms)
    return advanced.reshape(composition_matrix.shape), cond_means


def solution(mesh):
    in_specs = (
        P(None, "gx", "gy", "sec"),
        P("gx", "gy", "sec"),
        P("gx", "gy", "sec"),
        P(),
        P(),
        P("gx", "gy", "sec"),
        P(),
    )
    out_specs = (P(None, "gx", "gy", "sec"), P(None, "gx", None))
    return jax.shard_map(
        on_device, mesh=mesh, in_specs=in_specs, out_specs=out_specs, check_vma=False
    )
```
